128 devices in a mesh: dp: 8 (over y, core), seq: 2 (over z_hi), tensor: 8 (over x, z_lo).
Axes of the slice: x: 4, y: 4, z: 4 (z_hi: 2, z_lo: 2; z = z_hi * 2 + z_lo), core: 2. Of those that a mesh axis runs over, the one named last changes fastest.
Arguments:
- activations: bfloat16 [6144, 6144], P(('dp', 'seq'), 'tensor'), may hold values from -15 to 15
- qkv_weight: bfloat16 [6144, 8, 1024], P(('dp', 'seq'), 'tensor')
- out_weight: bfloat16 [8, 768, 6144], P('tensor', None, ('dp', 'seq')), may hold values from -0.078125 to 0.078125
- grad_out: bfloat16 [6144, 6144], P(('dp', 'seq'), 'tensor'), may hold values from -6 to 6
- segments: int32 [6144], P('dp'), may hold values from 0 to 4, as said below
- send_list: int32 [16, 16], P(('dp', 'seq')), may hold values from -1 to 11, as said below
- recv_list: int32 [16, 16], P(('dp', 'seq')), may hold values from -1 to 11, as said below
Outputs:
- attended: bfloat16 [6144, 6144], P(('dp', 'seq'), 'tensor')
- grad_in: bfloat16 [6144, 6144], P(('dp', 'seq'), 'tensor')
The draws below stay inside these ranges and needn't reach their ends.
Inputs may be any that keep to these rules, and one draw needn't show every extreme that they name: `send_list`: each row s lists, at entry d * 1 + c, the block of group s that goes to group d in slot c, or -1; each of the 12 blocks of s is listed exactly once. `recv_list`: each row d gives, at entry s * 1 + c, the block position in group d taken by the block that group s sends to d in slot c, and -1 exactly where send_list[s, d * 1 + c] is -1; each position of d is taken exactly once. `segments`: within each packed sequence of 768 rows the ids start at 0 on its first row, never fall and rise by at most 1 from a row to the next; every run of 384 rows that starts at a multiple of 384 holds exactly two first rows of documents besides a packed sequence's own first row, so the largest id of every packed sequence is 2 * 2.
All inputs are finite; a program needn't handle non-finite values.
Results may differ from the reference program's by a relative error of at most 0.035.
Values may be sent and summed in bfloat16 or wider, within the bound.
No kernel may reach another device: no remote copies, remote signals or barrier semaphores. Data moves between devices by JAX's collectives and lax.ppermute only.
A program may use at most 128 MiB of HBM per device.

```python
import math
import jax
import jax.numpy as jnp
from jax import lax

D = 6144
HS = 128
KVH = 8
GROUP = 6
ROWS = 384
BLK = 32
GROUPS = 16
LOCAL_KV = 1
HEADS = 48
NBLK = 12
CAP = 1
TOKENS = 6144
SEQLEN = 768
N_TENSOR = 8


def balance_tables(base_key):
    order_key = jax.random.fold_in(base_key, 101)
    place_key = jax.random.fold_in(base_key, 102)
    shuffle_key = jax.random.fold_in(base_key, 103)
    half_way = GROUPS // 2
    others = jax.random.permutation(order_key, GROUPS * CAP - 1)[:NBLK - 1].astype(jnp.int32)
    others = others + (others >= half_way).astype(jnp.int32)
    chosen = jnp.concatenate([jnp.full((1,), half_way, jnp.int32), others])
    slot_ids = chosen[jax.random.permutation(shuffle_key, NBLK)].astype(jnp.int32)
    offsets = slot_ids % GROUPS
    slot_rank = slot_ids // GROUPS
    places = jax.vmap(lambda sub_key: jax.random.permutation(sub_key, NBLK))(jax.random.split(place_key, GROUPS))
    devices = jnp.arange(GROUPS, dtype=jnp.int32)[:, None]
    blocks = jnp.broadcast_to(jnp.arange(NBLK, dtype=jnp.int32)[None, :], (GROUPS, NBLK))
    send_cols = (devices + offsets[None, :]) % GROUPS * CAP + slot_rank[None, :]
    recv_cols = (devices - offsets[None, :]) % GROUPS * CAP + slot_rank[None, :]
    send_table = jnp.full((GROUPS, GROUPS * CAP), -1, jnp.int32).at[devices, send_cols].set(blocks)
    recv_table = jnp.full((GROUPS, GROUPS * CAP), -1, jnp.int32).at[devices, recv_cols].set(places.astype(jnp.int32))
    return (send_table, recv_table)


def draw_send_list(key, part):
    return balance_tables(key)[0]


def draw_recv_list(key, part):
    return balance_tables(key)[1]


def draw_segments(key, part):
    key = jax.random.fold_in(key, 5)
    positions = jnp.arange(TOKENS, dtype=jnp.int32)
    within = positions % ROWS
    first_at = jax.random.randint(jax.random.fold_in(key, 2), (TOKENS // ROWS,), ROWS // 4, ROWS // 2 + 1)
    second_at = jax.random.randint(jax.random.fold_in(key, 3), (TOKENS // ROWS,), ROWS // 2 + 1, ROWS)
    starts = (within == jnp.repeat(first_at, ROWS)) | (within == jnp.repeat(second_at, ROWS))
    starts = starts | (positions % SEQLEN == 0)
    per_seq = starts.astype(jnp.int32).reshape(TOKENS // SEQLEN, SEQLEN)
    return (jnp.cumsum(per_seq, axis=1) - 1).astype(jnp.int32).reshape(TOKENS)


def draw_activations(key, part):
    key = jax.random.fold_in(key, 7)
    return jnp.clip(jax.random.normal(key, (TOKENS, D), jnp.float32), -6.0, 6.0).astype(jnp.bfloat16)


def draw_qkv_weight(key, part):
    key = jax.random.fold_in(key, 11)
    full_shape = (D, KVH, GROUP + 2, HS)
    normal_part = jnp.clip(jax.random.normal(key, full_shape, jnp.float32), -6.0, 6.0) / math.sqrt(D)
    return normal_part.reshape(D, KVH, (GROUP + 2) * HS).astype(jnp.bfloat16)


def shard_levels(own_key, shape, shards, smallest, largest):
    def one(dim, parts):
        draws = jax.random.uniform(jax.random.fold_in(jax.random.fold_in(own_key, 6), dim), (parts,), jnp.float32, smallest / len(shards), largest / len(shards))
        return jnp.repeat(jnp.exp(draws), shape[dim] // parts).reshape((-1,) + (1,) * (len(shape) - dim - 1))

    gain = one(*shards[0])
    for cut in shards[1:]:
        gain = gain * one(*cut)
    return gain


def normal_values(own_key, shape, scale, most, cuts=(), kind=jnp.bfloat16):
    gain = shard_levels(own_key, shape, cuts, -0.22, 0.18) if cuts else 1.0
    drawn = jax.random.normal(own_key, shape, jnp.float32) * scale * gain
    return jnp.minimum(jnp.maximum(drawn, -most), most).astype(kind)


def setup_inputs(seed: int = 0) -> dict:
    splits = jax.random.split(jax.random.key(seed), 8)
    activations = draw_activations(jax.random.fold_in(splits[7], 71), 0)
    qkv_weight = draw_qkv_weight(jax.random.fold_in(splits[7], 71), 0)
    out_weight = normal_values(splits[2], (KVH, GROUP * HS, D), (HEADS * HS) ** -0.5, 0.078125, ((0, 8), (2, 16)))
    grad_out = normal_values(splits[3], (TOKENS, D), 1.0, 6.0, ((0, 16), (1, 8)))
    segments = draw_segments(jax.random.fold_in(splits[7], 71), 0)
    send_list = draw_send_list(jax.random.fold_in(splits[7], 71), 0)
    recv_list = draw_recv_list(jax.random.fold_in(splits[7], 71), 0)
    return dict(activations=activations, qkv_weight=qkv_weight, out_weight=out_weight, grad_out=grad_out, segments=segments, send_list=send_list, recv_list=recv_list)


def lowered(value):
    return lax.optimization_barrier(value.astype(jnp.bfloat16))

def block_tables(send_list, recv_list):
    source = jnp.arange(GROUPS, dtype=jnp.int32)[:, None]
    slot_ids = jnp.arange(GROUPS * CAP, dtype=jnp.int32)[None, :]
    target = slot_ids // CAP
    slot_rank = slot_ids % CAP
    landing = recv_list[target, source * CAP + slot_rank]
    old_index = jnp.where(send_list >= 0, source * NBLK + send_list, GROUPS * NBLK).astype(jnp.int32)
    new_index = (target * NBLK + landing).astype(jnp.int32)
    everything = jnp.arange(GROUPS * NBLK, dtype=jnp.int32)
    new_of_old = jnp.zeros((GROUPS * NBLK,), jnp.int32).at[old_index.reshape(-1)].set(new_index.reshape(-1), mode='drop')
    old_of_new = jnp.zeros((GROUPS * NBLK,), jnp.int32).at[new_of_old].set(everything)
    return (new_of_old, old_of_new)

def attend(queries, key_rows, value_rows, grad_heads, segment_ids):
    precise = lax.Precision.HIGHEST
    seq_rows = queries.shape[0]
    positions = jnp.arange(seq_rows)
    allowed = (segment_ids[:, None] == segment_ids[None, :]) & (positions[None, :] <= positions[:, None])
    scaling = 1.0 / math.sqrt(HS)
    query_wide = queries.astype(jnp.float32)
    key_wide = key_rows.astype(jnp.float32)
    value_wide = value_rows.astype(jnp.float32)
    grad_wide = grad_heads.astype(jnp.float32)
    scores = jnp.einsum('qghd,kgd->ghqk', query_wide, key_wide, precision=precise) * scaling
    scores = jnp.where(allowed, scores, -1e+30)
    highest = lax.optimization_barrier(jnp.max(scores, axis=-1, keepdims=True))
    raised = jnp.exp(scores - highest)
    probability = raised / lax.optimization_barrier(jnp.sum(raised, axis=-1, keepdims=True))
    prob_wide = lowered(probability).astype(jnp.float32)
    head_out = lowered(jnp.einsum('ghqk,kgd->qghd', prob_wide, value_wide, precision=precise))
    row_delta = jnp.einsum('qghd,qghd->ghq', grad_wide, head_out.astype(jnp.float32), precision=precise)
    grad_values = jnp.einsum('ghqk,qghd->kgd', prob_wide, grad_wide, precision=precise).astype(jnp.bfloat16)
    grad_prob = jnp.einsum('qghd,kgd->ghqk', grad_wide, value_wide, precision=precise)
    score_grad = lowered(probability * (grad_prob - row_delta[..., None])).astype(jnp.float32)
    grad_queries = (jnp.einsum('ghqk,kgd->qghd', score_grad, key_wide, precision=precise) * scaling).astype(jnp.bfloat16)
    grad_keys = (jnp.einsum('ghqk,qghd->kgd', score_grad, query_wide, precision=precise) * scaling).astype(jnp.bfloat16)
    return (head_out, grad_queries, grad_keys, grad_values)

def reference(activations, qkv_weight, out_weight, grad_out, segments, send_list, recv_list):
    new_of_old, old_of_new = block_tables(send_list, recv_list)
    moved = activations.reshape(GROUPS * NBLK, BLK, D)[old_of_new].reshape(TOKENS, D)
    flat_in = qkv_weight.reshape(D, KVH * (GROUP + 2) * HS)
    flat_out = out_weight.reshape(HEADS * HS, D)
    projected = jnp.dot(moved, flat_in, preferred_element_type=jnp.float32).astype(jnp.bfloat16)
    projected = projected.reshape(TOKENS, KVH, GROUP + 2, HS)
    grad_heads = jnp.dot(grad_out, flat_out.T, preferred_element_type=jnp.float32).astype(jnp.bfloat16)
    grad_heads = grad_heads.reshape(TOKENS, KVH, GROUP, HS)
    sequences = TOKENS // SEQLEN
    stacked = (projected.reshape(sequences, SEQLEN, KVH, GROUP + 2, HS), grad_heads.reshape(sequences, SEQLEN, KVH, GROUP, HS), segments.reshape(sequences, SEQLEN))

    def one_sequence(pieces):
        packed, grad_rows, segment_ids = pieces
        return attend(packed[:, :, :GROUP], packed[:, :, GROUP], packed[:, :, GROUP + 1], grad_rows, segment_ids)
    head_out, grad_queries, grad_keys, grad_values = lax.map(one_sequence, stacked)
    flat_heads = head_out.reshape(TOKENS, HEADS * HS)
    grad_packed = jnp.concatenate([grad_queries, grad_keys[:, :, :, None], grad_values[:, :, :, None]], axis=3)
    grad_packed = grad_packed.reshape(TOKENS, KVH * (GROUP + 2) * HS)
    span_out = LOCAL_KV * GROUP * HS
    span_in = LOCAL_KV * (GROUP + 2) * HS
    mixed_sum = jnp.zeros((TOKENS, D), jnp.float32)
    back_sum = jnp.zeros((TOKENS, D), jnp.float32)
    for member in range(N_TENSOR):
        partial_out = lowered(jnp.dot(flat_heads[:, member * span_out:(member + 1) * span_out], flat_out[member * span_out:(member + 1) * span_out], preferred_element_type=jnp.float32))
        mixed_sum = mixed_sum + partial_out.astype(jnp.float32)
        partial_back = lowered(jnp.dot(grad_packed[:, member * span_in:(member + 1) * span_in], flat_in[:, member * span_in:(member + 1) * span_in].T, preferred_element_type=jnp.float32))
        back_sum = back_sum + partial_back.astype(jnp.float32)
    attended = mixed_sum.astype(jnp.bfloat16)
    grad_moved = back_sum.astype(jnp.bfloat16)
    grad_in = grad_moved.reshape(GROUPS * NBLK, BLK, D)[new_of_old].reshape(TOKENS, D)
    return (attended, grad_in)
```

```python
import math

import jax
import jax.numpy as jnp
from jax import lax
from jax.sharding import PartitionSpec as P

HS = 128
GROUP = 6
BLK = 32
AXES = ("dp", "seq", "tensor")
NX, NY, NZ = 4, 4, 4
X_GROUPS = [[0, 2, 4, 6], [1, 3, 5, 7]]


def place(index):
    dp, seq, tensor = index // 16, index // 8 % 2, index % 8
    return tensor // 2, dp // 2, seq, tensor % 2, dp % 2


def index_of(x, y, z_hi, z_lo, core):
    return (y % NY * 2 + core) * 16 + z_hi * 8 + x % NX * 2 + z_lo


def send(block, target):
    pairs = []
    for source in range(128):
        goal = target(*place(source))
        if goal is not None:
            pairs.append((source, index_of(*goal)))
    return lax.ppermute(block, AXES, pairs)


def along_y(block, distance):
    return send(block, lambda x, y, zh, zl, c: (x, y - distance, zh, zl, c))


def over_cores(block):
    return send(block, lambda x, y, zh, zl, c: (x, y, zh, zl, 1 - c))


def over_z_lo(block):
    return send(block, lambda x, y, zh, zl, c: (x, y, zh, 1 - zl, c))


def z_near(block):
    return send(
        block, lambda x, y, zh, zl, c: (x, y, zh, 1 - zl, 1 - c) if zl != c else None
    )


def z_far(block):
    return send(
        block,
        lambda x, y, zh, zl, c: (x, y, 1 - zh, zl, c)
        if zl == c
        else (x, y, 1 - zh, 1 - zl, 1 - c),
    )


def y_ring(block, axis):
    up = along_y(block, 1)
    down = along_y(block, -1)
    half = block.shape[axis] // 2
    first = along_y(lax.slice_in_dim(up, 0, half, axis=axis), 1)
    second = along_y(lax.slice_in_dim(down, half, 2 * half, axis=axis), -1)
    return [block, up, down, jnp.concatenate([first, second], axis=axis)]


def route_blocks(buffer):
    return lax.all_to_all(buffer, ("dp", "seq"), split_axis=0, concat_axis=0, tiled=True)


def dot(a, b, contract=((1,), (0,))):
    return lax.dot_general(a, b, (contract, ((), ())), preferred_element_type=jnp.float32)


NT = ((1,), (1,))


def body(activations, qkv_weight, out_weight, grad_out, segments, send_list, recv_list):
    row_count, shard_width = activations.shape
    block_count = row_count // BLK
    slot_total = send_list.shape[1]
    dp_index = lax.axis_index("dp")
    seq_index = lax.axis_index("seq")
    tensor_index = lax.axis_index("tensor")
    y_index, core = dp_index // 2, dp_index % 2
    x_index, z_lo = tensor_index // 2, tensor_index % 2
    straight = core == z_lo
    offsets = (0, 1, -1, 2)

    in_own, out_own = qkv_weight[:, 0, :], out_weight[0]

    def join_z(own, near, far, axis):
        here = jnp.where(straight, own, near)
        return jnp.where(
            seq_index == 0,
            jnp.concatenate([here, far], axis=axis),
            jnp.concatenate([far, here], axis=axis),
        )

    in_mine = y_ring(join_z(in_own, z_near(in_own), z_far(in_own), 0), 0)
    in_other = [over_cores(w) for w in in_mine]
    out_mine = [join_z(w, z_near(w), z_far(w), 1) for w in y_ring(out_own, 0)]
    out_other = [over_cores(w) for w in out_mine]

    send_slots = send_list[0]
    recv_slots = recv_list[0]
    slot_range = jnp.arange(slot_total, dtype=jnp.int32)
    blocks = activations.reshape(block_count, BLK, shard_width)
    sending = jnp.where(
        (send_slots >= 0)[:, None, None],
        blocks[jnp.maximum(send_slots, 0)],
        jnp.zeros((), jnp.bfloat16),
    )
    arrived = route_blocks(sending)
    slot_of = (
        jnp.zeros((block_count,), jnp.int32)
        .at[jnp.where(recv_slots >= 0, recv_slots, block_count)]
        .set(slot_range, mode="drop")
    )
    moved = arrived[slot_of].reshape(row_count, shard_width)

    def gather_x(block):
        return lax.all_gather(
            block, "tensor", axis=0, tiled=False, axis_index_groups=X_GROUPS
        )

    grad_x = gather_x(grad_out)
    moved_x = gather_x(moved)

    def chunk(stacked, offset):
        return lax.dynamic_index_in_dim(
            stacked, (y_index + offset) % NY, axis=0, keepdims=False
        )

    proj_mine = sum(dot(chunk(moved_x, o), w) for o, w in zip(offsets, in_mine))
    proj_other = sum(dot(chunk(moved_x, o), w) for o, w in zip(offsets, in_other))
    heads_mine = sum(dot(chunk(grad_x, o), w, NT) for o, w in zip(offsets, out_mine))
    heads_other = sum(dot(chunk(grad_x, o), w, NT) for o, w in zip(offsets, out_other))

    def sum_z(mine, other):
        keep = jnp.where(straight, mine, other)
        give = jnp.where(straight, other, mine).astype(jnp.bfloat16)
        return (keep + over_z_lo(give).astype(jnp.float32)).astype(jnp.bfloat16)

    projected = sum_z(proj_mine, proj_other)
    grad_heads = sum_z(heads_mine, heads_other).reshape(row_count, GROUP, HS)

    queries = projected[:, : GROUP * HS].reshape(row_count, GROUP, HS)
    own_kv = projected[:, GROUP * HS :]
    prev_kv = send(
        own_kv, lambda x, y, zh, zl, c: (x, y, 1, zl, c) if zh == 0 else None
    )
    all_kv = jnp.concatenate([prev_kv, own_kv], axis=0)
    all_keys, all_values = all_kv[:, :HS], all_kv[:, HS:]
    query_ids = lax.dynamic_slice_in_dim(segments, seq_index * row_count, row_count)
    padded_ids = jnp.concatenate([jnp.full((row_count,), -1, jnp.int32), segments])
    key_ids = lax.dynamic_slice_in_dim(padded_ids, seq_index * row_count, 2 * row_count)
    positions = jnp.arange(2 * row_count)
    allowed = (query_ids[:, None] == key_ids[None, :]) & (
        positions[None, :] <= positions[:row_count, None] + row_count
    )
    scaling = 1.0 / math.sqrt(HS)
    scores = (
        jnp.einsum("qhd,kd->hqk", queries, all_keys, preferred_element_type=jnp.float32)
        * scaling
    )
    scores = jnp.where(allowed, scores, -1e30)
    highest = jnp.max(scores, axis=-1, keepdims=True)
    raised = jnp.exp(scores - highest)
    probability = raised / jnp.sum(raised, axis=-1, keepdims=True)
    prob_low = probability.astype(jnp.bfloat16)
    head_out = jnp.einsum(
        "hqk,kd->qhd", prob_low, all_values, preferred_element_type=jnp.float32
    ).astype(jnp.bfloat16)

    def sum_x(parts):
        stacked = jnp.stack([p.astype(jnp.bfloat16) for p in parts])
        source = jnp.array([0, 1, 3, 2], jnp.int32)[(jnp.arange(NX) - y_index) % NX]
        ordered = stacked[source].reshape(NX * row_count, shard_width)
        return lax.psum_scatter(
            ordered, "tensor", scatter_dimension=0, tiled=True, axis_index_groups=X_GROUPS
        )

    def pair(own):
        theirs = over_z_lo(own)
        return jnp.where(straight, own, theirs), jnp.where(straight, theirs, own)

    out_mine_rows, out_other_rows = pair(head_out.reshape(row_count, GROUP * HS))
    attended = sum_x(
        [
            dot(out_mine_rows, a) + dot(out_other_rows, b)
            for a, b in zip(out_mine, out_other)
        ]
    )

    row_delta = jnp.einsum(
        "qhd,qhd->hq", grad_heads, head_out, preferred_element_type=jnp.float32
    )
    grad_values = jnp.einsum(
        "hqk,qhd->kd", prob_low, grad_heads, preferred_element_type=jnp.float32
    )
    grad_prob = jnp.einsum(
        "qhd,kd->hqk", grad_heads, all_values, preferred_element_type=jnp.float32
    )
    score_grad = (probability * (grad_prob - row_delta[..., None])).astype(jnp.bfloat16)
    grad_queries = (
        jnp.einsum("hqk,kd->qhd", score_grad, all_keys, preferred_element_type=jnp.float32)
        * scaling
    ).astype(jnp.bfloat16)
    grad_keys = (
        jnp.einsum("hqk,qhd->kd", score_grad, queries, preferred_element_type=jnp.float32)
        * scaling
    )
    grad_kv = jnp.concatenate([grad_keys, grad_values], axis=1)
    back_kv = send(
        grad_kv[:row_count].astype(jnp.bfloat16),
        lambda x, y, zh, zl, c: (x, y, 0, zl, c) if zh == 1 else None,
    )
    kv_total = (grad_kv[row_count:] + back_kv.astype(jnp.float32)).astype(jnp.bfloat16)
    grad_packed = jnp.concatenate(
        [grad_queries.reshape(row_count, GROUP * HS), kv_total], axis=1
    )
    in_mine_rows, in_other_rows = pair(grad_packed)
    grad_moved = sum_x(
        [
            dot(in_mine_rows, a, NT) + dot(in_other_rows, b, NT)
            for a, b in zip(in_mine, in_other)
        ]
    )

    back_blocks = grad_moved.reshape(block_count, BLK, shard_width)
    returning = jnp.where(
        (recv_slots >= 0)[:, None, None],
        back_blocks[jnp.maximum(recv_slots, 0)],
        jnp.zeros((), jnp.bfloat16),
    )
    returned = route_blocks(returning)
    anchor = (
        jnp.zeros((block_count,), jnp.int32)
        .at[jnp.where(send_slots >= 0, send_slots, block_count)]
        .set(slot_range, mode="drop")
    )
    grad_in = returned[anchor].reshape(row_count, shard_width)
    return (attended, grad_in)


def solution(mesh):
    placed = (
        P(("dp", "seq"), "tensor"),
        P(("dp", "seq"), "tensor", None),
        P("tensor", None, ("dp", "seq")),
        P(("dp", "seq"), "tensor"),
        P("dp"),
        P(("dp", "seq"), None),
        P(("dp", "seq"), None),
    )
    return jax.shard_map(
        body,
        mesh=mesh,
        in_specs=placed,
        out_specs=(P(("dp", "seq"), "tensor"), P(("dp", "seq"), "tensor")),
        check_vma=False,
    )
```

```python
import math

import jax
import jax.numpy as jnp
from jax import lax
from jax.experimental import pallas as pl
from jax.experimental.pallas import tpu as pltpu
from jax.sharding import PartitionSpec as P

HS = 128
GROUP = 6
BLK = 32
AXES = ("dp", "seq", "tensor")
NX, NY, NZ = 4, 4, 4
X_GROUPS = [[0, 2, 4, 6], [1, 3, 5, 7]]


def place(index):
    dp, seq, tensor = index // 16, index // 8 % 2, index % 8
    return tensor // 2, dp // 2, seq, tensor % 2, dp % 2


def index_of(x, y, z_hi, z_lo, core):
    return (y % NY * 2 + core) * 16 + z_hi * 8 + x % NX * 2 + z_lo


def send(block, target):
    pairs = []
    for source in range(128):
        goal = target(*place(source))
        if goal is not None:
            pairs.append((source, index_of(*goal)))
    return lax.ppermute(block, AXES, pairs)


def along_y(block, distance):
    return send(block, lambda x, y, zh, zl, c: (x, y - distance, zh, zl, c))


def over_cores(block):
    return send(block, lambda x, y, zh, zl, c: (x, y, zh, zl, 1 - c))


def over_z_lo(block):
    return send(block, lambda x, y, zh, zl, c: (x, y, zh, 1 - zl, c))


def z_near(block):
    return send(
        block, lambda x, y, zh, zl, c: (x, y, zh, 1 - zl, 1 - c) if zl != c else None
    )


def z_far(block):
    return send(
        block,
        lambda x, y, zh, zl, c: (x, y, 1 - zh, zl, c)
        if zl == c
        else (x, y, 1 - zh, 1 - zl, 1 - c),
    )


def y_ring(block, axis):
    up = along_y(block, 1)
    down = along_y(block, -1)
    half = block.shape[axis] // 2
    first = along_y(lax.slice_in_dim(up, 0, half, axis=axis), 1)
    second = along_y(lax.slice_in_dim(down, half, 2 * half, axis=axis), -1)
    return [block, up, down, jnp.concatenate([first, second], axis=axis)]


def route_blocks(relative):
    def over(block, dc, dz):
        return send(
            block,
            lambda x, y, zh, zl, c: (x, y, zh ^ dz, zl, c ^ dc),
        )

    held = [relative[0], over(relative[1], 0, 1), over(relative[2], 1, 0), over(relative[3], 1, 1)]
    held = jnp.stack(held, axis=1)
    return jnp.concatenate(
        [held[0], along_y(held[1], -1), along_y(held[2], 1), along_y(held[3], 2)], axis=0
    )


def dot(a, b, contract=((1,), (0,))):
    return lax.dot_general(a, b, (contract, ((), ())), preferred_element_type=jnp.float32)


NT = ((1,), (1,))
NN = ((1,), (0,))
MB = 1 << 20
OFFSETS = (0, 1, -1, 2)
POSITION = (0, 1, 3, 2)
TILE = 256


def vmem():
    return pl.BlockSpec(memory_space=pltpu.VMEM)


def smem():
    return pl.BlockSpec(memory_space=pltpu.SMEM)


def anywhere():
    return pl.BlockSpec(memory_space=pl.ANY)


def sum_kernel(contract, info, rows, *refs):
    weights, out, held, sems = refs[:8], refs[8], refs[9], refs[10]
    tiles = out.shape[1] // TILE

    def part(ref, tile):
        if contract == NT:
            return ref.at[pl.ds(pl.multiple_of(tile * TILE, TILE), TILE)]
        return ref.at[:, pl.ds(pl.multiple_of(tile * TILE, TILE), TILE)]

    for pick in range(2):

        @pl.when(info[0] == pick)
        def _():
            @pl.loop(0, tiles)
            def _(tile):
                for s in range(NY):
                    pltpu.make_async_copy(
                        part(weights[pick * NY + s], tile),
                        part(held.at[s], tile),
                        sems.at[tile, s],
                    ).start()

    @pl.loop(0, tiles)
    def _(tile):
        total = None
        for s in range(NY):
            pltpu.make_async_copy(
                part(weights[s], tile), part(held.at[s], tile), sems.at[tile, s]
            ).wait()
            term = dot(rows[info[1 + s]], part(held.at[s], tile)[...], contract)
            total = term if total is None else total + term
        out[:, pl.ds(pl.multiple_of(tile * TILE, TILE), TILE)] = total.astype(out.dtype)


def sum_product(use_other, chunk_order, rows, mine, other, contract, dtype):
    row_count, depth = rows.shape[1:]
    width = mine[0].shape[1] if contract == NN else mine[0].shape[0]
    info = jnp.concatenate([use_other.astype(jnp.int32)[None], chunk_order])
    return pl.pallas_call(
        lambda *refs: sum_kernel(contract, *refs),
        out_shape=jax.ShapeDtypeStruct((row_count, width), dtype),
        in_specs=[smem(), vmem()] + [anywhere()] * 8,
        out_specs=vmem(),
        scratch_shapes=[
            pltpu.VMEM((NY,) + mine[0].shape, jnp.bfloat16),
            pltpu.SemaphoreType.DMA((width // TILE, NY)),
        ],
        compiler_params=pltpu.CompilerParams(vmem_limit_bytes=20 * MB),
        cost_estimate=pl.CostEstimate(
            flops=2 * row_count * width * depth * NY,
            bytes_accessed=2 * NY * depth * (width + row_count),
            transcendentals=0,
        ),
    )(info, rows, *mine, *other)


def spread_kernel(contract, parts, info, *refs):
    own, theirs = refs[:parts], refs[parts : 2 * parts]
    weights = refs[2 * parts : 2 * parts + 8]
    outs = refs[2 * parts + 8 : -2]
    held, sems = refs[-2:]
    for j in range(NX):
        for pick in range(2):
            for s in range(NY):

                @pl.when((info[0] == pick) & (info[1 + j] == s))
                def _():
                    for side in range(2):
                        pltpu.make_async_copy(
                            weights[(pick ^ side) * NY + s], held.at[j, side], sems.at[j, side]
                        ).start()

    for j in range(NX):
        for side in range(2):
            pltpu.make_async_copy(weights[0], held.at[j, side], sems.at[j, side]).wait()
        out = outs[0].at[j] if len(outs) == 1 else outs[j]

        @pl.loop(0, out.shape[1] // TILE)
        def _(tile):
            columns = pl.ds(pl.multiple_of(tile * TILE, TILE), TILE)
            total = None
            for side, rows in ((0, own), (1, theirs)):
                start = 0
                for piece in rows:
                    depth = pl.ds(start, piece.shape[1])
                    start += piece.shape[1]
                    if contract == NT:
                        weight = held[j, side, columns, depth]
                    else:
                        weight = held[j, side, depth, columns]
                    term = dot(piece[...], weight, contract)
                    total = term if total is None else total + term
            out[:, columns] = total.astype(out.dtype)


def spread_product(use_other, order, own, theirs, mine, other, contract, joined):
    row_count = own[0].shape[0]
    depth = sum(p.shape[1] for p in own)
    width = mine[0].shape[1] if contract == NN else mine[0].shape[0]
    info = jnp.concatenate([use_other.astype(jnp.int32)[None], order])
    if joined:
        shapes = jax.ShapeDtypeStruct((NX, row_count, width), jnp.bfloat16)
        specs = vmem()
    else:
        shapes = [jax.ShapeDtypeStruct((row_count, width), jnp.bfloat16)] * NX
        specs = [vmem()] * NX
    return pl.pallas_call(
        lambda *refs: spread_kernel(contract, len(own), *refs),
        out_shape=shapes,
        in_specs=[smem()] + [vmem()] * (2 * len(own)) + [anywhere()] * 8,
        out_specs=specs,
        scratch_shapes=[
            pltpu.VMEM((NX, 2) + mine[0].shape, jnp.bfloat16),
            pltpu.SemaphoreType.DMA((NX, 2)),
        ],
        compiler_params=pltpu.CompilerParams(vmem_limit_bytes=28 * MB),
        cost_estimate=pl.CostEstimate(
            flops=4 * row_count * width * depth * NX,
            bytes_accessed=4 * NX * depth * width + 4 * row_count * (depth + 2 * width),
            transcendentals=0,
        ),
    )(info, *own, *theirs, *mine, *other)


SCALING = 1.0 / math.sqrt(HS)
SPAN = GROUP * HS


def forward_kernel(projected, prev_kv, mask, head_out, logs):
    keys = jnp.concatenate([prev_kv[:, :HS], projected[:, SPAN : SPAN + HS]], axis=0)
    values = jnp.concatenate([prev_kv[:, HS:], projected[:, SPAN + HS :]], axis=0)
    turned = values.T

    @pl.loop(0, GROUP)
    def _(h):
        lanes = pl.ds(pl.multiple_of(h * HS, HS), HS)
        scores = dot(keys, projected[:, lanes], NT) * SCALING
        scores = jnp.where(mask[...] > 0, scores, -1e30)
        highest = jnp.max(scores, axis=0, keepdims=True)
        raised = jnp.exp(scores - highest)
        total = jnp.sum(raised, axis=0, keepdims=True)
        logs[h, 0:1] = highest
        logs[h, 1:2] = 1.0 / total
        low = (raised * (1.0 / total)).astype(jnp.bfloat16)
        head_out[:, lanes] = dot(turned, low).T.astype(jnp.bfloat16)


def backward_kernel(projected, prev_kv, mask, head_out, logs, grad_heads, dq, dkv_prev, dkv_own, dk, dv):
    rows = projected.shape[0]
    keys = jnp.concatenate([prev_kv[:, :HS], projected[:, SPAN : SPAN + HS]], axis=0)
    values = jnp.concatenate([prev_kv[:, HS:], projected[:, SPAN + HS :]], axis=0)
    turned = keys.T
    dk[...] = jnp.zeros_like(dk)
    dv[...] = jnp.zeros_like(dv)

    @pl.loop(0, GROUP)
    def _(h):
        lanes = pl.ds(pl.multiple_of(h * HS, HS), HS)
        query, grad = projected[:, lanes], grad_heads[:, lanes]
        scores = dot(keys, query, NT) * SCALING
        scores = jnp.where(mask[...] > 0, scores, -1e30)
        probability = jnp.exp(scores - logs[h, 0:1]) * logs[h, 1:2]
        overlap = grad.astype(jnp.float32) * head_out[:, lanes].astype(jnp.float32)
        delta = jnp.sum(overlap.T, axis=0, keepdims=True)
        score_grad = (probability * (dot(values, grad, NT) - delta)).astype(jnp.bfloat16)
        dv[...] += dot(probability.astype(jnp.bfloat16), grad)
        dk[...] += dot(score_grad, query)
        dq[:, lanes] = (dot(turned, score_grad) * SCALING).T.astype(jnp.bfloat16)

    dkv_prev[:, :HS] = (dk[:rows] * SCALING).astype(jnp.bfloat16)
    dkv_prev[:, HS:] = dv[:rows].astype(jnp.bfloat16)
    dkv_own[:, :HS] = dk[rows:] * SCALING
    dkv_own[:, HS:] = dv[rows:]


def attend(projected, prev_kv, mask):
    rows = projected.shape[0]
    return pl.pallas_call(
        forward_kernel,
        out_shape=(
            jax.ShapeDtypeStruct((rows, SPAN), jnp.bfloat16),
            jax.ShapeDtypeStruct((GROUP, 8, rows), jnp.float32),
        ),
        in_specs=[vmem()] * 3,
        out_specs=(vmem(), vmem()),
        compiler_params=pltpu.CompilerParams(vmem_limit_bytes=24 * MB),
        cost_estimate=pl.CostEstimate(
            flops=8 * rows * rows * HS * GROUP * 2, bytes_accessed=4 * MB,
            transcendentals=2 * rows * rows * GROUP,
        ),
    )(projected, prev_kv, mask)


def attend_back(projected, prev_kv, mask, head_out, logs, grad_heads):
    rows = projected.shape[0]
    return pl.pallas_call(
        backward_kernel,
        out_shape=(
            jax.ShapeDtypeStruct((rows, SPAN), jnp.bfloat16),
            jax.ShapeDtypeStruct((rows, 2 * HS), jnp.bfloat16),
            jax.ShapeDtypeStruct((rows, 2 * HS), jnp.float32),
        ),
        in_specs=[vmem()] * 6,
        out_specs=(vmem(), vmem(), vmem()),
        scratch_shapes=[pltpu.VMEM((2 * rows, HS), jnp.float32)] * 2,
        compiler_params=pltpu.CompilerParams(vmem_limit_bytes=24 * MB),
        cost_estimate=pl.CostEstimate(
            flops=20 * rows * rows * HS * GROUP * 2, bytes_accessed=5 * MB,
            transcendentals=2 * rows * rows * GROUP,
        ),
    )(projected, prev_kv, mask, head_out, logs, grad_heads)


def exchange(array, leaving, landing):
    row_count, width = array.shape
    block_count, slot_total = row_count // BLK, leaving.shape[0]
    y_index, core = lax.axis_index("dp") // 2, lax.axis_index("dp") % 2
    z_hi = lax.axis_index("seq")
    apart = jnp.arange(4, dtype=jnp.int32)
    there = (
        (y_index + jnp.array(OFFSETS, jnp.int32)[None, :]) % NY * 4
        + (core ^ (apart // 2))[:, None] * 2
        + (z_hi ^ (apart % 2))[:, None]
    ).reshape(-1)
    blocks = array.reshape(block_count, BLK, width)
    chosen = leaving[there]
    relative = jnp.where(
        (chosen >= 0)[:, None, None],
        blocks[jnp.maximum(chosen, 0)],
        jnp.zeros((), jnp.bfloat16),
    )
    arrived = route_blocks(relative.reshape(4, NY, BLK, width))
    source_of = (
        jnp.zeros((block_count,), jnp.int32)
        .at[jnp.where(landing >= 0, landing, block_count)]
        .set(jnp.arange(slot_total, dtype=jnp.int32), mode="drop")
    )
    step = (y_index - source_of // 4) % NY
    place_of = (
        jnp.array(POSITION, jnp.int32)[step] * 4
        + (core ^ (source_of // 2 % 2)) * 2
        + (z_hi ^ (source_of % 2))
    )
    return arrived[place_of].reshape(row_count, width)


def body(activations, qkv_weight, out_weight, grad_out, segments, send_list, recv_list):
    row_count, shard_width = activations.shape
    dp_index = lax.axis_index("dp")
    seq_index = lax.axis_index("seq")
    tensor_index = lax.axis_index("tensor")
    y_index, core = dp_index // 2, dp_index % 2
    x_index, z_lo = tensor_index // 2, tensor_index % 2
    straight = core == z_lo

    in_own, out_own = qkv_weight[:, 0, :], out_weight[0]

    def join_z(own, near, far, axis):
        here = jnp.where(straight, own, near)
        return jnp.where(
            seq_index == 0,
            jnp.concatenate([here, far], axis=axis),
            jnp.concatenate([far, here], axis=axis),
        )

    in_mine = y_ring(join_z(in_own, z_near(in_own), z_far(in_own), 0), 0)
    in_other = [over_cores(w) for w in in_mine]
    out_mine = [join_z(w, z_near(w), z_far(w), 1) for w in y_ring(out_own, 0)]
    out_other = [over_cores(w) for w in out_mine]

    send_slots, recv_slots = send_list[0], recv_list[0]
    moved = exchange(activations, send_slots, recv_slots)

    def gather_x(block):
        return lax.all_gather(
            block, "tensor", axis=0, tiled=False, axis_index_groups=X_GROUPS
        )

    grad_x = gather_x(grad_out)
    moved_x = gather_x(moved)

    chunk_order = (y_index + jnp.array(OFFSETS, jnp.int32)) % NY

    def sum_z(rows, mine, other, contract):
        give = sum_product(straight, chunk_order, rows, mine, other, contract, jnp.bfloat16)
        keep = sum_product(~straight, chunk_order, rows, mine, other, contract, jnp.float32)
        return (keep + over_z_lo(give).astype(jnp.float32)).astype(jnp.bfloat16)

    projected = sum_z(moved_x, in_mine, in_other, NN)
    grad_heads = sum_z(grad_x, out_mine, out_other, NT)

    prev_kv = send(
        projected[:, SPAN:], lambda x, y, zh, zl, c: (x, y, 1, zl, c) if zh == 0 else None
    )
    query_ids = lax.dynamic_slice_in_dim(segments, seq_index * row_count, row_count)
    padded_ids = jnp.concatenate([jnp.full((row_count,), -1, jnp.int32), segments])
    key_ids = lax.dynamic_slice_in_dim(padded_ids, seq_index * row_count, 2 * row_count)
    positions = jnp.arange(2 * row_count)
    mask = (
        (query_ids[None, :] == key_ids[:, None])
        & (positions[:, None] <= positions[None, :row_count] + row_count)
    ).astype(jnp.float32)
    head_out, logs = attend(projected, prev_kv, mask)

    def target_order(base):
        return jnp.array(POSITION, jnp.int32)[(base + jnp.arange(NX) - y_index) % NY]

    parts = spread_product(
        ~straight,
        target_order(0),
        [head_out],
        [over_z_lo(head_out)],
        out_mine,
        out_other,
        NN,
        True,
    )
    attended = lax.psum_scatter(
        parts.reshape(NX * row_count, shard_width),
        "tensor",
        scatter_dimension=0,
        tiled=True,
        axis_index_groups=X_GROUPS,
    )

    grad_queries, dkv_prev, dkv_own = attend_back(
        projected, prev_kv, mask, head_out, logs, grad_heads
    )
    back_kv = send(
        dkv_prev, lambda x, y, zh, zl, c: (x, y, 0, zl, c) if zh == 1 else None
    )
    kv_total = (dkv_own + back_kv.astype(jnp.float32)).astype(jnp.bfloat16)
    here, up, across, down = spread_product(
        ~straight,
        target_order(x_index),
        [grad_queries, kv_total],
        [over_z_lo(grad_queries), over_z_lo(kv_total)],
        in_mine,
        in_other,
        NT,
        False,
    )

    def along_x(block, distance):
        return send(block, lambda x, y, zh, zl, c: (x + distance, y, zh, zl, c))

    half = row_count // 2
    from_below = along_x(across[:half], 1)
    from_above = along_x(across[half:], -1)
    wide = lambda block: block.astype(jnp.float32)
    up = jnp.concatenate(
        [(wide(up[:half]) + wide(from_below)).astype(jnp.bfloat16), up[half:]], axis=0
    )
    down = jnp.concatenate(
        [down[:half], (wide(down[half:]) + wide(from_above)).astype(jnp.bfloat16)], axis=0
    )
    grad_moved = (
        wide(here) + wide(along_x(up, 1)) + wide(along_x(down, -1))
    ).astype(jnp.bfloat16)

    return (attended, exchange(grad_moved, recv_slots, send_slots))


def solution(mesh):
    placed = (
        P(("dp", "seq"), "tensor"),
        P(("dp", "seq"), "tensor", None),
        P("tensor", None, ("dp", "seq")),
        P(("dp", "seq"), "tensor"),
        P("dp"),
        P(("dp", "seq"), None),
        P(("dp", "seq"), None),
    )
    return jax.shard_map(
        body,
        mesh=mesh,
        in_specs=placed,
        out_specs=(P(("dp", "seq"), "tensor"), P(("dp", "seq"), "tensor")),
        check_vma=False,
    )
```

```python
import math

import jax
import jax.numpy as jnp
from jax import lax
from jax.experimental import pallas as pl
from jax.experimental.pallas import tpu as pltpu
from jax.sharding import PartitionSpec as P

HS = 128
GROUP = 6
BLK = 32
AXES = ("dp", "seq", "tensor")
NX, NY, NZ = 4, 4, 4
X_GROUPS = [[0, 2, 4, 6], [1, 3, 5, 7]]


def place(index):
    dp, seq, tensor = index // 16, index // 8 % 2, index % 8
    return tensor // 2, dp // 2, seq, tensor % 2, dp % 2


def index_of(x, y, z_hi, z_lo, core):
    return (y % NY * 2 + core) * 16 + z_hi * 8 + x % NX * 2 + z_lo


def send(block, target):
    pairs = []
    for source in range(128):
        goal = target(*place(source))
        if goal is not None:
            pairs.append((source, index_of(*goal)))
    return lax.ppermute(block, AXES, pairs)


def along_y(block, distance):
    return send(block, lambda x, y, zh, zl, c: (x, y - distance, zh, zl, c))


def over_cores(block):
    return send(block, lambda x, y, zh, zl, c: (x, y, zh, zl, 1 - c))


def over_z_lo(block):
    return send(block, lambda x, y, zh, zl, c: (x, y, zh, 1 - zl, c))


def z_near(block):
    return send(
        block, lambda x, y, zh, zl, c: (x, y, zh, 1 - zl, 1 - c) if zl != c else None
    )


def z_far(block):
    return send(
        block,
        lambda x, y, zh, zl, c: (x, y, 1 - zh, zl, c)
        if zl == c
        else (x, y, 1 - zh, 1 - zl, 1 - c),
    )


def stage_one(relative):
    def over(block, dc, dz):
        return send(block, lambda x, y, zh, zl, c: (x, y, zh ^ dz, zl, c ^ dc))

    return [over(relative[1], 0, 1), over(relative[2], 1, 0), over(relative[3], 1, 1)]


def stage_two(held):
    return [along_y(held[1], -1), along_y(held[2], 1), along_y(held[3], 2)]


def nothing(*refs):
    pass


def fence(values, after=()):
    return pl.pallas_call(
        nothing,
        out_shape=[jax.ShapeDtypeStruct(v.shape, v.dtype) for v in values],
        in_specs=[anywhere()] * (len(values) + len(after)),
        out_specs=[anywhere()] * len(values),
        input_output_aliases={i: i for i in range(len(values))},
        cost_estimate=pl.CostEstimate(flops=0, bytes_accessed=0, transcendentals=0),
    )(*values, *after)


def dot(a, b, contract=((1,), (0,))):
    return lax.dot_general(a, b, (contract, ((), ())), preferred_element_type=jnp.float32)


NT = ((1,), (1,))
NN = ((1,), (0,))
MB = 1 << 20
OFFSETS = (0, 1, -1, 2)
POSITION = (0, 1, 3, 2)
TILE = 256


def vmem():
    return pl.BlockSpec(memory_space=pltpu.VMEM)


def smem():
    return pl.BlockSpec(memory_space=pltpu.SMEM)


def anywhere():
    return pl.BlockSpec(memory_space=pl.ANY)


def views(refs):
    return [v for r in refs for v in ([r.at[i] for i in range(r.shape[0])] if len(r.shape) == 3 else [r])]


def span(start, size):
    return pl.ds(start if isinstance(start, int) else pl.multiple_of(start, size), size)


def sum_kernel(contract, count, info, rows, *refs):
    mine, other = views(refs[:count]), views(refs[count : 2 * count])
    out, lhs, held, lhs_sems, sems = refs[2 * count :]
    depth = rows.shape[2]
    tiles = out.shape[1] // TILE

    def source(ref, tile):
        cut = span(tile * TILE, TILE)
        return ref.at[cut] if contract == NT else ref.at[:, cut]

    def landing(tile, chunk):
        cut, deep = span(tile * TILE, TILE), span(chunk * depth, depth)
        return held.at[cut, deep] if contract == NT else held.at[deep, cut]

    copies = [
        pltpu.make_async_copy(rows.at[k], lhs.at[:, span(k * depth, depth)], lhs_sems.at[k])
        for k in range(NY)
    ]
    for copy in copies:
        copy.start()
    for pick, weights in ((0, mine), (1, other)):

        @pl.when(info[0] == pick)
        def _():
            @pl.loop(0, tiles)
            def _(tile):
                for s in range(NY):
                    pltpu.make_async_copy(
                        source(weights[s], tile), landing(tile, info[1 + s]), sems.at[tile, s]
                    ).start()

    for copy in copies:
        copy.wait()

    @pl.loop(0, tiles)
    def _(tile):
        for s in range(NY):
            pltpu.make_async_copy(
                source(mine[s], tile), landing(tile, info[1 + s]), sems.at[tile, s]
            ).wait()
        cut = span(tile * TILE, TILE)
        weight = held[cut, :] if contract == NT else held[:, cut]
        out[:, cut] = dot(lhs[...], weight, contract).astype(out.dtype)


def sum_product(use_other, chunk_order, rows, mine, other, contract, dtype):
    row_count, depth = rows.shape[1:]
    width = mine[0].shape[-1] if contract == NN else mine[0].shape[-2]
    full = NY * depth
    info = jnp.concatenate([use_other.astype(jnp.int32)[None], chunk_order])
    return pl.pallas_call(
        lambda *refs: sum_kernel(contract, len(mine), *refs),
        out_shape=jax.ShapeDtypeStruct((row_count, width), dtype),
        in_specs=[smem()] + [anywhere()] * (1 + 2 * len(mine)),
        out_specs=vmem(),
        scratch_shapes=[
            pltpu.VMEM((row_count, full), jnp.bfloat16),
            pltpu.VMEM((full, width) if contract == NN else (width, full), jnp.bfloat16),
            pltpu.SemaphoreType.DMA((NY,)),
            pltpu.SemaphoreType.DMA((width // TILE, NY)),
        ],
        compiler_params=pltpu.CompilerParams(vmem_limit_bytes=56 * MB),
        cost_estimate=pl.CostEstimate(
            flops=2 * row_count * width * full,
            bytes_accessed=2 * full * (width + row_count),
            transcendentals=0,
        ),
    )(info, rows, *mine, *other)


def spread_kernel(contract, parts, count, info, *refs):
    own, theirs = refs[:parts], refs[parts : 2 * parts]
    weights = views(refs[2 * parts : 2 * parts + 2 * count])
    outs = refs[2 * parts + 2 * count : -4]
    lhs, held, lhs_sems, sems = refs[-4:]
    depth = lhs.shape[1] // 2
    copies, start = [], 0
    for piece in (*own, *theirs):
        copies.append(
            pltpu.make_async_copy(
                piece, lhs.at[:, pl.ds(start, piece.shape[1])], lhs_sems.at[len(copies)]
            )
        )
        copies[-1].start()
        start += piece.shape[1]

    def landing(j, side):
        deep = pl.ds(side * depth, depth)
        return held.at[j, :, deep] if contract == NT else held.at[j, deep]

    for j in range(NX):
        for pick in range(2):
            for s in range(NY):

                @pl.when((info[0] == pick) & (info[1 + j] == s))
                def _():
                    for side in range(2):
                        pltpu.make_async_copy(
                            weights[(pick ^ side) * NY + s], landing(j, side), sems.at[j, side]
                        ).start()

    for copy in copies:
        copy.wait()
    for j in range(NX):
        for side in range(2):
            pltpu.make_async_copy(weights[0], landing(j, side), sems.at[j, side]).wait()
        out = outs[0].at[j] if len(outs) == 1 else outs[j]

        @pl.loop(0, out.shape[1] // TILE)
        def _(tile):
            cut = span(tile * TILE, TILE)
            weight = held[j, cut, :] if contract == NT else held[j, :, cut]
            out[:, cut] = dot(lhs[...], weight, contract).astype(out.dtype)


def spread_product(use_other, order, own, theirs, mine, other, contract, joined):
    row_count = own[0].shape[0]
    full = 2 * sum(p.shape[1] for p in own)
    width = mine[0].shape[-1] if contract == NN else mine[0].shape[-2]
    info = jnp.concatenate([use_other.astype(jnp.int32)[None], order])
    if joined:
        shapes = jax.ShapeDtypeStruct((NX, row_count, width), jnp.bfloat16)
        specs = vmem()
    else:
        shapes = [jax.ShapeDtypeStruct((row_count, width), jnp.bfloat16)] * NX
        specs = [vmem()] * NX
    return pl.pallas_call(
        lambda *refs: spread_kernel(contract, len(own), len(mine), *refs),
        out_shape=shapes,
        in_specs=[smem()] + [anywhere()] * (2 * len(own) + 2 * len(mine)),
        out_specs=specs,
        scratch_shapes=[
            pltpu.VMEM((row_count, full), jnp.bfloat16),
            pltpu.VMEM((NX, full, width) if contract == NN else (NX, width, full), jnp.bfloat16),
            pltpu.SemaphoreType.DMA((2 * len(own),)),
            pltpu.SemaphoreType.DMA((NX, 2)),
        ],
        compiler_params=pltpu.CompilerParams(vmem_limit_bytes=56 * MB),
        cost_estimate=pl.CostEstimate(
            flops=2 * row_count * width * full * NX,
            bytes_accessed=2 * NX * full * width + 2 * row_count * (full + NX * width),
            transcendentals=0,
        ),
    )(info, *own, *theirs, *mine, *other)


SCALING = 1.0 / math.sqrt(HS)
SPAN = GROUP * HS


def forward_kernel(projected, prev_kv, mask, head_out, logs):
    keys = jnp.concatenate([prev_kv[:, :HS], projected[:, SPAN : SPAN + HS]], axis=0)
    values = jnp.concatenate([prev_kv[:, HS:], projected[:, SPAN + HS :]], axis=0)
    turned = values.T

    @pl.loop(0, GROUP)
    def _(h):
        lanes = pl.ds(pl.multiple_of(h * HS, HS), HS)
        scores = dot(keys, projected[:, lanes], NT) * SCALING
        scores = jnp.where(mask[...] > 0, scores, -1e30)
        highest = jnp.max(scores, axis=0, keepdims=True)
        raised = jnp.exp(scores - highest)
        total = jnp.sum(raised, axis=0, keepdims=True)
        logs[h, 0:1] = highest
        logs[h, 1:2] = 1.0 / total
        low = (raised * (1.0 / total)).astype(jnp.bfloat16)
        head_out[:, lanes] = dot(turned, low).T.astype(jnp.bfloat16)


def backward_kernel(projected, prev_kv, mask, head_out, logs, grad_heads, dq, dkv_prev, dkv_own, dk, dv):
    rows = projected.shape[0]
    keys = jnp.concatenate([prev_kv[:, :HS], projected[:, SPAN : SPAN + HS]], axis=0)
    values = jnp.concatenate([prev_kv[:, HS:], projected[:, SPAN + HS :]], axis=0)
    turned = keys.T
    dk[...] = jnp.zeros_like(dk)
    dv[...] = jnp.zeros_like(dv)

    @pl.loop(0, GROUP)
    def _(h):
        lanes = pl.ds(pl.multiple_of(h * HS, HS), HS)
        query, grad = projected[:, lanes], grad_heads[:, lanes]
        scores = dot(keys, query, NT) * SCALING
        scores = jnp.where(mask[...] > 0, scores, -1e30)
        probability = jnp.exp(scores - logs[h, 0:1]) * logs[h, 1:2]
        overlap = grad.astype(jnp.float32) * head_out[:, lanes].astype(jnp.float32)
        delta = jnp.sum(overlap.T, axis=0, keepdims=True)
        score_grad = (probability * (dot(values, grad, NT) - delta)).astype(jnp.bfloat16)
        dv[...] += dot(probability.astype(jnp.bfloat16), grad)
        dk[...] += dot(score_grad, query)
        dq[:, lanes] = (dot(turned, score_grad) * SCALING).T.astype(jnp.bfloat16)

    dkv_prev[:, :HS] = (dk[:rows] * SCALING).astype(jnp.bfloat16)
    dkv_prev[:, HS:] = dv[:rows].astype(jnp.bfloat16)
    dkv_own[:, :HS] = dk[rows:] * SCALING
    dkv_own[:, HS:] = dv[rows:]


def attend(projected, prev_kv, mask):
    rows = projected.shape[0]
    return pl.pallas_call(
        forward_kernel,
        out_shape=(
            jax.ShapeDtypeStruct((rows, SPAN), jnp.bfloat16),
            jax.ShapeDtypeStruct((GROUP, 8, rows), jnp.float32),
        ),
        in_specs=[vmem()] * 3,
        out_specs=(vmem(), vmem()),
        compiler_params=pltpu.CompilerParams(vmem_limit_bytes=56 * MB),
        cost_estimate=pl.CostEstimate(
            flops=8 * rows * rows * HS * GROUP * 2, bytes_accessed=4 * MB,
            transcendentals=2 * rows * rows * GROUP,
        ),
    )(projected, prev_kv, mask)


def attend_back(projected, prev_kv, mask, head_out, logs, grad_heads):
    rows = projected.shape[0]
    return pl.pallas_call(
        backward_kernel,
        out_shape=(
            jax.ShapeDtypeStruct((rows, SPAN), jnp.bfloat16),
            jax.ShapeDtypeStruct((rows, 2 * HS), jnp.bfloat16),
            jax.ShapeDtypeStruct((rows, 2 * HS), jnp.float32),
        ),
        in_specs=[vmem()] * 6,
        out_specs=(vmem(), vmem(), vmem()),
        scratch_shapes=[pltpu.VMEM((2 * rows, HS), jnp.float32)] * 2,
        compiler_params=pltpu.CompilerParams(vmem_limit_bytes=56 * MB),
        cost_estimate=pl.CostEstimate(
            flops=20 * rows * rows * HS * GROUP * 2, bytes_accessed=5 * MB,
            transcendentals=2 * rows * rows * GROUP,
        ),
    )(projected, prev_kv, mask, head_out, logs, grad_heads)


def pick_blocks(array, wanted):
    blocks = array.reshape(-1, BLK, array.shape[1])
    return jnp.where(
        (wanted >= 0)[:, None, None],
        blocks[jnp.maximum(wanted, 0)],
        jnp.zeros((), jnp.bfloat16),
    )


def sources(landing, block_count):
    return (
        jnp.zeros((block_count,), jnp.int32)
        .at[jnp.where(landing >= 0, landing, block_count)]
        .set(jnp.arange(landing.shape[0], dtype=jnp.int32), mode="drop")
    )


def relative_blocks(array, leaving):
    y_index, core = lax.axis_index("dp") // 2, lax.axis_index("dp") % 2
    z_hi = lax.axis_index("seq")
    apart = jnp.arange(4, dtype=jnp.int32)
    there = (
        (y_index + jnp.array(OFFSETS, jnp.int32)[None, :]) % NY * 4
        + (core ^ (apart // 2))[:, None] * 2
        + (z_hi ^ (apart % 2))[:, None]
    ).reshape(-1)
    return pick_blocks(array, leaving[there]).reshape(4, NY, BLK, array.shape[1])


def place_blocks(arrived, landing, block_count):
    y_index, core = lax.axis_index("dp") // 2, lax.axis_index("dp") % 2
    z_hi = lax.axis_index("seq")
    source_of = sources(landing, block_count)
    step = (y_index - source_of // 4) % NY
    place_of = (
        jnp.array(POSITION, jnp.int32)[step] * 4
        + (core ^ (source_of // 2 % 2)) * 2
        + (z_hi ^ (source_of % 2))
    )
    return arrived[place_of].reshape(block_count * BLK, arrived.shape[-1])


def body(activations, qkv_weight, out_weight, grad_out, segments, send_list, recv_list):
    row_count, shard_width = activations.shape
    dp_index = lax.axis_index("dp")
    seq_index = lax.axis_index("seq")
    tensor_index = lax.axis_index("tensor")
    y_index, core = dp_index // 2, dp_index % 2
    x_index, z_lo = tensor_index // 2, tensor_index % 2
    straight = core == z_lo

    block_count = row_count // BLK
    send_slots, recv_slots = send_list[0], recv_list[0]
    in_own, out_own = qkv_weight[:, 0, :], out_weight[0]

    def join_z(own, near, far, axis):
        here = jnp.where(straight, own, near)
        return jnp.where(
            seq_index == 0,
            jnp.concatenate([here, far], axis=axis),
            jnp.concatenate([far, here], axis=axis),
        )

    def gather_x(block):
        return lax.all_gather(
            block, "tensor", axis=0, tiled=False, axis_index_groups=X_GROUPS
        )

    grad_x = gather_x(grad_out)

    relative = relative_blocks(activations, send_slots)
    in_near, in_far, out_up, out_down, *came = fence(
        [
            z_near(in_own),
            z_far(in_own),
            along_y(out_own, 1),
            along_y(out_own, -1),
            *stage_one(relative),
        ]
    )

    in_zero = join_z(in_own, in_near, in_far, 0)
    out_three = jnp.stack([out_own, out_up, out_down])
    half = out_own.shape[0] // 2
    held = jnp.stack([relative[0], *came], axis=1)
    in_up, in_down, near, far, first, second, *came = fence(
        [
            along_y(in_zero, 1),
            along_y(in_zero, -1),
            z_near(out_three),
            z_far(out_three),
            along_y(out_up[:half], 1),
            along_y(out_down[half:], -1),
            *stage_two(held),
        ],
        [grad_x],
    )
    moved = place_blocks(jnp.concatenate([held[0], *came]), recv_slots, block_count)
    moved_x = gather_x(moved)

    out_three = join_z(out_three, near, far, 2)
    out_two = jnp.concatenate([first, second], axis=0)
    half = in_zero.shape[0] // 2
    in_zero_x, in_up_x, in_down_x = over_cores(in_zero), over_cores(in_up), over_cores(in_down)
    out_three_x = over_cores(out_three)
    first, second, near, far = fence(
        [
            along_y(in_up[:half], 1),
            along_y(in_down[half:], -1),
            z_near(out_two),
            z_far(out_two),
        ],
        [in_zero_x, in_up_x, in_down_x, out_three_x],
    )

    in_two = jnp.concatenate([first, second], axis=0)
    out_two = join_z(out_two, near, far, 1)
    in_mine = [in_zero, in_up, in_down, in_two]
    in_other = [in_zero_x, in_up_x, in_down_x, over_cores(in_two)]
    out_mine = [out_three, out_two]
    out_other = [out_three_x, over_cores(out_two)]

    chunk_order = (y_index + jnp.array(OFFSETS, jnp.int32)) % NY

    def sum_z(rows, mine, other, contract):
        give = sum_product(straight, chunk_order, rows, mine, other, contract, jnp.bfloat16)
        keep = sum_product(~straight, chunk_order, rows, mine, other, contract, jnp.float32)
        return (keep + over_z_lo(give).astype(jnp.float32)).astype(jnp.bfloat16)

    projected = sum_z(moved_x, in_mine, in_other, NN)
    grad_heads = sum_z(grad_x, out_mine, out_other, NT)

    prev_kv = send(
        projected[:, SPAN:], lambda x, y, zh, zl, c: (x, y, 1, zl, c) if zh == 0 else None
    )
    query_ids = lax.dynamic_slice_in_dim(segments, seq_index * row_count, row_count)
    padded_ids = jnp.concatenate([jnp.full((row_count,), -1, jnp.int32), segments])
    key_ids = lax.dynamic_slice_in_dim(padded_ids, seq_index * row_count, 2 * row_count)
    positions = jnp.arange(2 * row_count)
    mask = (
        (query_ids[None, :] == key_ids[:, None])
        & (positions[:, None] <= positions[None, :row_count] + row_count)
    ).astype(jnp.float32)
    head_out, logs = attend(projected, prev_kv, mask)

    def target_order(base):
        return jnp.array(POSITION, jnp.int32)[(base + jnp.arange(NX) - y_index) % NY]

    parts = spread_product(
        ~straight,
        target_order(0),
        [head_out],
        [over_z_lo(head_out)],
        out_mine,
        out_other,
        NN,
        True,
    )
    attended = lax.psum_scatter(
        parts.reshape(NX * row_count, shard_width),
        "tensor",
        scatter_dimension=0,
        tiled=True,
        axis_index_groups=X_GROUPS,
    )

    grad_queries, dkv_prev, dkv_own = attend_back(
        projected, prev_kv, mask, head_out, logs, grad_heads
    )
    back_kv = send(
        dkv_prev, lambda x, y, zh, zl, c: (x, y, 0, zl, c) if zh == 1 else None
    )
    kv_total = (dkv_own + back_kv.astype(jnp.float32)).astype(jnp.bfloat16)
    here, up, across, down = spread_product(
        ~straight,
        target_order(x_index),
        [grad_queries, kv_total],
        [over_z_lo(grad_queries), over_z_lo(kv_total)],
        in_mine,
        in_other,
        NT,
        False,
    )

    def along_x(block, distance):
        return send(block, lambda x, y, zh, zl, c: (x + distance, y, zh, zl, c))

    half = row_count // 2
    from_below = along_x(across[:half], 1)
    from_above = along_x(across[half:], -1)
    wide = lambda block: block.astype(jnp.float32)
    up = jnp.concatenate(
        [(wide(up[:half]) + wide(from_below)).astype(jnp.bfloat16), up[half:]], axis=0
    )
    down = jnp.concatenate(
        [down[:half], (wide(down[half:]) + wide(from_above)).astype(jnp.bfloat16)], axis=0
    )
    grad_moved = (
        wide(here) + wide(along_x(up, 1)) + wide(along_x(down, -1))
    ).astype(jnp.bfloat16)

    returned = lax.all_to_all(
        pick_blocks(grad_moved, recv_slots),
        ("dp", "seq"),
        split_axis=0,
        concat_axis=0,
        tiled=True,
    )
    grad_in = returned[sources(send_slots, block_count)]
    return (attended, grad_in.reshape(row_count, shard_width))


def solution(mesh):
    placed = (
        P(("dp", "seq"), "tensor"),
        P(("dp", "seq"), "tensor", None),
        P("tensor", None, ("dp", "seq")),
        P(("dp", "seq"), "tensor"),
        P("dp"),
        P(("dp", "seq"), None),
        P(("dp", "seq"), None),
    )
    return jax.shard_map(
        body,
        mesh=mesh,
        in_specs=placed,
        out_specs=(P(("dp", "seq"), "tensor"), P(("dp", "seq"), "tensor")),
        check_vma=False,
    )
```

```python
import math

import jax
import jax.numpy as jnp
from jax import lax
from jax.experimental import pallas as pl
from jax.experimental.pallas import tpu as pltpu
from jax.sharding import PartitionSpec as P

HS = 128
GROUP = 6
BLK = 32
AXES = ("dp", "seq", "tensor")
NX, NY, NZ = 4, 4, 4
X_GROUPS = [[0, 2, 4, 6], [1, 3, 5, 7]]


def place(index):
    dp, seq, tensor = index // 16, index // 8 % 2, index % 8
    return tensor // 2, dp // 2, seq, tensor % 2, dp % 2


def index_of(x, y, z_hi, z_lo, core):
    return (y % NY * 2 + core) * 16 + z_hi * 8 + x % NX * 2 + z_lo


def send(block, target):
    pairs = []
    for source in range(128):
        goal = target(*place(source))
        if goal is not None:
            pairs.append((source, index_of(*goal)))
    return lax.ppermute(block, AXES, pairs)


def along_y(block, distance):
    return send(block, lambda x, y, zh, zl, c: (x, y - distance, zh, zl, c))


def over_cores(block):
    return send(block, lambda x, y, zh, zl, c: (x, y, zh, zl, 1 - c))


def over_z_lo(block):
    return send(block, lambda x, y, zh, zl, c: (x, y, zh, 1 - zl, c))


def z_near(block):
    return send(
        block, lambda x, y, zh, zl, c: (x, y, zh, 1 - zl, 1 - c) if zl != c else None
    )


def z_far(block):
    return send(
        block,
        lambda x, y, zh, zl, c: (x, y, 1 - zh, zl, c)
        if zl == c
        else (x, y, 1 - zh, 1 - zl, 1 - c),
    )


def along_x(block, distance):
    return send(block, lambda x, y, zh, zl, c: (x - distance, y, zh, zl, c))


def route_blocks(buffer):
    return lax.all_to_all(buffer, ("dp", "seq"), split_axis=0, concat_axis=0, tiled=True)


def nothing(*refs):
    pass


def fence(values, after=()):
    return pl.pallas_call(
        nothing,
        out_shape=[jax.ShapeDtypeStruct(v.shape, v.dtype) for v in values],
        in_specs=[anywhere()] * (len(values) + len(after)),
        out_specs=[anywhere()] * len(values),
        input_output_aliases={i: i for i in range(len(values))},
        cost_estimate=pl.CostEstimate(flops=0, bytes_accessed=0, transcendentals=0),
    )(*values, *after)


def dot(a, b, contract=((1,), (0,))):
    return lax.dot_general(a, b, (contract, ((), ())), preferred_element_type=jnp.float32)


NT = ((1,), (1,))
NN = ((1,), (0,))
MB = 1 << 20
OFFSETS = (0, 1, -1, 2)
POSITION = (0, 1, 3, 2)


def vmem():
    return pl.BlockSpec(memory_space=pltpu.VMEM)


def smem():
    return pl.BlockSpec(memory_space=pltpu.SMEM)


def anywhere():
    return pl.BlockSpec(memory_space=pl.ANY)


def views(refs):
    return [v for r in refs for v in ([r.at[i] for i in range(r.shape[0])] if len(r.shape) == 3 else [r])]


def span(start, size):
    return pl.ds(start if isinstance(start, int) else pl.multiple_of(start, size), size)


def params():
    return pltpu.CompilerParams(vmem_limit_bytes=56 * MB)


def start_all(copies):
    for copy in copies:
        copy.start()


def wait_all(copies):
    for copy in copies:
        copy.wait()


def proj_kernel(info, *refs):
    rows, weights, out_kv, out_q = refs[:NX], refs[NX], refs[NX + 1], refs[NX + 2]
    lhs, held, lhs_sems, sems = refs[NX + 3 :]
    depth = rows[0].shape[1]
    wide = out_q.shape[1] // 2
    cuts = [(out_kv, 0, 2 * wide, 2 * HS), (out_q, 0, 0, wide), (out_q, wide, wide, wide)]
    lhs_copies = [
        pltpu.make_async_copy(rows[r], lhs.at[:, span(info[1 + r] * depth, depth)], lhs_sems.at[r])
        for r in range(NX)
    ]
    copies = [
        [
            pltpu.make_async_copy(
                weights.at[2 * k + info[0], :, pl.ds(start, size)],
                held.at[pl.ds(k * depth, depth), pl.ds(start, size)],
                sems.at[i, k],
            )
            for k in range(NY)
        ]
        for i, (_, _, start, size) in enumerate(cuts)
    ]
    start_all(lhs_copies)
    for group in copies:
        start_all(group)
    wait_all(lhs_copies)
    for (out, at, start, size), group in zip(cuts, copies):
        wait_all(group)
        product = dot(lhs[...], held[:, pl.ds(start, size)])
        out[:, pl.ds(at, size)] = product.astype(out.dtype)


def proj_product(head, places, rows, weights, dtype):
    row_count, depth = rows[0].shape
    width, full = weights.shape[2], NX * depth
    info = jnp.concatenate([head.astype(jnp.int32)[None], places])
    return pl.pallas_call(
        proj_kernel,
        out_shape=(
            jax.ShapeDtypeStruct((row_count, 2 * HS), dtype),
            jax.ShapeDtypeStruct((row_count, SPAN), dtype),
        ),
        in_specs=[smem()] + [anywhere()] * (NX + 1),
        out_specs=(vmem(), vmem()),
        scratch_shapes=[
            pltpu.VMEM((row_count, full), jnp.bfloat16),
            pltpu.VMEM((full, width), jnp.bfloat16),
            pltpu.SemaphoreType.DMA((NX,)),
            pltpu.SemaphoreType.DMA((3, NY)),
        ],
        compiler_params=params(),
        cost_estimate=pl.CostEstimate(
            flops=2 * row_count * width * full,
            bytes_accessed=2 * full * (width + row_count),
            transcendentals=0,
        ),
    )(info, *rows, weights)


def heads_kernel(info, rows, three, two, three_x, two_x, out, lhs, held, lhs_sems, sems):
    mine, other = views([three, two]), views([three_x, two_x])
    depth = rows.shape[2]
    wide = out.shape[1] // 2

    def copies_of(weights, i):
        cut = pl.ds(i * wide, wide)
        return [
            pltpu.make_async_copy(
                weights[s].at[cut], held.at[cut, span(info[1 + s] * depth, depth)], sems.at[i, s]
            )
            for s in range(NY)
        ]

    lhs_copies = [
        pltpu.make_async_copy(rows.at[k], lhs.at[:, pl.ds(k * depth, depth)], lhs_sems.at[k])
        for k in range(NX)
    ]
    start_all(lhs_copies)
    for pick, weights in ((0, mine), (1, other)):

        @pl.when(info[0] == pick)
        def _():
            for i in range(2):
                start_all(copies_of(weights, i))

    wait_all(lhs_copies)
    for i in range(2):
        wait_all(copies_of(mine, i))
        cut = pl.ds(i * wide, wide)
        out[:, cut] = dot(lhs[...], held[cut, :], NT).astype(out.dtype)


def heads_product(use_other, chunk_order, rows, mine, other, dtype):
    row_count, depth = rows.shape[1:]
    width, full = mine[0].shape[-2], NX * depth
    info = jnp.concatenate([use_other.astype(jnp.int32)[None], chunk_order])
    return pl.pallas_call(
        heads_kernel,
        out_shape=jax.ShapeDtypeStruct((row_count, width), dtype),
        in_specs=[smem()] + [anywhere()] * 5,
        out_specs=vmem(),
        scratch_shapes=[
            pltpu.VMEM((row_count, full), jnp.bfloat16),
            pltpu.VMEM((width, full), jnp.bfloat16),
            pltpu.SemaphoreType.DMA((NX,)),
            pltpu.SemaphoreType.DMA((2, NY)),
        ],
        compiler_params=params(),
        cost_estimate=pl.CostEstimate(
            flops=2 * row_count * width * full,
            bytes_accessed=2 * full * (width + row_count),
            transcendentals=0,
        ),
    )(info, rows, *mine, *other)


def mixed_kernel(info, own, theirs, three, two, three_x, two_x, out, lhs, held, lhs_sems, sems):
    weights = views([three, two]) + views([three_x, two_x])
    depth = own.shape[1]
    lhs_copies = [
        pltpu.make_async_copy(piece, lhs.at[:, pl.ds(i * depth, depth)], lhs_sems.at[i])
        for i, piece in enumerate((own, theirs))
    ]
    start_all(lhs_copies)

    def copies_of(j, pick, s):
        return [
            pltpu.make_async_copy(
                weights[(pick ^ side) * NY + s],
                held.at[j, pl.ds(side * depth, depth)],
                sems.at[j, side],
            )
            for side in range(2)
        ]

    for j in range(NX):
        for pick in range(2):
            for s in range(NY):

                @pl.when((info[0] == pick) & (info[1 + j] == s))
                def _():
                    start_all(copies_of(j, pick, s))

    wait_all(lhs_copies)
    for j in range(NX):
        wait_all(copies_of(j, 0, 0))
        out[j] = dot(lhs[...], held[j]).astype(out.dtype)


def mixed_product(use_other, order, own, theirs, mine, other):
    row_count, depth = own.shape
    width = mine[0].shape[-1]
    info = jnp.concatenate([use_other.astype(jnp.int32)[None], order])
    return pl.pallas_call(
        mixed_kernel,
        out_shape=jax.ShapeDtypeStruct((NX, row_count, width), jnp.bfloat16),
        in_specs=[smem()] + [anywhere()] * 6,
        out_specs=vmem(),
        scratch_shapes=[
            pltpu.VMEM((row_count, 2 * depth), jnp.bfloat16),
            pltpu.VMEM((NX, 2 * depth, width), jnp.bfloat16),
            pltpu.SemaphoreType.DMA((2,)),
            pltpu.SemaphoreType.DMA((NX, 2)),
        ],
        compiler_params=params(),
        cost_estimate=pl.CostEstimate(
            flops=4 * row_count * width * depth * NX,
            bytes_accessed=4 * NX * depth * width + 2 * row_count * (2 * depth + NX * width),
            transcendentals=0,
        ),
    )(info, own, theirs, *mine, *other)


def back_kernel(info, q, kv, q_x, kv_x, weights, *refs):
    outs = refs[:NX]
    lhs, held, lhs_sems, sems = refs[NX:]
    half = lhs.shape[1] // 2
    lhs_copies = [
        pltpu.make_async_copy(piece, lhs.at[:, pl.ds(start, piece.shape[1])], lhs_sems.at[i])
        for i, (piece, start) in enumerate(
            ((q, 0), (kv, SPAN), (q_x, half), (kv_x, half + SPAN))
        )
    ]
    copies = [
        [
            pltpu.make_async_copy(
                weights.at[2 * info[1 + j] + (info[0] + side) % 2],
                held.at[j, :, pl.ds(side * half, half)],
                sems.at[j, side],
            )
            for side in range(2)
        ]
        for j in range(NX)
    ]
    order = (2, 1, 3, 0)
    start_all(lhs_copies)
    for j in order:
        start_all(copies[j])
    wait_all(lhs_copies)
    for j in order:
        wait_all(copies[j])
        outs[j][...] = dot(lhs[...], held[j], NT).astype(jnp.bfloat16)


def back_product(head, places, q, kv, q_x, kv_x, weights):
    row_count = q.shape[0]
    width, half = weights.shape[1:]
    info = jnp.concatenate([head.astype(jnp.int32)[None], places])
    return pl.pallas_call(
        back_kernel,
        out_shape=[jax.ShapeDtypeStruct((row_count, width), jnp.bfloat16)] * NX,
        in_specs=[smem()] + [anywhere()] * 5,
        out_specs=[vmem()] * NX,
        scratch_shapes=[
            pltpu.VMEM((row_count, 2 * half), jnp.bfloat16),
            pltpu.VMEM((NX, width, 2 * half), jnp.bfloat16),
            pltpu.SemaphoreType.DMA((4,)),
            pltpu.SemaphoreType.DMA((NX, 2)),
        ],
        compiler_params=params(),
        cost_estimate=pl.CostEstimate(
            flops=4 * row_count * width * half * NX,
            bytes_accessed=4 * NX * half * width + 2 * row_count * (2 * half + NX * width),
            transcendentals=0,
        ),
    )(info, q, kv, q_x, kv_x, weights)


SCALING = 1.0 / math.sqrt(HS)
SPAN = GROUP * HS


def forward_kernel(queries, own_kv, prev_kv, mask, head_out, logs):
    keys = jnp.concatenate([prev_kv[:, :HS], own_kv[:, :HS]], axis=0)
    values = jnp.concatenate([prev_kv[:, HS:], own_kv[:, HS:]], axis=0)
    turned = values.T

    @pl.loop(0, GROUP)
    def _(h):
        lanes = pl.ds(pl.multiple_of(h * HS, HS), HS)
        scores = dot(keys, queries[:, lanes], NT) * SCALING
        scores = jnp.where(mask[...] > 0, scores, -1e30)
        highest = jnp.max(scores, axis=0, keepdims=True)
        raised = jnp.exp(scores - highest)
        total = jnp.sum(raised, axis=0, keepdims=True)
        logs[h, 0:1] = highest
        logs[h, 1:2] = 1.0 / total
        low = (raised * (1.0 / total)).astype(jnp.bfloat16)
        head_out[:, lanes] = dot(turned, low).T.astype(jnp.bfloat16)


def backward_kernel(
    queries, own_kv, prev_kv, mask, head_out, logs, grad_heads, dq, dkv_prev, dkv_own, dk, dv
):
    rows = queries.shape[0]
    keys = jnp.concatenate([prev_kv[:, :HS], own_kv[:, :HS]], axis=0)
    values = jnp.concatenate([prev_kv[:, HS:], own_kv[:, HS:]], axis=0)
    turned = keys.T
    dk[...] = jnp.zeros_like(dk)
    dv[...] = jnp.zeros_like(dv)

    @pl.loop(0, GROUP)
    def _(h):
        lanes = pl.ds(pl.multiple_of(h * HS, HS), HS)
        query, grad = queries[:, lanes], grad_heads[:, lanes]
        scores = dot(keys, query, NT) * SCALING
        scores = jnp.where(mask[...] > 0, scores, -1e30)
        probability = jnp.exp(scores - logs[h, 0:1]) * logs[h, 1:2]
        overlap = grad.astype(jnp.float32) * head_out[:, lanes].astype(jnp.float32)
        delta = jnp.sum(overlap.T, axis=0, keepdims=True)
        score_grad = (probability * (dot(values, grad, NT) - delta)).astype(jnp.bfloat16)
        dv[...] += dot(probability.astype(jnp.bfloat16), grad)
        dk[...] += dot(score_grad, query)
        dq[:, lanes] = (dot(turned, score_grad) * SCALING).T.astype(jnp.bfloat16)

    dkv_prev[:, :HS] = (dk[:rows] * SCALING).astype(jnp.bfloat16)
    dkv_prev[:, HS:] = dv[:rows].astype(jnp.bfloat16)
    dkv_own[:, :HS] = dk[rows:] * SCALING
    dkv_own[:, HS:] = dv[rows:]


def attend(queries, own_kv, prev_kv, mask):
    rows = queries.shape[0]
    return pl.pallas_call(
        forward_kernel,
        out_shape=(
            jax.ShapeDtypeStruct((rows, SPAN), jnp.bfloat16),
            jax.ShapeDtypeStruct((GROUP, 8, rows), jnp.float32),
        ),
        in_specs=[vmem()] * 4,
        out_specs=(vmem(), vmem()),
        compiler_params=params(),
        cost_estimate=pl.CostEstimate(
            flops=8 * rows * rows * HS * GROUP * 2, bytes_accessed=4 * MB,
            transcendentals=2 * rows * rows * GROUP,
        ),
    )(queries, own_kv, prev_kv, mask)


def attend_back(queries, own_kv, prev_kv, mask, head_out, logs, grad_heads):
    rows = queries.shape[0]
    return pl.pallas_call(
        backward_kernel,
        out_shape=(
            jax.ShapeDtypeStruct((rows, SPAN), jnp.bfloat16),
            jax.ShapeDtypeStruct((rows, 2 * HS), jnp.bfloat16),
            jax.ShapeDtypeStruct((rows, 2 * HS), jnp.float32),
        ),
        in_specs=[vmem()] * 7,
        out_specs=(vmem(), vmem(), vmem()),
        scratch_shapes=[pltpu.VMEM((2 * rows, HS), jnp.float32)] * 2,
        compiler_params=params(),
        cost_estimate=pl.CostEstimate(
            flops=20 * rows * rows * HS * GROUP * 2, bytes_accessed=5 * MB,
            transcendentals=2 * rows * rows * GROUP,
        ),
    )(queries, own_kv, prev_kv, mask, head_out, logs, grad_heads)


def pick_blocks(array, wanted):
    blocks = array.reshape(-1, BLK, array.shape[1])
    return jnp.where(
        (wanted >= 0)[:, None, None],
        blocks[jnp.maximum(wanted, 0)],
        jnp.zeros((), jnp.bfloat16),
    )


def sources(landing, block_count):
    return (
        jnp.zeros((block_count,), jnp.int32)
        .at[jnp.where(landing >= 0, landing, block_count)]
        .set(jnp.arange(landing.shape[0], dtype=jnp.int32), mode="drop")
    )


def body(activations, qkv_weight, out_weight, grad_out, segments, send_list, recv_list):
    row_count, shard_width = activations.shape
    dp_index = lax.axis_index("dp")
    seq_index = lax.axis_index("seq")
    tensor_index = lax.axis_index("tensor")
    y_index, core = dp_index // 2, dp_index % 2
    x_index, z_lo = tensor_index // 2, tensor_index % 2
    straight = core == z_lo

    block_count = row_count // BLK
    send_slots, recv_slots = send_list[0], recv_list[0]
    in_own, out_own = qkv_weight[:, 0, :], out_weight[0]

    def join_z(own, near, far, axis):
        here = jnp.where(straight, own, near)
        return jnp.where(
            seq_index == 0,
            jnp.concatenate([here, far], axis=axis),
            jnp.concatenate([far, here], axis=axis),
        )

    def gather_x(block):
        return lax.all_gather(
            block, "tensor", axis=0, tiled=False, axis_index_groups=X_GROUPS
        )

    grad_x = gather_x(grad_out)

    in_near, in_far, out_up, out_down, arrived = fence(
        [
            z_near(in_own),
            z_far(in_own),
            along_y(out_own, 1),
            along_y(out_own, -1),
            route_blocks(pick_blocks(activations, send_slots)),
        ]
    )

    in_all = lax.all_gather(join_z(in_own, in_near, in_far, 0), "dp", axis=0, tiled=False)
    moved = arrived[sources(recv_slots, block_count)].reshape(row_count, shard_width)
    out_three = jnp.stack([out_own, out_up, out_down])
    half = out_own.shape[0] // 2
    near, far, first, second, *moved_x = fence(
        [
            z_near(out_three),
            z_far(out_three),
            along_y(out_up[:half], 1),
            along_y(out_down[half:], -1),
            along_x(moved, 1),
            along_x(moved, -1),
            along_x(moved, 2),
        ],
        [grad_x],
    )
    moved_x = [moved, *moved_x]

    out_three = join_z(out_three, near, far, 2)
    out_two = jnp.concatenate([first, second], axis=0)
    near, far, out_three_x = fence([z_near(out_two), z_far(out_two), over_cores(out_three)])
    out_two = join_z(out_two, near, far, 1)
    out_mine = [out_three, out_two]
    out_other = [out_three_x, over_cores(out_two)]

    def sum_z(keep, give):
        return (keep + over_z_lo(give).astype(jnp.float32)).astype(jnp.bfloat16)

    offsets = jnp.array(OFFSETS, jnp.int32)
    chunk_order = (y_index + offsets) % NY
    grad_heads = sum_z(
        heads_product(~straight, chunk_order, grad_x, out_mine, out_other, jnp.float32),
        heads_product(straight, chunk_order, grad_x, out_mine, out_other, jnp.bfloat16),
    )
    places = (x_index + offsets) % NX
    give_kv, give_q = proj_product(1 - z_lo, places, moved_x, in_all, jnp.bfloat16)
    keep_kv, keep_q = proj_product(z_lo, places, moved_x, in_all, jnp.float32)
    own_kv = sum_z(keep_kv, give_kv)
    queries = sum_z(keep_q, give_q)

    prev_kv = send(
        own_kv, lambda x, y, zh, zl, c: (x, y, 1, zl, c) if zh == 0 else None
    )
    query_ids = lax.dynamic_slice_in_dim(segments, seq_index * row_count, row_count)
    padded_ids = jnp.concatenate([jnp.full((row_count,), -1, jnp.int32), segments])
    key_ids = lax.dynamic_slice_in_dim(padded_ids, seq_index * row_count, 2 * row_count)
    positions = jnp.arange(2 * row_count)
    mask = (
        (query_ids[None, :] == key_ids[:, None])
        & (positions[:, None] <= positions[None, :row_count] + row_count)
    ).astype(jnp.float32)
    head_out, logs = attend(queries, own_kv, prev_kv, mask)

    order = jnp.array(POSITION, jnp.int32)[(jnp.arange(NX) - y_index) % NY]
    parts = mixed_product(
        ~straight, order, head_out, over_z_lo(head_out), out_mine, out_other
    )
    attended = lax.psum_scatter(
        parts.reshape(NX * row_count, shard_width),
        "tensor",
        scatter_dimension=0,
        tiled=True,
        axis_index_groups=X_GROUPS,
    )

    grad_queries, dkv_prev, dkv_own = attend_back(
        queries, own_kv, prev_kv, mask, head_out, logs, grad_heads
    )
    back_kv = send(
        dkv_prev, lambda x, y, zh, zl, c: (x, y, 0, zl, c) if zh == 1 else None
    )
    kv_total = (dkv_own + back_kv.astype(jnp.float32)).astype(jnp.bfloat16)
    here, up, across, down = back_product(
        z_lo,
        (x_index + jnp.arange(NX)) % NX,
        grad_queries,
        kv_total,
        over_z_lo(grad_queries),
        over_z_lo(kv_total),
        in_all,
    )

    half = row_count // 2
    from_below = along_x(across[:half], -1)
    from_above = along_x(across[half:], 1)
    wide = lambda block: block.astype(jnp.float32)
    up = jnp.concatenate(
        [(wide(up[:half]) + wide(from_below)).astype(jnp.bfloat16), up[half:]], axis=0
    )
    down = jnp.concatenate(
        [down[:half], (wide(down[half:]) + wide(from_above)).astype(jnp.bfloat16)], axis=0
    )
    grad_moved = (
        wide(here) + wide(along_x(up, -1)) + wide(along_x(down, 1))
    ).astype(jnp.bfloat16)

    returned = route_blocks(pick_blocks(grad_moved, recv_slots))
    grad_in = returned[sources(send_slots, block_count)]
    return (attended, grad_in.reshape(row_count, shard_width))


def solution(mesh):
    placed = (
        P(("dp", "seq"), "tensor"),
        P(("dp", "seq"), "tensor", None),
        P("tensor", None, ("dp", "seq")),
        P(("dp", "seq"), "tensor"),
        P("dp"),
        P(("dp", "seq"), None),
        P(("dp", "seq"), None),
    )
    return jax.shard_map(
        body,
        mesh=mesh,
        in_specs=placed,
        out_specs=(P(("dp", "seq"), "tensor"), P(("dp", "seq"), "tensor")),
        check_vma=False,
    )
```

```python
import math

import jax
import jax.numpy as jnp
from jax import lax
from jax.experimental import pallas as pl
from jax.experimental.pallas import tpu as pltpu
from jax.sharding import PartitionSpec as P

HS = 128
GROUP = 6
BLK = 32
AXES = ("dp", "seq", "tensor")
NX, NY, NZ = 4, 4, 4
X_GROUPS = [[0, 2, 4, 6], [1, 3, 5, 7]]


def place(index):
    dp, seq, tensor = index // 16, index // 8 % 2, index % 8
    return tensor // 2, dp // 2, seq, tensor % 2, dp % 2


def index_of(x, y, z_hi, z_lo, core):
    return (y % NY * 2 + core) * 16 + z_hi * 8 + x % NX * 2 + z_lo


def send(block, target):
    pairs = []
    for source in range(128):
        goal = target(*place(source))
        if goal is not None:
            pairs.append((source, index_of(*goal)))
    return lax.ppermute(block, AXES, pairs)


def along_y(block, distance):
    return send(block, lambda x, y, zh, zl, c: (x, y - distance, zh, zl, c))


def over_cores(block):
    return send(block, lambda x, y, zh, zl, c: (x, y, zh, zl, 1 - c))


def over_z_lo(block):
    return send(block, lambda x, y, zh, zl, c: (x, y, zh, 1 - zl, c))


def z_near(block):
    return send(
        block, lambda x, y, zh, zl, c: (x, y, zh, 1 - zl, 1 - c) if zl != c else None
    )


def z_far(block):
    return send(
        block,
        lambda x, y, zh, zl, c: (x, y, 1 - zh, zl, c)
        if zl == c
        else (x, y, 1 - zh, 1 - zl, 1 - c),
    )


def along_x(block, distance):
    return send(block, lambda x, y, zh, zl, c: (x - distance, y, zh, zl, c))


def route_blocks(buffer):
    return lax.all_to_all(buffer, ("dp", "seq"), split_axis=0, concat_axis=0, tiled=True)


def nothing(*refs):
    pass


def fence(values, after=()):
    return pl.pallas_call(
        nothing,
        out_shape=[jax.ShapeDtypeStruct(v.shape, v.dtype) for v in values],
        in_specs=[anywhere()] * (len(values) + len(after)),
        out_specs=[anywhere()] * len(values),
        input_output_aliases={i: i for i in range(len(values))},
        cost_estimate=pl.CostEstimate(flops=0, bytes_accessed=0, transcendentals=0),
    )(*values, *after)


def dot(a, b, contract=((1,), (0,))):
    return lax.dot_general(a, b, (contract, ((), ())), preferred_element_type=jnp.float32)


NT = ((1,), (1,))
NN = ((1,), (0,))
MB = 1 << 20
OFFSETS = (0, 1, -1, 2)
POSITION = (0, 1, 3, 2)


def vmem():
    return pl.BlockSpec(memory_space=pltpu.VMEM)


def smem():
    return pl.BlockSpec(memory_space=pltpu.SMEM)


def anywhere():
    return pl.BlockSpec(memory_space=pl.ANY)


def params(size=24):
    return pltpu.CompilerParams(vmem_limit_bytes=size * MB)


def start_all(copies):
    for copy in copies:
        copy.start()


def wait_all(copies):
    for copy in copies:
        copy.wait()


def proj_kernel(info, *refs):
    rows, weights, out_kv, out_q = refs[:NX], refs[NX], refs[NX + 1], refs[NX + 2]
    lhs, held, total, lhs_sems, sems = refs[NX + 3 :]
    copies = [
        [
            pltpu.make_async_copy(rows[r], lhs.at[r], lhs_sems.at[r]),
            pltpu.make_async_copy(
                weights.at[2 * info[1 + r] + info[0]], held.at[r], sems.at[r]
            ),
        ]
        for r in range(NX)
    ]
    start_all(copies[0])
    start_all(copies[1])
    for r in range(NX):
        wait_all(copies[r])
        if r + 2 < NX:
            start_all(copies[r + 2])
        term = dot(lhs[r], held[r])
        if r == 0:
            total[...] = term
        elif r < NX - 1:
            total[...] += term
        else:
            term = (total[...] + term).astype(out_q.dtype)
            out_q[...] = term[:, :SPAN]
            out_kv[...] = term[:, SPAN:]


def proj_product(head, places, rows, weights, dtype):
    row_count, depth = rows[0].shape
    width, full = weights.shape[2], NX * depth
    info = jnp.concatenate([head.astype(jnp.int32)[None], places])
    return pl.pallas_call(
        proj_kernel,
        out_shape=(
            jax.ShapeDtypeStruct((row_count, 2 * HS), dtype),
            jax.ShapeDtypeStruct((row_count, SPAN), dtype),
        ),
        in_specs=[smem()] + [anywhere()] * (NX + 1),
        out_specs=(vmem(), vmem()),
        scratch_shapes=[
            pltpu.VMEM((NX, row_count, depth), jnp.bfloat16),
            pltpu.VMEM((NX, depth, width), jnp.bfloat16),
            pltpu.VMEM((row_count, width), jnp.float32),
            pltpu.SemaphoreType.DMA((NX,)),
            pltpu.SemaphoreType.DMA((NX,)),
        ],
        compiler_params=params(),
        cost_estimate=pl.CostEstimate(
            flops=2 * row_count * width * full,
            bytes_accessed=2 * full * (width + row_count),
            transcendentals=0,
        ),
    )(info, *rows, weights)


def heads_kernel(info, *refs):
    rows, mine, other, out = refs[:NX], refs[NX], refs[NX + 1], refs[NX + 2]
    lhs, held, total, lhs_sems, sems = refs[NX + 3 :]

    def copies_of(weights, r):
        return [
            pltpu.make_async_copy(rows[r], lhs.at[r], lhs_sems.at[r]),
            pltpu.make_async_copy(weights.at[info[1 + r]], held.at[r], sems.at[r]),
        ]

    def begin(r):
        for pick, weights in ((0, mine), (1, other)):

            @pl.when(info[0] == pick)
            def _():
                start_all(copies_of(weights, r))

    begin(0)
    begin(1)
    for r in range(NX):
        wait_all(copies_of(mine, r))
        if r + 2 < NX:
            begin(r + 2)
        term = dot(lhs[r], held[r], NT)
        if r == 0:
            total[...] = term
        elif r < NX - 1:
            total[...] += term
        else:
            out[...] = (total[...] + term).astype(out.dtype)


def heads_product(use_other, order, rows, mine, other, dtype):
    row_count, depth = rows[0].shape
    width, full = mine.shape[1], NX * depth
    info = jnp.concatenate([use_other.astype(jnp.int32)[None], order])
    return pl.pallas_call(
        heads_kernel,
        out_shape=jax.ShapeDtypeStruct((row_count, width), dtype),
        in_specs=[smem()] + [anywhere()] * (NX + 2),
        out_specs=vmem(),
        scratch_shapes=[
            pltpu.VMEM((NX, row_count, depth), jnp.bfloat16),
            pltpu.VMEM((NX, width, depth), jnp.bfloat16),
            pltpu.VMEM((row_count, width), jnp.float32),
            pltpu.SemaphoreType.DMA((NX,)),
            pltpu.SemaphoreType.DMA((NX,)),
        ],
        compiler_params=params(),
        cost_estimate=pl.CostEstimate(
            flops=2 * row_count * width * full,
            bytes_accessed=2 * full * (width + row_count),
            transcendentals=0,
        ),
    )(info, *rows, mine, other)


def mixed_kernel(
    info, own, theirs, mine, other, out, lhs, held, ready, lhs_sems, sems, out_sems
):
    depth = own.shape[1]
    lhs_copies = [
        pltpu.make_async_copy(piece, lhs.at[:, pl.ds(i * depth, depth)], lhs_sems.at[i])
        for i, piece in enumerate((own, theirs))
    ]

    def copies_of(j, pair):
        return [
            pltpu.make_async_copy(
                weights.at[info[1 + j]], held.at[j, pl.ds(side * depth, depth)], sems.at[j, side]
            )
            for side, weights in enumerate(pair)
        ]

    def begin(j):
        for pick, pair in ((0, (mine, other)), (1, (other, mine))):

            @pl.when(info[0] == pick)
            def _():
                start_all(copies_of(j, pair))

    done = [pltpu.make_async_copy(ready.at[j], out.at[j], out_sems.at[j]) for j in range(NX)]
    begin(0)
    start_all(lhs_copies)
    wait_all(lhs_copies)
    begin(1)
    for j in range(NX):
        wait_all(copies_of(j, (mine, other)))
        if j + 2 < NX:
            begin(j + 2)
        ready[j] = dot(lhs[...], held[j]).astype(out.dtype)
        done[j].start()
    wait_all(done)


def mixed_product(use_other, order, own, theirs, mine, other):
    row_count, depth = own.shape
    width = mine.shape[-1]
    info = jnp.concatenate([use_other.astype(jnp.int32)[None], order])
    return pl.pallas_call(
        mixed_kernel,
        out_shape=jax.ShapeDtypeStruct((NX, row_count, width), jnp.bfloat16),
        in_specs=[smem()] + [anywhere()] * 4,
        out_specs=anywhere(),
        scratch_shapes=[
            pltpu.VMEM((row_count, 2 * depth), jnp.bfloat16),
            pltpu.VMEM((NX, 2 * depth, width), jnp.bfloat16),
            pltpu.VMEM((NX, row_count, width), jnp.bfloat16),
            pltpu.SemaphoreType.DMA((2,)),
            pltpu.SemaphoreType.DMA((NX, 2)),
            pltpu.SemaphoreType.DMA((NX,)),
        ],
        compiler_params=params(),
        cost_estimate=pl.CostEstimate(
            flops=4 * row_count * width * depth * NX,
            bytes_accessed=4 * NX * depth * width + 2 * row_count * (2 * depth + NX * width),
            transcendentals=0,
        ),
    )(info, own, theirs, mine, other)


def wide(value):
    return value.astype(jnp.float32)


def low(value):
    return value.astype(jnp.bfloat16)


def back_kernel(info, q, kv, kv_back, q_x, kv_x, kv_back_x, weights, *refs):
    outs, sems = refs[:NX], refs[-1]
    held = refs[NX : 2 * NX]
    copies = [pltpu.make_async_copy(held[j], outs[j], sems.at[j]) for j in range(NX)]
    kv_low = low(kv[...] + wide(kv_back[...]))
    kv_x_low = low(wide(kv_x[...]) + wide(kv_back_x[...]))
    for j in (2, 1, 3, 0):
        own = weights.at[2 * info[1 + j] + info[0]]
        theirs = weights.at[2 * info[1 + j] + 1 - info[0]]
        total = dot(q[...], own[:, :SPAN], NT) + dot(kv_low, own[:, SPAN:], NT)
        total += dot(q_x[...], theirs[:, :SPAN], NT) + dot(kv_x_low, theirs[:, SPAN:], NT)
        held[j][...] = low(total)
        copies[j].start()
    wait_all(copies)


def back_product(head, places, operands, weights):
    row_count = operands[0].shape[0]
    width, half = weights.shape[1:]
    info = jnp.concatenate([head.astype(jnp.int32)[None], places])
    return pl.pallas_call(
        back_kernel,
        out_shape=[jax.ShapeDtypeStruct((row_count, width), jnp.bfloat16)] * NX,
        in_specs=[smem()] + [vmem()] * 7,
        out_specs=[anywhere()] * NX,
        scratch_shapes=[pltpu.VMEM((row_count, width), jnp.bfloat16)] * NX
        + [pltpu.SemaphoreType.DMA((NX,))],
        compiler_params=params(36),
        cost_estimate=pl.CostEstimate(
            flops=4 * row_count * width * half * NX,
            bytes_accessed=4 * NX * half * width + 2 * row_count * (2 * half + NX * width),
            transcendentals=0,
        ),
    )(info, *operands, weights)


SCALING = 1.0 / math.sqrt(HS)
SPAN = GROUP * HS


def forward_kernel(
    keep_q, came_q, keep_kv, came_kv, prev_a, prev_b, mask, head_out, logs, queries, kv
):
    rows = keep_q.shape[0]
    queries[...] = low(keep_q[...] + wide(came_q[...]))
    kv[:rows] = low(wide(prev_a[...]) + wide(prev_b[...]))
    kv[rows:] = low(keep_kv[...] + wide(came_kv[...]))
    keys, turned = kv[:, :HS], kv[:, HS:].T

    @pl.loop(0, GROUP, unroll=GROUP)
    def _(h):
        lanes = pl.ds(pl.multiple_of(h * HS, HS), HS)
        scores = dot(keys, queries[:, lanes], NT) * SCALING
        scores = jnp.where(mask[...] > 0, scores, -1e30)
        highest = jnp.max(scores, axis=0, keepdims=True)
        raised = jnp.exp(scores - highest)
        inverse = 1.0 / jnp.sum(raised, axis=0, keepdims=True)
        logs[h, 0:1] = highest
        logs[h, 1:2] = inverse
        head_out[:, lanes] = low(dot(turned, low(raised * inverse)).T)


def backward_kernel(
    queries, kv, mask, head_out, logs, keep_grad, came_grad,
    dq, dkv_prev, dkv_own, dkv_low, dk, dv, grad_heads,
):
    rows = queries.shape[0]
    grad_heads[...] = low(keep_grad[...] + wide(came_grad[...]))
    keys, values = kv[:, :HS], kv[:, HS:]
    turned = keys.T
    dk[...] = jnp.zeros_like(dk)
    dv[...] = jnp.zeros_like(dv)

    @pl.loop(0, GROUP, unroll=GROUP)
    def _(h):
        lanes = pl.ds(pl.multiple_of(h * HS, HS), HS)
        query, grad = queries[:, lanes], grad_heads[:, lanes]
        scores = dot(keys, query, NT) * SCALING
        scores = jnp.where(mask[...] > 0, scores, -1e30)
        probability = jnp.exp(scores - logs[h, 0:1]) * logs[h, 1:2]
        delta = jnp.sum((wide(grad) * wide(head_out[:, lanes])).T, axis=0, keepdims=True)
        score_grad = low(probability * (dot(values, grad, NT) - delta))
        dv[...] += dot(low(probability), grad)
        dk[...] += dot(score_grad, query)
        dq[:, lanes] = low((dot(turned, score_grad) * SCALING).T)

    dkv_prev[:, :HS] = low(dk[:rows] * SCALING)
    dkv_prev[:, HS:] = low(dv[:rows])
    dkv_own[:, :HS] = dk[rows:] * SCALING
    dkv_own[:, HS:] = dv[rows:]
    dkv_low[...] = low(dkv_own[...])


def attend(keep_q, came_q, keep_kv, came_kv, prev_a, prev_b, mask):
    rows = keep_q.shape[0]
    return pl.pallas_call(
        forward_kernel,
        out_shape=(
            jax.ShapeDtypeStruct((rows, SPAN), jnp.bfloat16),
            jax.ShapeDtypeStruct((GROUP, 8, rows), jnp.float32),
            jax.ShapeDtypeStruct((rows, SPAN), jnp.bfloat16),
            jax.ShapeDtypeStruct((2 * rows, 2 * HS), jnp.bfloat16),
        ),
        in_specs=[vmem()] * 7,
        out_specs=(vmem(),) * 4,
        compiler_params=params(),
        cost_estimate=pl.CostEstimate(
            flops=8 * rows * rows * HS * GROUP * 2, bytes_accessed=4 * MB,
            transcendentals=2 * rows * rows * GROUP,
        ),
    )(keep_q, came_q, keep_kv, came_kv, prev_a, prev_b, mask)


def attend_back(queries, kv, mask, head_out, logs, keep_grad, came_grad):
    rows = queries.shape[0]
    return pl.pallas_call(
        backward_kernel,
        out_shape=(
            jax.ShapeDtypeStruct((rows, SPAN), jnp.bfloat16),
            jax.ShapeDtypeStruct((rows, 2 * HS), jnp.bfloat16),
            jax.ShapeDtypeStruct((rows, 2 * HS), jnp.float32),
            jax.ShapeDtypeStruct((rows, 2 * HS), jnp.bfloat16),
        ),
        in_specs=[vmem()] * 7,
        out_specs=(vmem(),) * 4,
        scratch_shapes=[pltpu.VMEM((2 * rows, HS), jnp.float32)] * 2
        + [pltpu.VMEM((rows, SPAN), jnp.bfloat16)],
        compiler_params=params(),
        cost_estimate=pl.CostEstimate(
            flops=20 * rows * rows * HS * GROUP * 2, bytes_accessed=5 * MB,
            transcendentals=2 * rows * rows * GROUP,
        ),
    )(queries, kv, mask, head_out, logs, keep_grad, came_grad)


def pick_blocks(array, wanted):
    blocks = array.reshape(-1, BLK, array.shape[1])
    return jnp.where(
        (wanted >= 0)[:, None, None],
        blocks[jnp.maximum(wanted, 0)],
        jnp.zeros((), jnp.bfloat16),
    )


def sources(landing, block_count):
    return (
        jnp.zeros((block_count,), jnp.int32)
        .at[jnp.where(landing >= 0, landing, block_count)]
        .set(jnp.arange(landing.shape[0], dtype=jnp.int32), mode="drop")
    )


def body(activations, qkv_weight, out_weight, grad_out, segments, send_list, recv_list):
    row_count, shard_width = activations.shape
    dp_index = lax.axis_index("dp")
    seq_index = lax.axis_index("seq")
    tensor_index = lax.axis_index("tensor")
    y_index, core = dp_index // 2, dp_index % 2
    x_index, z_lo = tensor_index // 2, tensor_index % 2
    straight = core == z_lo

    block_count = row_count // BLK
    send_slots, recv_slots = send_list[0], recv_list[0]
    in_own, out_own = qkv_weight[:, 0, :], out_weight[0]

    def join_z(own, near, far, axis):
        here = jnp.where(straight, own, near)
        return jnp.where(
            seq_index == 0,
            jnp.concatenate([here, far], axis=axis),
            jnp.concatenate([far, here], axis=axis),
        )

    arrived = route_blocks(pick_blocks(activations, send_slots))
    in_near, in_far, *out_far = fence(
        [
            z_near(in_own),
            z_far(in_own),
            along_y(out_own, 1),
            along_y(out_own, -1),
            along_y(out_own, 2),
        ]
    )

    in_all = lax.all_gather(join_z(in_own, in_near, in_far, 0), "dp", axis=0, tiled=False)
    moved = arrived[sources(recv_slots, block_count)].reshape(row_count, shard_width)
    out_four = jnp.stack([out_own, *out_far])
    near, far, *others = fence(
        [z_near(out_four), z_far(out_four)]
        + [along_x(grad_out, distance) for distance in OFFSETS[1:]]
        + [along_x(moved, distance) for distance in OFFSETS[1:]]
    )
    grad_x = [grad_out, *others[:3]]
    moved_x = [moved, *others[3:]]

    out_mine = join_z(out_four, near, far, 2)
    out_other = over_cores(out_mine)

    offsets = jnp.array(OFFSETS, jnp.int32)
    places = (x_index + offsets) % NX
    give_kv, give_q = proj_product(1 - z_lo, places, moved_x, in_all, jnp.bfloat16)
    keep_kv, keep_q = proj_product(z_lo, places, moved_x, in_all, jnp.float32)
    chunk_order = jnp.array(POSITION, jnp.int32)[(x_index + offsets - y_index) % NY]
    give_grad = heads_product(straight, chunk_order, grad_x, out_mine, out_other, jnp.bfloat16)
    keep_grad = heads_product(~straight, chunk_order, grad_x, out_mine, out_other, jnp.float32)

    prev_a = send(
        give_kv, lambda x, y, zh, zl, c: (x, y, 1, 1 - zl, c) if zh == 0 else None
    )
    prev_b = send(
        low(keep_kv), lambda x, y, zh, zl, c: (x, y, 1, zl, c) if zh == 0 else None
    )
    query_ids = lax.dynamic_slice_in_dim(segments, seq_index * row_count, row_count)
    padded_ids = jnp.concatenate([jnp.full((row_count,), -1, jnp.int32), segments])
    key_ids = lax.dynamic_slice_in_dim(padded_ids, seq_index * row_count, 2 * row_count)
    positions = jnp.arange(2 * row_count)
    mask = (
        (query_ids[None, :] == key_ids[:, None])
        & (positions[:, None] <= positions[None, :row_count] + row_count)
    ).astype(jnp.float32)
    head_out, logs, queries, kv = attend(
        keep_q, over_z_lo(give_q), keep_kv, over_z_lo(give_kv), prev_a, prev_b, mask
    )
    grad_queries, dkv_prev, dkv_own, dkv_low = attend_back(
        queries, kv, mask, head_out, logs, keep_grad, over_z_lo(give_grad)
    )
    grad_queries_x = over_z_lo(grad_queries)
    back = send(
        dkv_prev, lambda x, y, zh, zl, c: (x, y, 0, zl, c) if zh == 1 else None
    )
    back_x = send(
        dkv_prev, lambda x, y, zh, zl, c: (x, y, 0, 1 - zl, c) if zh == 1 else None
    )
    here, up, across, down = back_product(
        z_lo,
        (x_index + jnp.arange(NX)) % NX,
        [grad_queries, dkv_own, back, grad_queries_x, over_z_lo(dkv_low), back_x],
        in_all,
    )

    (heads,) = fence([head_out], [grad_queries_x])
    order = jnp.array(POSITION, jnp.int32)[(jnp.arange(NX) - y_index) % NY]
    parts = mixed_product(~straight, order, heads, over_z_lo(heads), out_mine, out_other)
    attended = lax.psum_scatter(
        parts.reshape(NX * row_count, shard_width),
        "tensor",
        scatter_dimension=0,
        tiled=True,
        axis_index_groups=X_GROUPS,
    )

    half = row_count // 2
    from_below = along_x(across[:half], -1)
    from_above = along_x(across[half:], 1)
    up = jnp.concatenate(
        [(wide(up[:half]) + wide(from_below)).astype(jnp.bfloat16), up[half:]], axis=0
    )
    down = jnp.concatenate(
        [down[:half], (wide(down[half:]) + wide(from_above)).astype(jnp.bfloat16)], axis=0
    )
    grad_moved = (
        wide(here) + wide(along_x(up, -1)) + wide(along_x(down, 1))
    ).astype(jnp.bfloat16)

    returned = route_blocks(pick_blocks(grad_moved, recv_slots))
    grad_in = returned[sources(send_slots, block_count)]
    return (attended, grad_in.reshape(row_count, shard_width))


def solution(mesh):
    placed = (
        P(("dp", "seq"), "tensor"),
        P(("dp", "seq"), "tensor", None),
        P("tensor", None, ("dp", "seq")),
        P(("dp", "seq"), "tensor"),
        P("dp"),
        P(("dp", "seq"), None),
        P(("dp", "seq"), None),
    )
    return jax.shard_map(
        body,
        mesh=mesh,
        in_specs=placed,
        out_specs=(P(("dp", "seq"), "tensor"), P(("dp", "seq"), "tensor")),
        check_vma=False,
    )
```

```python
import math

import jax
import jax.numpy as jnp
from jax import lax
from jax.experimental import pallas as pl
from jax.experimental.pallas import tpu as pltpu
from jax.sharding import PartitionSpec as P

HS = 128
GROUP = 6
BLK = 32
AXES = ("dp", "seq", "tensor")
NX, NY, NZ = 4, 4, 4
X_GROUPS = [[0, 2, 4, 6], [1, 3, 5, 7]]


def place(index):
    dp, seq, tensor = index // 16, index // 8 % 2, index % 8
    return tensor // 2, dp // 2, seq, tensor % 2, dp % 2


def index_of(x, y, z_hi, z_lo, core):
    return (y % NY * 2 + core) * 16 + z_hi * 8 + x % NX * 2 + z_lo


def send(block, target):
    pairs = []
    for source in range(128):
        goal = target(*place(source))
        if goal is not None:
            pairs.append((source, index_of(*goal)))
    return lax.ppermute(block, AXES, pairs)


def along_y(block, distance):
    return send(block, lambda x, y, zh, zl, c: (x, y - distance, zh, zl, c))


def over_cores(block):
    return send(block, lambda x, y, zh, zl, c: (x, y, zh, zl, 1 - c))


def over_z_lo(block):
    return send(block, lambda x, y, zh, zl, c: (x, y, zh, 1 - zl, c))


def z_near(block):
    return send(
        block, lambda x, y, zh, zl, c: (x, y, zh, 1 - zl, 1 - c) if zl != c else None
    )


def z_far(block):
    return send(
        block,
        lambda x, y, zh, zl, c: (x, y, 1 - zh, zl, c)
        if zl == c
        else (x, y, 1 - zh, 1 - zl, 1 - c),
    )


def along_x(block, distance):
    return send(block, lambda x, y, zh, zl, c: (x - distance, y, zh, zl, c))


def route_blocks(buffer):
    return lax.all_to_all(buffer, ("dp", "seq"), split_axis=0, concat_axis=0, tiled=True)


def nothing(*refs):
    pass


def fence(values, after=()):
    return pl.pallas_call(
        nothing,
        out_shape=[jax.ShapeDtypeStruct(v.shape, v.dtype) for v in values],
        in_specs=[anywhere()] * (len(values) + len(after)),
        out_specs=[anywhere()] * len(values),
        input_output_aliases={i: i for i in range(len(values))},
        cost_estimate=pl.CostEstimate(flops=0, bytes_accessed=0, transcendentals=0),
    )(*values, *after)


def dot(a, b, contract=((1,), (0,))):
    return lax.dot_general(a, b, (contract, ((), ())), preferred_element_type=jnp.float32)


NT = ((1,), (1,))
NN = ((1,), (0,))
MB = 1 << 20
OFFSETS = (0, 1, -1, 2)
POSITION = (0, 1, 3, 2)


def vmem():
    return pl.BlockSpec(memory_space=pltpu.VMEM)


def smem():
    return pl.BlockSpec(memory_space=pltpu.SMEM)


def anywhere():
    return pl.BlockSpec(memory_space=pl.ANY)


def params(size=24):
    return pltpu.CompilerParams(vmem_limit_bytes=size * MB)


def start_all(copies):
    for copy in copies:
        copy.start()


def wait_all(copies):
    for copy in copies:
        copy.wait()


def proj_kernel(info, *refs):
    rows, weights, out_kv, out_q = refs[:NX], refs[NX], refs[NX + 1], refs[NX + 2]
    lhs, held, total, lhs_sems, sems = refs[NX + 3 :]
    copies = [
        [
            pltpu.make_async_copy(rows[r], lhs.at[r], lhs_sems.at[r]),
            pltpu.make_async_copy(
                weights.at[2 * info[1 + r] + info[0]], held.at[r], sems.at[r]
            ),
        ]
        for r in range(NX)
    ]
    start_all(copies[0])
    start_all(copies[1])
    for r in range(NX):
        wait_all(copies[r])
        if r + 2 < NX:
            start_all(copies[r + 2])
        term = dot(lhs[r], held[r])
        if r == 0:
            total[...] = term
        elif r < NX - 1:
            total[...] += term
        else:
            term = (total[...] + term).astype(out_q.dtype)
            out_q[...] = term[:, :SPAN]
            out_kv[...] = term[:, SPAN:]


def proj_product(head, places, rows, weights, dtype):
    row_count, depth = rows[0].shape
    width, full = weights.shape[2], NX * depth
    info = jnp.concatenate([head.astype(jnp.int32)[None], places])
    return pl.pallas_call(
        proj_kernel,
        out_shape=(
            jax.ShapeDtypeStruct((row_count, 2 * HS), dtype),
            jax.ShapeDtypeStruct((row_count, SPAN), dtype),
        ),
        in_specs=[smem()] + [anywhere()] * (NX + 1),
        out_specs=(vmem(), vmem()),
        scratch_shapes=[
            pltpu.VMEM((NX, row_count, depth), jnp.bfloat16),
            pltpu.VMEM((NX, depth, width), jnp.bfloat16),
            pltpu.VMEM((row_count, width), jnp.float32),
            pltpu.SemaphoreType.DMA((NX,)),
            pltpu.SemaphoreType.DMA((NX,)),
        ],
        compiler_params=params(56),
        cost_estimate=pl.CostEstimate(
            flops=2 * row_count * width * full,
            bytes_accessed=2 * full * (width + row_count),
            transcendentals=0,
        ),
    )(info, *rows, weights)


def heads_kernel(info, *refs):
    rows, mine, other, out = refs[:NX], refs[NX], refs[NX + 1], refs[NX + 2]
    lhs, held, total, lhs_sems, sems = refs[NX + 3 :]

    def copies_of(weights, r):
        return [
            pltpu.make_async_copy(rows[r], lhs.at[r], lhs_sems.at[r]),
            pltpu.make_async_copy(weights.at[info[1 + r]], held.at[r], sems.at[r]),
        ]

    def begin(r):
        for pick, weights in ((0, mine), (1, other)):

            @pl.when(info[0] == pick)
            def _():
                start_all(copies_of(weights, r))

    begin(0)
    begin(1)
    for r in range(NX):
        wait_all(copies_of(mine, r))
        if r + 2 < NX:
            begin(r + 2)
        term = dot(lhs[r], held[r], NT)
        if r == 0:
            total[...] = term
        elif r < NX - 1:
            total[...] += term
        else:
            out[...] = (total[...] + term).astype(out.dtype)


def heads_product(use_other, order, rows, mine, other, dtype):
    row_count, depth = rows[0].shape
    width, full = mine.shape[1], NX * depth
    info = jnp.concatenate([use_other.astype(jnp.int32)[None], order])
    return pl.pallas_call(
        heads_kernel,
        out_shape=jax.ShapeDtypeStruct((row_count, width), dtype),
        in_specs=[smem()] + [anywhere()] * (NX + 2),
        out_specs=vmem(),
        scratch_shapes=[
            pltpu.VMEM((NX, row_count, depth), jnp.bfloat16),
            pltpu.VMEM((NX, width, depth), jnp.bfloat16),
            pltpu.VMEM((row_count, width), jnp.float32),
            pltpu.SemaphoreType.DMA((NX,)),
            pltpu.SemaphoreType.DMA((NX,)),
        ],
        compiler_params=params(),
        cost_estimate=pl.CostEstimate(
            flops=2 * row_count * width * full,
            bytes_accessed=2 * full * (width + row_count),
            transcendentals=0,
        ),
    )(info, *rows, mine, other)


def mixed_kernel(
    info, own, theirs, mine, other, out, lhs, held, ready, lhs_sems, sems, out_sems
):
    depth = own.shape[1]
    lhs_copies = [
        pltpu.make_async_copy(piece, lhs.at[:, pl.ds(i * depth, depth)], lhs_sems.at[i])
        for i, piece in enumerate((own, theirs))
    ]

    def copies_of(j, pair):
        return [
            pltpu.make_async_copy(
                weights.at[info[1 + j]], held.at[j, pl.ds(side * depth, depth)], sems.at[j, side]
            )
            for side, weights in enumerate(pair)
        ]

    def begin(j):
        for pick, pair in ((0, (mine, other)), (1, (other, mine))):

            @pl.when(info[0] == pick)
            def _():
                start_all(copies_of(j, pair))

    done = [pltpu.make_async_copy(ready.at[j], out.at[j], out_sems.at[j]) for j in range(NX)]
    begin(0)
    start_all(lhs_copies)
    wait_all(lhs_copies)
    begin(1)
    for j in range(NX):
        wait_all(copies_of(j, (mine, other)))
        if j + 2 < NX:
            begin(j + 2)
        ready[j] = dot(lhs[...], held[j]).astype(out.dtype)
        done[j].start()
    wait_all(done)


def mixed_product(use_other, order, own, theirs, mine, other):
    row_count, depth = own.shape
    width = mine.shape[-1]
    info = jnp.concatenate([use_other.astype(jnp.int32)[None], order])
    return pl.pallas_call(
        mixed_kernel,
        out_shape=jax.ShapeDtypeStruct((NX, row_count, width), jnp.bfloat16),
        in_specs=[smem()] + [anywhere()] * 4,
        out_specs=anywhere(),
        scratch_shapes=[
            pltpu.VMEM((row_count, 2 * depth), jnp.bfloat16),
            pltpu.VMEM((NX, 2 * depth, width), jnp.bfloat16),
            pltpu.VMEM((NX, row_count, width), jnp.bfloat16),
            pltpu.SemaphoreType.DMA((2,)),
            pltpu.SemaphoreType.DMA((NX, 2)),
            pltpu.SemaphoreType.DMA((NX,)),
        ],
        compiler_params=params(),
        cost_estimate=pl.CostEstimate(
            flops=4 * row_count * width * depth * NX,
            bytes_accessed=4 * NX * depth * width + 2 * row_count * (2 * depth + NX * width),
            transcendentals=0,
        ),
    )(info, own, theirs, mine, other)


def wide(value):
    return value.astype(jnp.float32)


def low(value):
    return value.astype(jnp.bfloat16)


def own_kernel(info, q, weights, *refs):
    outs, held, sems = refs[:NX], refs[NX], refs[NX + 1]
    copies = [
        pltpu.make_async_copy(
            weights.at[2 * info[1 + j] + info[0], :, pl.ds(0, SPAN)], held.at[j], sems.at[j]
        )
        for j in range(NX)
    ]
    copies[0].start()
    copies[1].start()
    for j in range(NX):
        copies[j].wait()
        if j + 2 < NX:
            copies[j + 2].start()
        outs[j][...] = dot(q[...], held[j], NT)


def rest_kernel(info, *refs):
    parts = refs[:NX]
    kv, kv_back, q_x, kv_x, kv_back_x, weights = refs[NX : NX + 6]
    outs = refs[NX + 6 : 2 * NX + 6]
    lhs, held, ready, sems, out_sems = refs[2 * NX + 6 :]
    full = SPAN + 2 * HS
    copies = [
        [
            pltpu.make_async_copy(
                weights.at[2 * info[1 + j] + 1 - info[0]],
                held.at[j, :, pl.ds(0, full)],
                sems.at[j, 0],
            ),
            pltpu.make_async_copy(
                weights.at[2 * info[1 + j] + info[0], :, pl.ds(SPAN, 2 * HS)],
                held.at[j, :, pl.ds(full, 2 * HS)],
                sems.at[j, 1],
            ),
        ]
        for j in range(NX)
    ]
    done = [pltpu.make_async_copy(ready.at[j], outs[j], out_sems.at[j]) for j in range(NX)]
    order = (2, 1, 3, 0)
    start_all(copies[order[0]])
    start_all(copies[order[1]])
    lhs[:, :SPAN] = q_x[...]
    lhs[:, SPAN:full] = low(wide(kv_x[...]) + wide(kv_back_x[...]))
    lhs[:, full:] = low(kv[...] + wide(kv_back[...]))
    for i, j in enumerate(order):
        wait_all(copies[j])
        if i + 2 < NX:
            start_all(copies[order[i + 2]])
        ready[j] = low(parts[j][...] + dot(lhs[...], held[j], NT))
        done[j].start()
    wait_all(done)


def own_product(info, q, weights):
    row_count, width = q.shape[0], weights.shape[1]
    return pl.pallas_call(
        own_kernel,
        out_shape=[jax.ShapeDtypeStruct((row_count, width), jnp.float32)] * NX,
        in_specs=[smem(), vmem(), anywhere()],
        out_specs=[vmem()] * NX,
        scratch_shapes=[
            pltpu.VMEM((NX, width, SPAN), jnp.bfloat16),
            pltpu.SemaphoreType.DMA((NX,)),
        ],
        compiler_params=params(48),
        cost_estimate=pl.CostEstimate(
            flops=2 * row_count * width * SPAN * NX,
            bytes_accessed=2 * NX * SPAN * width + 4 * row_count * NX * width,
            transcendentals=0,
        ),
    )(info, q, weights)


def rest_product(info, parts, operands, weights):
    row_count, width = parts[0].shape
    full = SPAN + 4 * HS
    return pl.pallas_call(
        rest_kernel,
        out_shape=[jax.ShapeDtypeStruct((row_count, width), jnp.bfloat16)] * NX,
        in_specs=[smem()] + [vmem()] * (NX + 5) + [anywhere()],
        out_specs=[anywhere()] * NX,
        scratch_shapes=[
            pltpu.VMEM((row_count, full), jnp.bfloat16),
            pltpu.VMEM((NX, width, full), jnp.bfloat16),
            pltpu.VMEM((NX, row_count, width), jnp.bfloat16),
            pltpu.SemaphoreType.DMA((NX, 2)),
            pltpu.SemaphoreType.DMA((NX,)),
        ],
        compiler_params=params(48),
        cost_estimate=pl.CostEstimate(
            flops=2 * row_count * width * full * NX,
            bytes_accessed=2 * NX * full * width + 6 * row_count * NX * width,
            transcendentals=0,
        ),
    )(info, *parts, *operands, weights)


SCALING = 1.0 / math.sqrt(HS)
SPAN = GROUP * HS


def forward_kernel(
    keep_q, came_q, keep_kv, came_kv, prev_a, prev_b, mask, head_out, logs, queries, kv
):
    rows = keep_q.shape[0]
    queries[...] = low(keep_q[...] + wide(came_q[...]))
    kv[:rows] = low(wide(prev_a[...]) + wide(prev_b[...]))
    kv[rows:] = low(keep_kv[...] + wide(came_kv[...]))
    keys, turned = kv[:, :HS], kv[:, HS:].T

    @pl.loop(0, GROUP, unroll=GROUP)
    def _(h):
        lanes = pl.ds(pl.multiple_of(h * HS, HS), HS)
        scores = dot(keys, queries[:, lanes], NT) * SCALING
        scores = jnp.where(mask[...] > 0, scores, -1e30)
        highest = jnp.max(scores, axis=0, keepdims=True)
        raised = jnp.exp(scores - highest)
        inverse = 1.0 / jnp.sum(raised, axis=0, keepdims=True)
        logs[h, 0:1] = highest
        logs[h, 1:2] = inverse
        head_out[:, lanes] = low(dot(turned, low(raised * inverse)).T)


def backward_kernel(
    queries, kv, mask, head_out, logs, keep_grad, came_grad,
    dq, dkv_prev, dkv_own, dkv_low, dk, dv, grad_heads,
):
    rows = queries.shape[0]
    grad_heads[...] = low(keep_grad[...] + wide(came_grad[...]))
    keys, values = kv[:, :HS], kv[:, HS:]
    turned = keys.T
    dk[...] = jnp.zeros_like(dk)
    dv[...] = jnp.zeros_like(dv)

    @pl.loop(0, GROUP, unroll=GROUP)
    def _(h):
        lanes = pl.ds(pl.multiple_of(h * HS, HS), HS)
        query, grad = queries[:, lanes], grad_heads[:, lanes]
        scores = dot(keys, query, NT) * SCALING
        scores = jnp.where(mask[...] > 0, scores, -1e30)
        probability = jnp.exp(scores - logs[h, 0:1]) * logs[h, 1:2]
        delta = jnp.sum((wide(grad) * wide(head_out[:, lanes])).T, axis=0, keepdims=True)
        score_grad = low(probability * (dot(values, grad, NT) - delta))
        dv[...] += dot(low(probability), grad)
        dk[...] += dot(score_grad, query)
        dq[:, lanes] = low((dot(turned, score_grad) * SCALING).T)

    dkv_prev[:, :HS] = low(dk[:rows] * SCALING)
    dkv_prev[:, HS:] = low(dv[:rows])
    dkv_own[:, :HS] = dk[rows:] * SCALING
    dkv_own[:, HS:] = dv[rows:]
    dkv_low[...] = low(dkv_own[...])


def attend(keep_q, came_q, keep_kv, came_kv, prev_a, prev_b, mask):
    rows = keep_q.shape[0]
    return pl.pallas_call(
        forward_kernel,
        out_shape=(
            jax.ShapeDtypeStruct((rows, SPAN), jnp.bfloat16),
            jax.ShapeDtypeStruct((GROUP, 8, rows), jnp.float32),
            jax.ShapeDtypeStruct((rows, SPAN), jnp.bfloat16),
            jax.ShapeDtypeStruct((2 * rows, 2 * HS), jnp.bfloat16),
        ),
        in_specs=[vmem()] * 7,
        out_specs=(vmem(),) * 4,
        compiler_params=params(),
        cost_estimate=pl.CostEstimate(
            flops=8 * rows * rows * HS * GROUP * 2, bytes_accessed=4 * MB,
            transcendentals=2 * rows * rows * GROUP,
        ),
    )(keep_q, came_q, keep_kv, came_kv, prev_a, prev_b, mask)


def attend_back(queries, kv, mask, head_out, logs, keep_grad, came_grad):
    rows = queries.shape[0]
    return pl.pallas_call(
        backward_kernel,
        out_shape=(
            jax.ShapeDtypeStruct((rows, SPAN), jnp.bfloat16),
            jax.ShapeDtypeStruct((rows, 2 * HS), jnp.bfloat16),
            jax.ShapeDtypeStruct((rows, 2 * HS), jnp.float32),
            jax.ShapeDtypeStruct((rows, 2 * HS), jnp.bfloat16),
        ),
        in_specs=[vmem()] * 7,
        out_specs=(vmem(),) * 4,
        scratch_shapes=[pltpu.VMEM((2 * rows, HS), jnp.float32)] * 2
        + [pltpu.VMEM((rows, SPAN), jnp.bfloat16)],
        compiler_params=params(),
        cost_estimate=pl.CostEstimate(
            flops=20 * rows * rows * HS * GROUP * 2, bytes_accessed=5 * MB,
            transcendentals=2 * rows * rows * GROUP,
        ),
    )(queries, kv, mask, head_out, logs, keep_grad, came_grad)


def pick_blocks(array, wanted):
    blocks = array.reshape(-1, BLK, array.shape[1])
    return jnp.where(
        (wanted >= 0)[:, None, None],
        blocks[jnp.maximum(wanted, 0)],
        jnp.zeros((), jnp.bfloat16),
    )


def sources(landing, block_count):
    return (
        jnp.zeros((block_count,), jnp.int32)
        .at[jnp.where(landing >= 0, landing, block_count)]
        .set(jnp.arange(landing.shape[0], dtype=jnp.int32), mode="drop")
    )


def body(activations, qkv_weight, out_weight, grad_out, segments, send_list, recv_list):
    row_count, shard_width = activations.shape
    dp_index = lax.axis_index("dp")
    seq_index = lax.axis_index("seq")
    tensor_index = lax.axis_index("tensor")
    y_index, core = dp_index // 2, dp_index % 2
    x_index, z_lo = tensor_index // 2, tensor_index % 2
    straight = core == z_lo

    block_count = row_count // BLK
    send_slots, recv_slots = send_list[0], recv_list[0]
    in_own, out_own = qkv_weight[:, 0, :], out_weight[0]

    def join_z(own, near, far, axis):
        here = jnp.where(straight, own, near)
        return jnp.where(
            seq_index == 0,
            jnp.concatenate([here, far], axis=axis),
            jnp.concatenate([far, here], axis=axis),
        )

    in_near, in_far, out_up, out_down = fence(
        [z_near(in_own), z_far(in_own), along_y(out_own, 1), along_y(out_own, -1)]
    )
    out_two, arrived = fence(
        [along_y(out_own, 2), route_blocks(pick_blocks(activations, send_slots))]
    )
    out_far = [out_up, out_down, out_two]

    in_all = lax.all_gather(join_z(in_own, in_near, in_far, 0), "dp", axis=0, tiled=False)
    moved = arrived[sources(recv_slots, block_count)].reshape(row_count, shard_width)
    out_four = jnp.stack([out_own, *out_far])
    near, far, *others = fence(
        [z_near(out_four), z_far(out_four)]
        + [along_x(grad_out, distance) for distance in OFFSETS[1:]]
        + [along_x(moved, distance) for distance in OFFSETS[1:]]
    )
    grad_x = [grad_out, *others[:3]]
    moved_x = [moved, *others[3:]]

    out_mine = join_z(out_four, near, far, 2)
    out_other = over_cores(out_mine)

    offsets = jnp.array(OFFSETS, jnp.int32)
    places = (x_index + offsets) % NX
    give_kv, give_q = proj_product(1 - z_lo, places, moved_x, in_all, jnp.bfloat16)
    keep_kv, keep_q = proj_product(z_lo, places, moved_x, in_all, jnp.float32)
    chunk_order = jnp.array(POSITION, jnp.int32)[(x_index + offsets - y_index) % NY]
    give_grad = heads_product(straight, chunk_order, grad_x, out_mine, out_other, jnp.bfloat16)
    keep_grad = heads_product(~straight, chunk_order, grad_x, out_mine, out_other, jnp.float32)

    prev_a = send(
        give_kv, lambda x, y, zh, zl, c: (x, y, 1, 1 - zl, c) if zh == 0 else None
    )
    prev_b = send(
        low(keep_kv), lambda x, y, zh, zl, c: (x, y, 1, zl, c) if zh == 0 else None
    )
    query_ids = lax.dynamic_slice_in_dim(segments, seq_index * row_count, row_count)
    padded_ids = jnp.concatenate([jnp.full((row_count,), -1, jnp.int32), segments])
    key_ids = lax.dynamic_slice_in_dim(padded_ids, seq_index * row_count, 2 * row_count)
    positions = jnp.arange(2 * row_count)
    mask = (
        (query_ids[None, :] == key_ids[:, None])
        & (positions[:, None] <= positions[None, :row_count] + row_count)
    ).astype(jnp.float32)
    head_out, logs, queries, kv = attend(
        keep_q, over_z_lo(give_q), keep_kv, over_z_lo(give_kv), prev_a, prev_b, mask
    )
    grad_queries, dkv_prev, dkv_own, dkv_low = attend_back(
        queries, kv, mask, head_out, logs, keep_grad, over_z_lo(give_grad)
    )
    info = jnp.concatenate([z_lo[None], (x_index + jnp.arange(NX)) % NX]).astype(jnp.int32)
    own_parts = own_product(info, grad_queries, in_all)
    grad_queries_x = over_z_lo(grad_queries)
    back = send(
        dkv_prev, lambda x, y, zh, zl, c: (x, y, 0, zl, c) if zh == 1 else None
    )
    back_x = send(
        dkv_prev, lambda x, y, zh, zl, c: (x, y, 0, 1 - zl, c) if zh == 1 else None
    )
    here, up, across, down = rest_product(
        info,
        own_parts,
        [dkv_own, back, grad_queries_x, over_z_lo(dkv_low), back_x],
        in_all,
    )

    (heads,) = fence([head_out], [back_x])
    (heads_x,) = fence([over_z_lo(heads)], [here])
    order = jnp.array(POSITION, jnp.int32)[(jnp.arange(NX) - y_index) % NY]
    parts = mixed_product(~straight, order, heads, heads_x, out_mine, out_other)
    attended = lax.psum_scatter(
        parts.reshape(NX * row_count, shard_width),
        "tensor",
        scatter_dimension=0,
        tiled=True,
        axis_index_groups=X_GROUPS,
    )

    half = row_count // 2
    from_below = along_x(across[:half], -1)
    from_above = along_x(across[half:], 1)
    up = jnp.concatenate(
        [(wide(up[:half]) + wide(from_below)).astype(jnp.bfloat16), up[half:]], axis=0
    )
    down = jnp.concatenate(
        [down[:half], (wide(down[half:]) + wide(from_above)).astype(jnp.bfloat16)], axis=0
    )
    grad_moved = (
        wide(here) + wide(along_x(up, -1)) + wide(along_x(down, 1))
    ).astype(jnp.bfloat16)

    returned = route_blocks(pick_blocks(grad_moved, recv_slots))
    grad_in = returned[sources(send_slots, block_count)]
    return (attended, grad_in.reshape(row_count, shard_width))


def solution(mesh):
    placed = (
        P(("dp", "seq"), "tensor"),
        P(("dp", "seq"), "tensor", None),
        P("tensor", None, ("dp", "seq")),
        P(("dp", "seq"), "tensor"),
        P("dp"),
        P(("dp", "seq"), None),
        P(("dp", "seq"), None),
    )
    return jax.shard_map(
        body,
        mesh=mesh,
        in_specs=placed,
        out_specs=(P(("dp", "seq"), "tensor"), P(("dp", "seq"), "tensor")),
        check_vma=False,
    )
```

```python
import math

import jax
import jax.numpy as jnp
from jax import lax
from jax.experimental import pallas as pl
from jax.experimental.pallas import tpu as pltpu
from jax.sharding import PartitionSpec as P

HS = 128
GROUP = 6
BLK = 32
AXES = ("dp", "seq", "tensor")
NX, NY, NZ = 4, 4, 4
X_GROUPS = [[0, 2, 4, 6], [1, 3, 5, 7]]


def place(index):
    dp, seq, tensor = index // 16, index // 8 % 2, index % 8
    return tensor // 2, dp // 2, seq, tensor % 2, dp % 2


def index_of(x, y, z_hi, z_lo, core):
    return (y % NY * 2 + core) * 16 + z_hi * 8 + x % NX * 2 + z_lo


def send(block, target):
    pairs = []
    for source in range(128):
        goal = target(*place(source))
        if goal is not None:
            pairs.append((source, index_of(*goal)))
    return lax.ppermute(block, AXES, pairs)


def along_y(block, distance):
    return send(block, lambda x, y, zh, zl, c: (x, y - distance, zh, zl, c))


def over_cores(block):
    return send(block, lambda x, y, zh, zl, c: (x, y, zh, zl, 1 - c))


def over_z_lo(block):
    return send(block, lambda x, y, zh, zl, c: (x, y, zh, 1 - zl, c))


def z_near(block):
    return send(
        block, lambda x, y, zh, zl, c: (x, y, zh, 1 - zl, 1 - c) if zl != c else None
    )


def z_far(block):
    return send(
        block,
        lambda x, y, zh, zl, c: (x, y, 1 - zh, zl, c)
        if zl == c
        else (x, y, 1 - zh, 1 - zl, 1 - c),
    )


def along_x(block, distance):
    return send(block, lambda x, y, zh, zl, c: (x - distance, y, zh, zl, c))


def route_blocks(buffer):
    return lax.all_to_all(buffer, ("dp", "seq"), split_axis=0, concat_axis=0, tiled=True)


def nothing(*refs):
    pass


def fence(values, after=()):
    return pl.pallas_call(
        nothing,
        out_shape=[jax.ShapeDtypeStruct(v.shape, v.dtype) for v in values],
        in_specs=[anywhere()] * (len(values) + len(after)),
        out_specs=[anywhere()] * len(values),
        input_output_aliases={i: i for i in range(len(values))},
        cost_estimate=pl.CostEstimate(flops=0, bytes_accessed=0, transcendentals=0),
    )(*values, *after)


def dot(a, b, contract=((1,), (0,))):
    return lax.dot_general(a, b, (contract, ((), ())), preferred_element_type=jnp.float32)


NT = ((1,), (1,))
NN = ((1,), (0,))
MB = 1 << 20
OFFSETS = (0, 1, -1, 2)
POSITION = (0, 1, 3, 2)


def vmem():
    return pl.BlockSpec(memory_space=pltpu.VMEM)


def smem():
    return pl.BlockSpec(memory_space=pltpu.SMEM)


def anywhere():
    return pl.BlockSpec(memory_space=pl.ANY)


def params(size=24):
    return pltpu.CompilerParams(vmem_limit_bytes=size * MB)


def start_all(copies):
    for copy in copies:
        copy.start()


def wait_all(copies):
    for copy in copies:
        copy.wait()


def proj_kernel(info, *refs):
    rows, weights, out_kv, out_q = refs[:NX], refs[NX], refs[NX + 1], refs[NX + 2]
    lhs, held, total, lhs_sems, sems = refs[NX + 3 :]
    copies = [
        [
            pltpu.make_async_copy(rows[r], lhs.at[r], lhs_sems.at[r]),
            pltpu.make_async_copy(
                weights.at[2 * info[1 + r] + info[0]], held.at[r], sems.at[r]
            ),
        ]
        for r in range(NX)
    ]
    start_all(copies[0])
    start_all(copies[1])
    for r in range(NX):
        wait_all(copies[r])
        if r + 2 < NX:
            start_all(copies[r + 2])
        term = dot(lhs[r], held[r])
        if r == 0:
            total[...] = term
        elif r < NX - 1:
            total[...] += term
        else:
            term = (total[...] + term).astype(out_q.dtype)
            out_q[...] = term[:, :SPAN]
            out_kv[...] = term[:, SPAN:]


def proj_product(head, places, rows, weights, dtype):
    row_count, depth = rows[0].shape
    width, full = weights.shape[2], NX * depth
    info = jnp.concatenate([head.astype(jnp.int32)[None], places])
    return pl.pallas_call(
        proj_kernel,
        out_shape=(
            jax.ShapeDtypeStruct((row_count, 2 * HS), dtype),
            jax.ShapeDtypeStruct((row_count, SPAN), dtype),
        ),
        in_specs=[smem()] + [anywhere()] * (NX + 1),
        out_specs=(vmem(), vmem()),
        scratch_shapes=[
            pltpu.VMEM((NX, row_count, depth), jnp.bfloat16),
            pltpu.VMEM((NX, depth, width), jnp.bfloat16),
            pltpu.VMEM((row_count, width), jnp.float32),
            pltpu.SemaphoreType.DMA((NX,)),
            pltpu.SemaphoreType.DMA((NX,)),
        ],
        compiler_params=params(53),
        cost_estimate=pl.CostEstimate(
            flops=2 * row_count * width * full,
            bytes_accessed=2 * full * (width + row_count),
            transcendentals=0,
        ),
    )(info, *rows, weights)


def heads_kernel(info, *refs):
    rows, mine, other, out = refs[:NX], refs[NX], refs[NX + 1], refs[NX + 2]
    lhs, held, total, lhs_sems, sems = refs[NX + 3 :]

    def copies_of(weights, r):
        return [
            pltpu.make_async_copy(rows[r], lhs.at[r], lhs_sems.at[r]),
            pltpu.make_async_copy(weights.at[info[1 + r]], held.at[r], sems.at[r]),
        ]

    def begin(r):
        for pick, weights in ((0, mine), (1, other)):

            @pl.when(info[0] == pick)
            def _():
                start_all(copies_of(weights, r))

    begin(0)
    begin(1)
    for r in range(NX):
        wait_all(copies_of(mine, r))
        if r + 2 < NX:
            begin(r + 2)
        term = dot(lhs[r], held[r], NT)
        if r == 0:
            total[...] = term
        elif r < NX - 1:
            total[...] += term
        else:
            out[...] = (total[...] + term).astype(out.dtype)


def heads_product(use_other, order, rows, mine, other, dtype):
    row_count, depth = rows[0].shape
    width, full = mine.shape[1], NX * depth
    info = jnp.concatenate([use_other.astype(jnp.int32)[None], order])
    return pl.pallas_call(
        heads_kernel,
        out_shape=jax.ShapeDtypeStruct((row_count, width), dtype),
        in_specs=[smem()] + [anywhere()] * (NX + 2),
        out_specs=vmem(),
        scratch_shapes=[
            pltpu.VMEM((NX, row_count, depth), jnp.bfloat16),
            pltpu.VMEM((NX, width, depth), jnp.bfloat16),
            pltpu.VMEM((row_count, width), jnp.float32),
            pltpu.SemaphoreType.DMA((NX,)),
            pltpu.SemaphoreType.DMA((NX,)),
        ],
        compiler_params=params(53),
        cost_estimate=pl.CostEstimate(
            flops=2 * row_count * width * full,
            bytes_accessed=2 * full * (width + row_count),
            transcendentals=0,
        ),
    )(info, *rows, mine, other)


def mixed_kernel(
    info, own, theirs, mine, other, out, lhs, held, ready, lhs_sems, sems, out_sems
):
    depth = own.shape[1]
    lhs_copies = [
        pltpu.make_async_copy(piece, lhs.at[:, pl.ds(i * depth, depth)], lhs_sems.at[i])
        for i, piece in enumerate((own, theirs))
    ]

    def copies_of(j, pair):
        return [
            pltpu.make_async_copy(
                weights.at[info[1 + j]], held.at[j, pl.ds(side * depth, depth)], sems.at[j, side]
            )
            for side, weights in enumerate(pair)
        ]

    def begin(j):
        for pick, pair in ((0, (mine, other)), (1, (other, mine))):

            @pl.when(info[0] == pick)
            def _():
                start_all(copies_of(j, pair))

    done = [pltpu.make_async_copy(ready.at[j], out.at[j], out_sems.at[j]) for j in range(NX)]
    begin(0)
    start_all(lhs_copies)
    wait_all(lhs_copies)
    begin(1)
    for j in range(NX):
        wait_all(copies_of(j, (mine, other)))
        if j + 2 < NX:
            begin(j + 2)
        ready[j] = dot(lhs[...], held[j]).astype(out.dtype)
        done[j].start()
    wait_all(done)


def mixed_product(use_other, order, own, theirs, mine, other):
    row_count, depth = own.shape
    width = mine.shape[-1]
    info = jnp.concatenate([use_other.astype(jnp.int32)[None], order])
    return pl.pallas_call(
        mixed_kernel,
        out_shape=jax.ShapeDtypeStruct((NX, row_count, width), jnp.bfloat16),
        in_specs=[smem()] + [anywhere()] * 4,
        out_specs=anywhere(),
        scratch_shapes=[
            pltpu.VMEM((row_count, 2 * depth), jnp.bfloat16),
            pltpu.VMEM((NX, 2 * depth, width), jnp.bfloat16),
            pltpu.VMEM((NX, row_count, width), jnp.bfloat16),
            pltpu.SemaphoreType.DMA((2,)),
            pltpu.SemaphoreType.DMA((NX, 2)),
            pltpu.SemaphoreType.DMA((NX,)),
        ],
        compiler_params=params(53),
        cost_estimate=pl.CostEstimate(
            flops=4 * row_count * width * depth * NX,
            bytes_accessed=4 * NX * depth * width + 2 * row_count * (2 * depth + NX * width),
            transcendentals=0,
        ),
    )(info, own, theirs, mine, other)


def wide(value):
    return value.astype(jnp.float32)


def low(value):
    return value.astype(jnp.bfloat16)


def own_kernel(info, q, weights, *refs):
    outs, held, sems = refs[:NX], refs[NX], refs[NX + 1]
    copies = [
        pltpu.make_async_copy(
            weights.at[2 * info[1 + j] + info[0], :, pl.ds(0, SPAN)], held.at[j], sems.at[j]
        )
        for j in range(NX)
    ]
    copies[0].start()
    copies[1].start()
    for j in range(NX):
        copies[j].wait()
        if j + 2 < NX:
            copies[j + 2].start()
        outs[j][...] = dot(q[...], held[j], NT)


def rest_kernel(info, *refs):
    parts = refs[:NX]
    kv, kv_back, q_x, kv_x, kv_back_x, weights = refs[NX : NX + 6]
    outs = refs[NX + 6 : 2 * NX + 6]
    lhs, held, ready, sems, out_sems = refs[2 * NX + 6 :]
    full = SPAN + 2 * HS
    copies = [
        [
            pltpu.make_async_copy(
                weights.at[2 * info[1 + j] + 1 - info[0]],
                held.at[j, :, pl.ds(0, full)],
                sems.at[j, 0],
            ),
            pltpu.make_async_copy(
                weights.at[2 * info[1 + j] + info[0], :, pl.ds(SPAN, 2 * HS)],
                held.at[j, :, pl.ds(full, 2 * HS)],
                sems.at[j, 1],
            ),
        ]
        for j in range(NX)
    ]
    done = [pltpu.make_async_copy(ready.at[j], outs[j], out_sems.at[j]) for j in range(NX)]
    order = (2, 1, 3, 0)
    start_all(copies[order[0]])
    start_all(copies[order[1]])
    lhs[:, :SPAN] = q_x[...]
    lhs[:, SPAN:full] = low(wide(kv_x[...]) + wide(kv_back_x[...]))
    lhs[:, full:] = low(kv[...] + wide(kv_back[...]))
    for i, j in enumerate(order):
        wait_all(copies[j])
        if i + 2 < NX:
            start_all(copies[order[i + 2]])
        ready[j] = low(parts[j][...] + dot(lhs[...], held[j], NT))
        done[j].start()
    wait_all(done)


def own_product(info, q, weights):
    row_count, width = q.shape[0], weights.shape[1]
    return pl.pallas_call(
        own_kernel,
        out_shape=[jax.ShapeDtypeStruct((row_count, width), jnp.float32)] * NX,
        in_specs=[smem(), vmem(), anywhere()],
        out_specs=[vmem()] * NX,
        scratch_shapes=[
            pltpu.VMEM((NX, width, SPAN), jnp.bfloat16),
            pltpu.SemaphoreType.DMA((NX,)),
        ],
        compiler_params=params(53),
        cost_estimate=pl.CostEstimate(
            flops=2 * row_count * width * SPAN * NX,
            bytes_accessed=2 * NX * SPAN * width + 4 * row_count * NX * width,
            transcendentals=0,
        ),
    )(info, q, weights)


def rest_product(info, parts, operands, weights):
    row_count, width = parts[0].shape
    full = SPAN + 4 * HS
    return pl.pallas_call(
        rest_kernel,
        out_shape=[jax.ShapeDtypeStruct((row_count, width), jnp.bfloat16)] * NX,
        in_specs=[smem()] + [vmem()] * (NX + 5) + [anywhere()],
        out_specs=[anywhere()] * NX,
        scratch_shapes=[
            pltpu.VMEM((row_count, full), jnp.bfloat16),
            pltpu.VMEM((NX, width, full), jnp.bfloat16),
            pltpu.VMEM((NX, row_count, width), jnp.bfloat16),
            pltpu.SemaphoreType.DMA((NX, 2)),
            pltpu.SemaphoreType.DMA((NX,)),
        ],
        compiler_params=params(53),
        cost_estimate=pl.CostEstimate(
            flops=2 * row_count * width * full * NX,
            bytes_accessed=2 * NX * full * width + 6 * row_count * NX * width,
            transcendentals=0,
        ),
    )(info, *parts, *operands, weights)


SCALING = 1.0 / math.sqrt(HS)
SPAN = GROUP * HS


def forward_kernel(
    keep_q, came_q, keep_kv, came_kv, prev_a, prev_b, mask, head_out, logs, queries, kv
):
    rows = keep_q.shape[0]
    queries[...] = low(keep_q[...] + wide(came_q[...]))
    kv[:rows] = low(wide(prev_a[...]) + wide(prev_b[...]))
    kv[rows:] = low(keep_kv[...] + wide(came_kv[...]))
    keys, turned = kv[:, :HS], kv[:, HS:].T

    @pl.loop(0, GROUP, unroll=GROUP)
    def _(h):
        lanes = pl.ds(pl.multiple_of(h * HS, HS), HS)
        scores = dot(keys, queries[:, lanes], NT) * SCALING
        scores = jnp.where(mask[...] > 0, scores, -1e30)
        highest = jnp.max(scores, axis=0, keepdims=True)
        raised = jnp.exp(scores - highest)
        inverse = 1.0 / jnp.sum(raised, axis=0, keepdims=True)
        logs[h, 0:1] = highest
        logs[h, 1:2] = inverse
        head_out[:, lanes] = low(dot(turned, low(raised * inverse)).T)


def backward_kernel(
    queries, kv, mask, head_out, logs, keep_grad, came_grad,
    dq, dkv_prev, dkv_own, dkv_low, dk, dv, grad_heads,
):
    rows = queries.shape[0]
    grad_heads[...] = low(keep_grad[...] + wide(came_grad[...]))
    keys, values = kv[:, :HS], kv[:, HS:]
    turned = keys.T
    dk[...] = jnp.zeros_like(dk)
    dv[...] = jnp.zeros_like(dv)

    @pl.loop(0, GROUP, unroll=GROUP)
    def _(h):
        lanes = pl.ds(pl.multiple_of(h * HS, HS), HS)
        query, grad = queries[:, lanes], grad_heads[:, lanes]
        scores = dot(keys, query, NT) * SCALING
        scores = jnp.where(mask[...] > 0, scores, -1e30)
        probability = jnp.exp(scores - logs[h, 0:1]) * logs[h, 1:2]
        delta = jnp.sum((wide(grad) * wide(head_out[:, lanes])).T, axis=0, keepdims=True)
        score_grad = low(probability * (dot(values, grad, NT) - delta))
        dv[...] += dot(low(probability), grad)
        dk[...] += dot(score_grad, query)
        dq[:, lanes] = low((dot(turned, score_grad) * SCALING).T)

    dkv_prev[:, :HS] = low(dk[:rows] * SCALING)
    dkv_prev[:, HS:] = low(dv[:rows])
    dkv_own[:, :HS] = dk[rows:] * SCALING
    dkv_own[:, HS:] = dv[rows:]
    dkv_low[...] = low(dkv_own[...])


def attend(keep_q, came_q, keep_kv, came_kv, prev_a, prev_b, mask):
    rows = keep_q.shape[0]
    return pl.pallas_call(
        forward_kernel,
        out_shape=(
            jax.ShapeDtypeStruct((rows, SPAN), jnp.bfloat16),
            jax.ShapeDtypeStruct((GROUP, 8, rows), jnp.float32),
            jax.ShapeDtypeStruct((rows, SPAN), jnp.bfloat16),
            jax.ShapeDtypeStruct((2 * rows, 2 * HS), jnp.bfloat16),
        ),
        in_specs=[vmem()] * 7,
        out_specs=(vmem(),) * 4,
        compiler_params=params(),
        cost_estimate=pl.CostEstimate(
            flops=8 * rows * rows * HS * GROUP * 2, bytes_accessed=4 * MB,
            transcendentals=2 * rows * rows * GROUP,
        ),
    )(keep_q, came_q, keep_kv, came_kv, prev_a, prev_b, mask)


def attend_back(queries, kv, mask, head_out, logs, keep_grad, came_grad):
    rows = queries.shape[0]
    return pl.pallas_call(
        backward_kernel,
        out_shape=(
            jax.ShapeDtypeStruct((rows, SPAN), jnp.bfloat16),
            jax.ShapeDtypeStruct((rows, 2 * HS), jnp.bfloat16),
            jax.ShapeDtypeStruct((rows, 2 * HS), jnp.float32),
            jax.ShapeDtypeStruct((rows, 2 * HS), jnp.bfloat16),
        ),
        in_specs=[vmem()] * 7,
        out_specs=(vmem(),) * 4,
        scratch_shapes=[pltpu.VMEM((2 * rows, HS), jnp.float32)] * 2
        + [pltpu.VMEM((rows, SPAN), jnp.bfloat16)],
        compiler_params=params(),
        cost_estimate=pl.CostEstimate(
            flops=20 * rows * rows * HS * GROUP * 2, bytes_accessed=5 * MB,
            transcendentals=2 * rows * rows * GROUP,
        ),
    )(queries, kv, mask, head_out, logs, keep_grad, came_grad)


def pick_blocks(array, wanted):
    blocks = array.reshape(-1, BLK, array.shape[1])
    return jnp.where(
        (wanted >= 0)[:, None, None],
        blocks[jnp.maximum(wanted, 0)],
        jnp.zeros((), jnp.bfloat16),
    )


def sources(landing, block_count):
    return (
        jnp.zeros((block_count,), jnp.int32)
        .at[jnp.where(landing >= 0, landing, block_count)]
        .set(jnp.arange(landing.shape[0], dtype=jnp.int32), mode="drop")
    )


def body(activations, qkv_weight, out_weight, grad_out, segments, send_list, recv_list):
    row_count, shard_width = activations.shape
    dp_index = lax.axis_index("dp")
    seq_index = lax.axis_index("seq")
    tensor_index = lax.axis_index("tensor")
    y_index, core = dp_index // 2, dp_index % 2
    x_index, z_lo = tensor_index // 2, tensor_index % 2
    straight = core == z_lo

    block_count = row_count // BLK
    send_slots, recv_slots = send_list[0], recv_list[0]
    in_own, out_own = qkv_weight[:, 0, :], out_weight[0]

    def join_z(own, near, far, axis):
        here = jnp.where(straight, own, near)
        return jnp.where(
            seq_index == 0,
            jnp.concatenate([here, far], axis=axis),
            jnp.concatenate([far, here], axis=axis),
        )

    in_near, in_far, *out_far = fence(
        [z_near(in_own), z_far(in_own)]
        + [along_y(out_own, distance) for distance in OFFSETS[1:]]
        + [route_blocks(pick_blocks(activations, send_slots))]
    )
    *out_far, arrived = out_far

    in_all = lax.all_gather(join_z(in_own, in_near, in_far, 0), "dp", axis=0, tiled=False)
    moved = arrived[sources(recv_slots, block_count)].reshape(row_count, shard_width)
    out_four = jnp.stack([out_own, *out_far])
    near, far, *others = fence(
        [z_near(out_four), z_far(out_four)]
        + [along_x(grad_out, distance) for distance in OFFSETS[1:]]
        + [along_x(moved, distance) for distance in OFFSETS[1:]]
    )
    grad_x = [grad_out, *others[:3]]
    moved_x = [moved, *others[3:]]

    out_mine = join_z(out_four, near, far, 2)
    out_other = over_cores(out_mine)

    offsets = jnp.array(OFFSETS, jnp.int32)
    places = (x_index + offsets) % NX
    chunk_order = jnp.array(POSITION, jnp.int32)[(x_index + offsets - y_index) % NY]
    give_grad = heads_product(straight, chunk_order, grad_x, out_mine, out_other, jnp.bfloat16)
    (places,) = fence([places], [give_grad])
    give_kv, give_q = proj_product(1 - z_lo, places, moved_x, in_all, jnp.bfloat16)
    keep_kv, keep_q = proj_product(z_lo, places, moved_x, in_all, jnp.float32)
    keep_grad = heads_product(~straight, chunk_order, grad_x, out_mine, out_other, jnp.float32)

    prev_a = send(
        give_kv, lambda x, y, zh, zl, c: (x, y, 1, 1 - zl, c) if zh == 0 else None
    )
    prev_b = send(
        low(keep_kv), lambda x, y, zh, zl, c: (x, y, 1, zl, c) if zh == 0 else None
    )
    query_ids = lax.dynamic_slice_in_dim(segments, seq_index * row_count, row_count)
    padded_ids = jnp.concatenate([jnp.full((row_count,), -1, jnp.int32), segments])
    key_ids = lax.dynamic_slice_in_dim(padded_ids, seq_index * row_count, 2 * row_count)
    positions = jnp.arange(2 * row_count)
    mask = (
        (query_ids[None, :] == key_ids[:, None])
        & (positions[:, None] <= positions[None, :row_count] + row_count)
    ).astype(jnp.float32)
    head_out, logs, queries, kv = attend(
        keep_q, over_z_lo(give_q), keep_kv, over_z_lo(give_kv), prev_a, prev_b, mask
    )
    grad_queries, dkv_prev, dkv_own, dkv_low = attend_back(
        queries, kv, mask, head_out, logs, keep_grad, over_z_lo(give_grad)
    )
    info = jnp.concatenate([z_lo[None], (x_index + jnp.arange(NX)) % NX]).astype(jnp.int32)
    own_parts = own_product(info, grad_queries, in_all)
    grad_queries_x = over_z_lo(grad_queries)
    back = send(
        dkv_prev, lambda x, y, zh, zl, c: (x, y, 0, zl, c) if zh == 1 else None
    )
    back_x = send(
        dkv_prev, lambda x, y, zh, zl, c: (x, y, 0, 1 - zl, c) if zh == 1 else None
    )
    here, up, across, down = rest_product(
        info,
        own_parts,
        [dkv_own, back, grad_queries_x, over_z_lo(dkv_low), back_x],
        in_all,
    )

    half = row_count // 2
    from_below = along_x(across[:half], -1)
    from_above = along_x(across[half:], 1)

    up = jnp.concatenate(
        [(wide(up[:half]) + wide(from_below)).astype(jnp.bfloat16), up[half:]], axis=0
    )
    down = jnp.concatenate(
        [down[:half], (wide(down[half:]) + wide(from_above)).astype(jnp.bfloat16)], axis=0
    )
    up, down = along_x(up, -1), along_x(down, 1)
    grad_moved = (wide(here) + wide(up) + wide(down)).astype(jnp.bfloat16)

    (heads,) = fence([head_out], [grad_queries_x])
    order = jnp.array(POSITION, jnp.int32)[(jnp.arange(NX) - y_index) % NY]
    parts = mixed_product(~straight, order, heads, over_z_lo(heads), out_mine, out_other)
    (parts,) = fence([parts], [up, down])
    attended = lax.psum_scatter(
        parts.reshape(NX * row_count, shard_width),
        "tensor",
        scatter_dimension=0,
        tiled=True,
        axis_index_groups=X_GROUPS,
    )

    returned = route_blocks(pick_blocks(grad_moved, recv_slots))
    grad_in = returned[sources(send_slots, block_count)]
    return (attended, grad_in.reshape(row_count, shard_width))


def solution(mesh):
    placed = (
        P(("dp", "seq"), "tensor"),
        P(("dp", "seq"), "tensor", None),
        P("tensor", None, ("dp", "seq")),
        P(("dp", "seq"), "tensor"),
        P("dp"),
        P(("dp", "seq"), None),
        P(("dp", "seq"), None),
    )
    return jax.shard_map(
        body,
        mesh=mesh,
        in_specs=placed,
        out_specs=(P(("dp", "seq"), "tensor"), P(("dp", "seq"), "tensor")),
        check_vma=False,
    )
```

```python
import math

import jax
import jax.numpy as jnp
from jax import lax
from jax.experimental import pallas as pl
from jax.experimental.pallas import tpu as pltpu
from jax.sharding import PartitionSpec as P

HS = 128
GROUP = 6
BLK = 32
AXES = ("dp", "seq", "tensor")
NX, NY, NZ = 4, 4, 4
X_GROUPS = [[0, 2, 4, 6], [1, 3, 5, 7]]


def place(index):
    dp, seq, tensor = index // 16, index // 8 % 2, index % 8
    return tensor // 2, dp // 2, seq, tensor % 2, dp % 2


def index_of(x, y, z_hi, z_lo, core):
    return (y % NY * 2 + core) * 16 + z_hi * 8 + x % NX * 2 + z_lo


def send(block, target):
    pairs = []
    for source in range(128):
        goal = target(*place(source))
        if goal is not None:
            pairs.append((source, index_of(*goal)))
    return lax.ppermute(block, AXES, pairs)


def along_y(block, distance):
    return send(block, lambda x, y, zh, zl, c: (x, y - distance, zh, zl, c))


def over_cores(block):
    return send(block, lambda x, y, zh, zl, c: (x, y, zh, zl, 1 - c))


def over_z_lo(block):
    return send(block, lambda x, y, zh, zl, c: (x, y, zh, 1 - zl, c))


def z_near(block):
    return send(
        block, lambda x, y, zh, zl, c: (x, y, zh, 1 - zl, 1 - c) if zl != c else None
    )


def z_far(block):
    return send(
        block,
        lambda x, y, zh, zl, c: (x, y, 1 - zh, zl, c)
        if zl == c
        else (x, y, 1 - zh, 1 - zl, 1 - c),
    )


def along_x(block, distance):
    return send(block, lambda x, y, zh, zl, c: (x - distance, y, zh, zl, c))


def route_blocks(buffer):
    return lax.all_to_all(buffer, ("dp", "seq"), split_axis=0, concat_axis=0, tiled=True)


def nothing(*refs):
    pass


def fence(values, after=()):
    return pl.pallas_call(
        nothing,
        out_shape=[jax.ShapeDtypeStruct(v.shape, v.dtype) for v in values],
        in_specs=[anywhere()] * (len(values) + len(after)),
        out_specs=[anywhere()] * len(values),
        input_output_aliases={i: i for i in range(len(values))},
        cost_estimate=pl.CostEstimate(flops=0, bytes_accessed=0, transcendentals=0),
    )(*values, *after)


def dot(a, b, contract=((1,), (0,))):
    return lax.dot_general(a, b, (contract, ((), ())), preferred_element_type=jnp.float32)


NT = ((1,), (1,))
NN = ((1,), (0,))
MB = 1 << 20
OFFSETS = (0, 1, -1, 2)
POSITION = (0, 1, 3, 2)


def vmem():
    return pl.BlockSpec(memory_space=pltpu.VMEM)


def smem():
    return pl.BlockSpec(memory_space=pltpu.SMEM)


def anywhere():
    return pl.BlockSpec(memory_space=pl.ANY)


def params(size=24):
    return pltpu.CompilerParams(vmem_limit_bytes=size * MB)


def start_all(copies):
    for copy in copies:
        copy.start()


def wait_all(copies):
    for copy in copies:
        copy.wait()


def proj_kernel(info, *refs):
    rows, weights, out_kv, out_q = refs[:NX], refs[NX], refs[NX + 1], refs[NX + 2]
    lhs, held, total, lhs_sems, sems = refs[NX + 3 :]
    copies = [
        [
            pltpu.make_async_copy(rows[r], lhs.at[r], lhs_sems.at[r]),
            pltpu.make_async_copy(
                weights.at[2 * info[1 + r] + info[0]], held.at[r], sems.at[r]
            ),
        ]
        for r in range(NX)
    ]
    start_all(copies[0])
    start_all(copies[1])
    for r in range(NX):
        wait_all(copies[r])
        if r + 2 < NX:
            start_all(copies[r + 2])
        term = dot(lhs[r], held[r])
        if r == 0:
            total[...] = term
        elif r < NX - 1:
            total[...] += term
        else:
            term = (total[...] + term).astype(out_q.dtype)
            out_q[...] = term[:, :SPAN]
            out_kv[...] = term[:, SPAN:]


def proj_product(head, places, rows, weights, dtype):
    row_count, depth = rows[0].shape
    width, full = weights.shape[2], NX * depth
    info = jnp.concatenate([head.astype(jnp.int32)[None], places])
    return pl.pallas_call(
        proj_kernel,
        out_shape=(
            jax.ShapeDtypeStruct((row_count, 2 * HS), dtype),
            jax.ShapeDtypeStruct((row_count, SPAN), dtype),
        ),
        in_specs=[smem()] + [anywhere()] * (NX + 1),
        out_specs=(vmem(), vmem()),
        scratch_shapes=[
            pltpu.VMEM((NX, row_count, depth), jnp.bfloat16),
            pltpu.VMEM((NX, depth, width), jnp.bfloat16),
            pltpu.VMEM((row_count, width), jnp.float32),
            pltpu.SemaphoreType.DMA((NX,)),
            pltpu.SemaphoreType.DMA((NX,)),
        ],
        compiler_params=params(53),
        cost_estimate=pl.CostEstimate(
            flops=2 * row_count * width * full,
            bytes_accessed=2 * full * (width + row_count),
            transcendentals=0,
        ),
    )(info, *rows, weights)


def chunk_copies(here, far, z_hi, index, held, at, rows, sems):
    half = here.shape[2]
    return [
        pltpu.make_async_copy(
            piece.at[index],
            held.at[at, rows, pl.ds(pl.multiple_of(z * half, half), half)],
            sems.at[i],
        )
        for i, (piece, z) in enumerate(((here, z_hi), (far, 1 - z_hi)))
    ]


def heads_kernel(
    info, rows, here, far, here_x, far_x, out, lhs, held, total, lhs_sems, sems
):
    def copies_of(pair, r):
        every = pl.ds(0, held.shape[1])
        return [pltpu.make_async_copy(rows.at[r], lhs.at[r], lhs_sems.at[r])] + chunk_copies(
            *pair, info[1], info[2 + r], held, r, every, sems.at[r]
        )

    def begin(r):
        for pick, pair in ((0, (here, far)), (1, (here_x, far_x))):

            @pl.when(info[0] == pick)
            def _():
                start_all(copies_of(pair, r))

    begin(0)
    begin(1)
    for r in range(NX):
        wait_all(copies_of((here, far), r))
        if r + 2 < NX:
            begin(r + 2)
        term = dot(lhs[r], held[r], NT)
        if r == 0:
            total[...] = term
        elif r < NX - 1:
            total[...] += term
        else:
            out[...] = (total[...] + term).astype(out.dtype)


def heads_product(info, rows, weights, dtype):
    row_count, depth = rows.shape[1:]
    width, full = weights[0].shape[1], NX * depth
    return pl.pallas_call(
        heads_kernel,
        out_shape=jax.ShapeDtypeStruct((row_count, width), dtype),
        in_specs=[smem()] + [anywhere()] * 5,
        out_specs=vmem(),
        scratch_shapes=[
            pltpu.VMEM((NX, row_count, depth), jnp.bfloat16),
            pltpu.VMEM((NX, width, depth), jnp.bfloat16),
            pltpu.VMEM((row_count, width), jnp.float32),
            pltpu.SemaphoreType.DMA((NX,)),
            pltpu.SemaphoreType.DMA((NX, 2)),
        ],
        compiler_params=params(53),
        cost_estimate=pl.CostEstimate(
            flops=2 * row_count * width * full,
            bytes_accessed=2 * full * (width + row_count),
            transcendentals=0,
        ),
    )(info, rows, *weights)


def mixed_kernel(
    info, own, theirs, here, far, here_x, far_x, out, lhs, held, ready, lhs_sems, sems, out_sems
):
    depth = own.shape[1]
    lhs_copies = [
        pltpu.make_async_copy(piece, lhs.at[:, pl.ds(i * depth, depth)], lhs_sems.at[i])
        for i, piece in enumerate((own, theirs))
    ]
    mine, other = (here, far), (here_x, far_x)

    def copies_of(j, pairs):
        return [
            copy
            for side, pair in enumerate(pairs)
            for copy in chunk_copies(
                *pair, info[1], info[2 + j], held, j, pl.ds(side * depth, depth), sems.at[j, side]
            )
        ]

    def begin(j):
        for pick, pairs in ((0, (mine, other)), (1, (other, mine))):

            @pl.when(info[0] == pick)
            def _():
                start_all(copies_of(j, pairs))

    done = [pltpu.make_async_copy(ready.at[j], out.at[j], out_sems.at[j]) for j in range(NX)]
    begin(0)
    start_all(lhs_copies)
    wait_all(lhs_copies)
    begin(1)
    for j in range(NX):
        wait_all(copies_of(j, (mine, other)))
        if j + 2 < NX:
            begin(j + 2)
        ready[j] = dot(lhs[...], held[j]).astype(out.dtype)
        done[j].start()
    wait_all(done)


def mixed_product(info, own, theirs, weights):
    row_count, depth = own.shape
    width = 2 * weights[0].shape[2]
    return pl.pallas_call(
        mixed_kernel,
        out_shape=jax.ShapeDtypeStruct((NX, row_count, width), jnp.bfloat16),
        in_specs=[smem()] + [anywhere()] * 6,
        out_specs=anywhere(),
        scratch_shapes=[
            pltpu.VMEM((row_count, 2 * depth), jnp.bfloat16),
            pltpu.VMEM((NX, 2 * depth, width), jnp.bfloat16),
            pltpu.VMEM((NX, row_count, width), jnp.bfloat16),
            pltpu.SemaphoreType.DMA((2,)),
            pltpu.SemaphoreType.DMA((NX, 2, 2)),
            pltpu.SemaphoreType.DMA((NX,)),
        ],
        compiler_params=params(53),
        cost_estimate=pl.CostEstimate(
            flops=4 * row_count * width * depth * NX,
            bytes_accessed=4 * NX * depth * width + 2 * row_count * (2 * depth + NX * width),
            transcendentals=0,
        ),
    )(info, own, theirs, *weights)


def wide(value):
    return value.astype(jnp.float32)


def low(value):
    return value.astype(jnp.bfloat16)


def query_kernel(count, info, q, weights, *refs):
    parts, outs = refs[:count], refs[count : count + NX]
    held, sems = refs[-2:]
    copies = [
        pltpu.make_async_copy(
            weights.at[2 * info[1 + j] + info[0], :, pl.ds(0, SPAN)], held.at[j], sems.at[j]
        )
        for j in range(NX)
    ]
    copies[0].start()
    copies[1].start()
    for j in range(NX):
        copies[j].wait()
        if j + 2 < NX:
            copies[j + 2].start()
        product = dot(q[...], held[j], NT)
        outs[j][...] = product + parts[j][...] if count else product


def query_product(head, places, q, weights, parts=()):
    row_count, width = q.shape[0], weights.shape[1]
    info = jnp.concatenate([head[None], places]).astype(jnp.int32)
    return pl.pallas_call(
        lambda *refs: query_kernel(len(parts), *refs),
        out_shape=[jax.ShapeDtypeStruct((row_count, width), jnp.float32)] * NX,
        in_specs=[smem(), vmem(), anywhere()] + [vmem()] * len(parts),
        out_specs=[vmem()] * NX,
        scratch_shapes=[
            pltpu.VMEM((NX, width, SPAN), jnp.bfloat16),
            pltpu.SemaphoreType.DMA((NX,)),
        ],
        compiler_params=params(48),
        cost_estimate=pl.CostEstimate(
            flops=2 * row_count * width * SPAN * NX,
            bytes_accessed=2 * NX * SPAN * width + 4 * row_count * NX * width,
            transcendentals=0,
        ),
    )(info, q, weights, *parts)


def rest_kernel(info, *refs):
    parts = refs[:NX]
    kv, kv_back, kv_x, kv_back_x, weights = refs[NX : NX + 5]
    outs = refs[NX + 5 : 2 * NX + 5]
    lhs, held, ready, sems, out_sems = refs[2 * NX + 5 :]
    copies = [
        [
            pltpu.make_async_copy(
                weights.at[2 * info[1 + j] + (info[0] + side) % 2, :, pl.ds(SPAN, 2 * HS)],
                held.at[j, :, pl.ds(side * 2 * HS, 2 * HS)],
                sems.at[j, side],
            )
            for side in range(2)
        ]
        for j in range(NX)
    ]
    done = [pltpu.make_async_copy(ready.at[j], outs[j], out_sems.at[j]) for j in range(NX)]
    order = (2, 1, 3, 0)
    start_all(copies[order[0]])
    start_all(copies[order[1]])
    lhs[:, : 2 * HS] = low(kv[...] + wide(kv_back[...]))
    lhs[:, 2 * HS :] = low(wide(kv_x[...]) + wide(kv_back_x[...]))
    for i, j in enumerate(order):
        wait_all(copies[j])
        if i + 2 < NX:
            start_all(copies[order[i + 2]])
        ready[j] = low(parts[j][...] + dot(lhs[...], held[j], NT))
        done[j].start()
    wait_all(done)


def rest_product(head, places, parts, operands, weights):
    row_count, width = parts[0].shape
    info = jnp.concatenate([head[None], places]).astype(jnp.int32)
    return pl.pallas_call(
        rest_kernel,
        out_shape=[jax.ShapeDtypeStruct((row_count, width), jnp.bfloat16)] * NX,
        in_specs=[smem()] + [vmem()] * (NX + 4) + [anywhere()],
        out_specs=[anywhere()] * NX,
        scratch_shapes=[
            pltpu.VMEM((row_count, 4 * HS), jnp.bfloat16),
            pltpu.VMEM((NX, width, 4 * HS), jnp.bfloat16),
            pltpu.VMEM((NX, row_count, width), jnp.bfloat16),
            pltpu.SemaphoreType.DMA((NX, 2)),
            pltpu.SemaphoreType.DMA((NX,)),
        ],
        compiler_params=params(48),
        cost_estimate=pl.CostEstimate(
            flops=8 * row_count * width * HS * NX,
            bytes_accessed=8 * NX * HS * width + 6 * row_count * NX * width,
            transcendentals=0,
        ),
    )(info, *parts, *operands, weights)


SCALING = 1.0 / math.sqrt(HS)
SPAN = GROUP * HS


def forward_kernel(
    keep_q, came_q, keep_kv, came_kv, prev_a, prev_b, mask, head_out, logs, queries, kv
):
    rows = keep_q.shape[0]
    queries[...] = low(keep_q[...] + wide(came_q[...]))
    kv[:rows] = low(wide(prev_a[...]) + wide(prev_b[...]))
    kv[rows:] = low(keep_kv[...] + wide(came_kv[...]))
    keys, turned = kv[:, :HS], kv[:, HS:].T

    @pl.loop(0, GROUP, unroll=GROUP)
    def _(h):
        lanes = pl.ds(pl.multiple_of(h * HS, HS), HS)
        scores = dot(keys, queries[:, lanes], NT) * SCALING
        scores = jnp.where(mask[...] > 0, scores, -1e30)
        highest = jnp.max(scores, axis=0, keepdims=True)
        raised = jnp.exp(scores - highest)
        inverse = 1.0 / jnp.sum(raised, axis=0, keepdims=True)
        logs[h, 0:1] = highest
        logs[h, 1:2] = inverse
        head_out[:, lanes] = low(dot(turned, low(raised * inverse)).T)


def backward_kernel(
    queries, kv, mask, head_out, logs, keep_grad, came_grad,
    dq, dkv_prev, dkv_own, dkv_low, dk, dv, grad_heads,
):
    rows = queries.shape[0]
    grad_heads[...] = low(keep_grad[...] + wide(came_grad[...]))
    keys, values = kv[:, :HS], kv[:, HS:]
    turned = keys.T
    dk[...] = jnp.zeros_like(dk)
    dv[...] = jnp.zeros_like(dv)

    @pl.loop(0, GROUP, unroll=GROUP)
    def _(h):
        lanes = pl.ds(pl.multiple_of(h * HS, HS), HS)
        query, grad = queries[:, lanes], grad_heads[:, lanes]
        scores = dot(keys, query, NT) * SCALING
        scores = jnp.where(mask[...] > 0, scores, -1e30)
        probability = jnp.exp(scores - logs[h, 0:1]) * logs[h, 1:2]
        delta = jnp.sum((wide(grad) * wide(head_out[:, lanes])).T, axis=0, keepdims=True)
        score_grad = low(probability * (dot(values, grad, NT) - delta))
        dv[...] += dot(low(probability), grad)
        dk[...] += dot(score_grad, query)
        dq[:, lanes] = low((dot(turned, score_grad) * SCALING).T)

    dkv_prev[:, :HS] = low(dk[:rows] * SCALING)
    dkv_prev[:, HS:] = low(dv[:rows])
    dkv_own[:, :HS] = dk[rows:] * SCALING
    dkv_own[:, HS:] = dv[rows:]
    dkv_low[...] = low(dkv_own[...])


def attend(keep_q, came_q, keep_kv, came_kv, prev_a, prev_b, mask):
    rows = keep_q.shape[0]
    return pl.pallas_call(
        forward_kernel,
        out_shape=(
            jax.ShapeDtypeStruct((rows, SPAN), jnp.bfloat16),
            jax.ShapeDtypeStruct((GROUP, 8, rows), jnp.float32),
            jax.ShapeDtypeStruct((rows, SPAN), jnp.bfloat16),
            jax.ShapeDtypeStruct((2 * rows, 2 * HS), jnp.bfloat16),
        ),
        in_specs=[vmem()] * 7,
        out_specs=(vmem(),) * 4,
        compiler_params=params(),
        cost_estimate=pl.CostEstimate(
            flops=8 * rows * rows * HS * GROUP * 2, bytes_accessed=4 * MB,
            transcendentals=2 * rows * rows * GROUP,
        ),
    )(keep_q, came_q, keep_kv, came_kv, prev_a, prev_b, mask)


def attend_back(queries, kv, mask, head_out, logs, keep_grad, came_grad):
    rows = queries.shape[0]
    return pl.pallas_call(
        backward_kernel,
        out_shape=(
            jax.ShapeDtypeStruct((rows, SPAN), jnp.bfloat16),
            jax.ShapeDtypeStruct((rows, 2 * HS), jnp.bfloat16),
            jax.ShapeDtypeStruct((rows, 2 * HS), jnp.float32),
            jax.ShapeDtypeStruct((rows, 2 * HS), jnp.bfloat16),
        ),
        in_specs=[vmem()] * 7,
        out_specs=(vmem(),) * 4,
        scratch_shapes=[pltpu.VMEM((2 * rows, HS), jnp.float32)] * 2
        + [pltpu.VMEM((rows, SPAN), jnp.bfloat16)],
        compiler_params=params(),
        cost_estimate=pl.CostEstimate(
            flops=20 * rows * rows * HS * GROUP * 2, bytes_accessed=5 * MB,
            transcendentals=2 * rows * rows * GROUP,
        ),
    )(queries, kv, mask, head_out, logs, keep_grad, came_grad)


def pick_blocks(array, wanted):
    blocks = array.reshape(-1, BLK, array.shape[1])
    return jnp.where(
        (wanted >= 0)[:, None, None],
        blocks[jnp.maximum(wanted, 0)],
        jnp.zeros((), jnp.bfloat16),
    )


def sources(landing, block_count):
    return (
        jnp.zeros((block_count,), jnp.int32)
        .at[jnp.where(landing >= 0, landing, block_count)]
        .set(jnp.arange(landing.shape[0], dtype=jnp.int32), mode="drop")
    )


def body(activations, qkv_weight, out_weight, grad_out, segments, send_list, recv_list):
    row_count, shard_width = activations.shape
    dp_index = lax.axis_index("dp")
    seq_index = lax.axis_index("seq")
    tensor_index = lax.axis_index("tensor")
    y_index, core = dp_index // 2, dp_index % 2
    x_index, z_lo = tensor_index // 2, tensor_index % 2
    straight = core == z_lo

    block_count = row_count // BLK
    send_slots, recv_slots = send_list[0], recv_list[0]
    in_own, out_own = qkv_weight[:, 0, :], out_weight[0]

    def join_z(own, near, far, axis):
        here = jnp.where(straight, own, near)
        return jnp.where(
            seq_index == 0,
            jnp.concatenate([here, far], axis=axis),
            jnp.concatenate([far, here], axis=axis),
        )

    grad_x = lax.all_gather(
        grad_out, "tensor", axis=0, tiled=False, axis_index_groups=X_GROUPS
    )
    in_near, in_far, *out_far, arrived = fence(
        [z_near(in_own), z_far(in_own)]
        + [along_y(out_own, distance) for distance in OFFSETS[1:]]
        + [route_blocks(pick_blocks(activations, send_slots))],
        [grad_x],
    )

    in_all = lax.all_gather(join_z(in_own, in_near, in_far, 0), "dp", axis=0, tiled=False)
    moved = arrived[sources(recv_slots, block_count)].reshape(row_count, shard_width)
    out_four = jnp.stack([out_own, *out_far])
    near, out_far, *moved_x = fence(
        [z_near(out_four), z_far(out_four)]
        + [along_x(moved, distance) for distance in OFFSETS[1:]]
    )
    moved_x = [moved, *moved_x]

    out_here = jnp.where(straight, out_four, near)
    out_all = [out_here, out_far, over_cores(out_here), over_cores(out_far)]

    places = (x_index + jnp.array(OFFSETS, jnp.int32)) % NX
    order = jnp.array(POSITION, jnp.int32)[(jnp.arange(NX) - y_index) % NY]
    give_info = jnp.concatenate([jnp.stack([straight, seq_index]), order]).astype(jnp.int32)
    keep_info = jnp.concatenate([jnp.stack([~straight, seq_index]), order]).astype(jnp.int32)
    give_grad = heads_product(give_info, grad_x, out_all, jnp.bfloat16)
    (places,) = fence([places], [give_grad])
    give_kv, give_q = proj_product(1 - z_lo, places, moved_x, in_all, jnp.bfloat16)
    keep_kv, keep_q = proj_product(z_lo, places, moved_x, in_all, jnp.float32)
    keep_grad = heads_product(keep_info, grad_x, out_all, jnp.float32)

    prev_a = send(
        give_kv, lambda x, y, zh, zl, c: (x, y, 1, 1 - zl, c) if zh == 0 else None
    )
    prev_b = send(
        low(keep_kv), lambda x, y, zh, zl, c: (x, y, 1, zl, c) if zh == 0 else None
    )
    query_ids = lax.dynamic_slice_in_dim(segments, seq_index * row_count, row_count)
    padded_ids = jnp.concatenate([jnp.full((row_count,), -1, jnp.int32), segments])
    key_ids = lax.dynamic_slice_in_dim(padded_ids, seq_index * row_count, 2 * row_count)
    positions = jnp.arange(2 * row_count)
    mask = (
        (query_ids[None, :] == key_ids[:, None])
        & (positions[:, None] <= positions[None, :row_count] + row_count)
    ).astype(jnp.float32)
    head_out, logs, queries, kv = attend(
        keep_q, over_z_lo(give_q), keep_kv, over_z_lo(give_kv), prev_a, prev_b, mask
    )
    grad_queries, dkv_prev, dkv_own, dkv_low = attend_back(
        queries, kv, mask, head_out, logs, keep_grad, over_z_lo(give_grad)
    )
    targets = (x_index + jnp.arange(NX)) % NX
    grad_queries_x = over_z_lo(grad_queries)
    back = send(
        dkv_prev, lambda x, y, zh, zl, c: (x, y, 0, zl, c) if zh == 1 else None
    )
    back_x = send(
        dkv_prev, lambda x, y, zh, zl, c: (x, y, 0, 1 - zl, c) if zh == 1 else None
    )
    totals = query_product(z_lo, targets, grad_queries, in_all)
    totals = query_product(1 - z_lo, targets, grad_queries_x, in_all, totals)
    here, up, across, down = rest_product(
        z_lo, targets, totals, [dkv_own, back, over_z_lo(dkv_low), back_x], in_all
    )

    half = row_count // 2
    from_below = along_x(across[:half], -1)
    from_above = along_x(across[half:], 1)

    up = jnp.concatenate(
        [(wide(up[:half]) + wide(from_below)).astype(jnp.bfloat16), up[half:]], axis=0
    )
    down = jnp.concatenate(
        [down[:half], (wide(down[half:]) + wide(from_above)).astype(jnp.bfloat16)], axis=0
    )
    up, down = along_x(up, -1), along_x(down, 1)
    grad_moved = (wide(here) + wide(up) + wide(down)).astype(jnp.bfloat16)

    (heads,) = fence([head_out], [grad_queries_x])
    parts = mixed_product(keep_info, heads, over_z_lo(heads), out_all)
    (parts,) = fence([parts], [up, down])
    attended = lax.psum_scatter(
        parts.reshape(NX * row_count, shard_width),
        "tensor",
        scatter_dimension=0,
        tiled=True,
        axis_index_groups=X_GROUPS,
    )

    returned = route_blocks(pick_blocks(grad_moved, recv_slots))
    grad_in = returned[sources(send_slots, block_count)]
    return (attended, grad_in.reshape(row_count, shard_width))


def solution(mesh):
    placed = (
        P(("dp", "seq"), "tensor"),
        P(("dp", "seq"), "tensor", None),
        P("tensor", None, ("dp", "seq")),
        P(("dp", "seq"), "tensor"),
        P("dp"),
        P(("dp", "seq"), None),
        P(("dp", "seq"), None),
    )
    return jax.shard_map(
        body,
        mesh=mesh,
        in_specs=placed,
        out_specs=(P(("dp", "seq"), "tensor"), P(("dp", "seq"), "tensor")),
        check_vma=False,
    )
```

```python
import math

import jax
import jax.numpy as jnp
from jax import lax
from jax.experimental import pallas as pl
from jax.experimental.pallas import tpu as pltpu
from jax.sharding import PartitionSpec as P

HS = 128
GROUP = 6
BLK = 32
AXES = ("dp", "seq", "tensor")
NX, NY, NZ = 4, 4, 4
X_GROUPS = [[0, 2, 4, 6], [1, 3, 5, 7]]


def place(index):
    dp, seq, tensor = index // 16, index // 8 % 2, index % 8
    return tensor // 2, dp // 2, seq, tensor % 2, dp % 2


def index_of(x, y, z_hi, z_lo, core):
    return (y % NY * 2 + core) * 16 + z_hi * 8 + x % NX * 2 + z_lo


def send(block, target):
    pairs = []
    for source in range(128):
        goal = target(*place(source))
        if goal is not None:
            pairs.append((source, index_of(*goal)))
    return lax.ppermute(block, AXES, pairs)


def along_y(block, distance):
    return send(block, lambda x, y, zh, zl, c: (x, y - distance, zh, zl, c))


def over_cores(block):
    return send(block, lambda x, y, zh, zl, c: (x, y, zh, zl, 1 - c))


def over_z_lo(block):
    return send(block, lambda x, y, zh, zl, c: (x, y, zh, 1 - zl, c))


def z_near(block):
    return send(
        block, lambda x, y, zh, zl, c: (x, y, zh, 1 - zl, 1 - c) if zl != c else None
    )


def z_far(block):
    return send(
        block,
        lambda x, y, zh, zl, c: (x, y, 1 - zh, zl, c)
        if zl == c
        else (x, y, 1 - zh, 1 - zl, 1 - c),
    )


def along_x(block, distance):
    return send(block, lambda x, y, zh, zl, c: (x - distance, y, zh, zl, c))


def route_blocks(buffer):
    return lax.all_to_all(buffer, ("dp", "seq"), split_axis=0, concat_axis=0, tiled=True)


def nothing(*refs):
    pass


def fence(values, after=()):
    return pl.pallas_call(
        nothing,
        out_shape=[jax.ShapeDtypeStruct(v.shape, v.dtype) for v in values],
        in_specs=[anywhere()] * (len(values) + len(after)),
        out_specs=[anywhere()] * len(values),
        input_output_aliases={i: i for i in range(len(values))},
        cost_estimate=pl.CostEstimate(flops=0, bytes_accessed=0, transcendentals=0),
    )(*values, *after)


def dot(a, b, contract=((1,), (0,))):
    return lax.dot_general(a, b, (contract, ((), ())), preferred_element_type=jnp.float32)


NT = ((1,), (1,))
NN = ((1,), (0,))
MB = 1 << 20
OFFSETS = (0, 1, -1, 2)
POSITION = (0, 1, 3, 2)


def vmem():
    return pl.BlockSpec(memory_space=pltpu.VMEM)


def smem():
    return pl.BlockSpec(memory_space=pltpu.SMEM)


def anywhere():
    return pl.BlockSpec(memory_space=pl.ANY)


def params(size=24):
    return pltpu.CompilerParams(vmem_limit_bytes=size * MB)


def start_all(copies):
    for copy in copies:
        copy.start()


def wait_all(copies):
    for copy in copies:
        copy.wait()


def proj_kernel(info, *refs):
    rows, weights, out_kv, out_q = refs[:NX], refs[NX], refs[NX + 1], refs[NX + 2]
    lhs, held, total, lhs_sems, sems = refs[NX + 3 :]
    cuts = halves(info[1 + NX], weights.shape[2])
    copies = [
        [pltpu.make_async_copy(rows[r], lhs.at[r], lhs_sems.at[r])]
        + [
            pltpu.make_async_copy(
                weights.at[2 * info[1 + r] + info[0], i], held.at[r, cut], sems.at[r, i]
            )
            for i, cut in enumerate(cuts)
        ]
        for r in range(NX)
    ]
    start_all(copies[0])
    start_all(copies[1])
    for r in range(NX):
        wait_all(copies[r])
        if r + 2 < NX:
            start_all(copies[r + 2])
        term = dot(lhs[r], held[r])
        if r == 0:
            total[...] = term
        elif r < NX - 1:
            total[...] += term
        else:
            term = (total[...] + term).astype(out_q.dtype)
            out_q[...] = term[:, :SPAN]
            out_kv[...] = term[:, SPAN:]


def proj_product(info, rows, weights, dtype):
    row_count, depth = rows[0].shape
    width, full = weights.shape[3], NX * depth
    return pl.pallas_call(
        proj_kernel,
        out_shape=(
            jax.ShapeDtypeStruct((row_count, 2 * HS), dtype),
            jax.ShapeDtypeStruct((row_count, SPAN), dtype),
        ),
        in_specs=[smem()] + [anywhere()] * (NX + 1),
        out_specs=(vmem(), vmem()),
        scratch_shapes=[
            pltpu.VMEM((NX, row_count, depth), jnp.bfloat16),
            pltpu.VMEM((NX, depth, width), jnp.bfloat16),
            pltpu.VMEM((row_count, width), jnp.float32),
            pltpu.SemaphoreType.DMA((NX,)),
            pltpu.SemaphoreType.DMA((NX, 2)),
        ],
        compiler_params=params(53),
        cost_estimate=pl.CostEstimate(
            flops=2 * row_count * width * full,
            bytes_accessed=2 * full * (width + row_count),
            transcendentals=0,
        ),
    )(info, *rows, weights)


def halves(z_hi, size):
    return [pl.ds(pl.multiple_of(z * size, size), size) for z in (z_hi, 1 - z_hi)]


def chunk_copies(weights, z_hi, index, held, at, rows, sems):
    return [
        pltpu.make_async_copy(piece.at[index], held.at[at, rows, cut], sems.at[i])
        for i, (piece, cut) in enumerate(zip(weights, halves(z_hi, weights[0].shape[2])))
    ]


def heads_kernel(info, rows, *refs):
    weights, (out, lhs, held, total, lhs_sems, sems) = refs[:8], refs[8:]

    def copies_of(r, pair, index):
        every = pl.ds(0, held.shape[1])
        return [pltpu.make_async_copy(rows.at[r], lhs.at[r], lhs_sems.at[r])] + chunk_copies(
            pair, info[1], index, held, r, every, sems.at[r]
        )

    def begin(r):
        for pick in range(2):
            three, one = weights[4 * pick : 4 * pick + 2], weights[4 * pick + 2 : 4 * pick + 4]

            @pl.when((info[0] == pick) & (info[2 + r] < 3))
            def _():
                start_all(copies_of(r, three, info[2 + r]))

            @pl.when((info[0] == pick) & (info[2 + r] == 3))
            def _():
                start_all(copies_of(r, one, 0))

    begin(0)
    begin(1)
    for r in range(NX):
        wait_all(copies_of(r, weights[:2], 0))
        if r + 2 < NX:
            begin(r + 2)
        term = dot(lhs[r], held[r], NT)
        if r == 0:
            total[...] = term
        elif r < NX - 1:
            total[...] += term
        else:
            out[...] = (total[...] + term).astype(out.dtype)


def heads_product(info, rows, weights, dtype):
    row_count, depth = rows.shape[1:]
    width, full = weights[0].shape[1], NX * depth
    return pl.pallas_call(
        heads_kernel,
        out_shape=jax.ShapeDtypeStruct((row_count, width), dtype),
        in_specs=[smem()] + [anywhere()] * 9,
        out_specs=vmem(),
        scratch_shapes=[
            pltpu.VMEM((NX, row_count, depth), jnp.bfloat16),
            pltpu.VMEM((NX, width, depth), jnp.bfloat16),
            pltpu.VMEM((row_count, width), jnp.float32),
            pltpu.SemaphoreType.DMA((NX,)),
            pltpu.SemaphoreType.DMA((NX, 2)),
        ],
        compiler_params=params(53),
        cost_estimate=pl.CostEstimate(
            flops=2 * row_count * width * full,
            bytes_accessed=2 * full * (width + row_count),
            transcendentals=0,
        ),
    )(info, rows, *weights)


def mixed_kernel(info, own, theirs, *refs):
    weights, (out, lhs, held, ready, lhs_sems, sems, out_sems) = refs[:8], refs[8:]
    depth = own.shape[1]
    lhs_copies = [
        pltpu.make_async_copy(piece, lhs.at[:, pl.ds(i * depth, depth)], lhs_sems.at[i])
        for i, piece in enumerate((own, theirs))
    ]

    def copies_of(j, first, index):
        return [
            copy
            for side in range(2)
            for copy in chunk_copies(
                weights[(first + 4 * side) % 8 : (first + 4 * side) % 8 + 2],
                info[1], index, held, j, pl.ds(side * depth, depth), sems.at[j, side],
            )
        ]

    def begin(j):
        for pick in range(2):

            @pl.when((info[0] == pick) & (info[2 + j] < 3))
            def _():
                start_all(copies_of(j, 4 * pick, info[2 + j]))

            @pl.when((info[0] == pick) & (info[2 + j] == 3))
            def _():
                start_all(copies_of(j, 4 * pick + 2, 0))

    done = [pltpu.make_async_copy(ready.at[j], out.at[j], out_sems.at[j]) for j in range(NX)]
    begin(0)
    start_all(lhs_copies)
    wait_all(lhs_copies)
    begin(1)
    for j in range(NX):
        wait_all(copies_of(j, 0, 0))
        if j + 2 < NX:
            begin(j + 2)
        ready[j] = dot(lhs[...], held[j]).astype(out.dtype)
        done[j].start()
    wait_all(done)


def mixed_product(info, own, theirs, weights):
    row_count, depth = own.shape
    width = 2 * weights[0].shape[2]
    return pl.pallas_call(
        mixed_kernel,
        out_shape=jax.ShapeDtypeStruct((NX, row_count, width), jnp.bfloat16),
        in_specs=[smem()] + [anywhere()] * 10,
        out_specs=anywhere(),
        scratch_shapes=[
            pltpu.VMEM((row_count, 2 * depth), jnp.bfloat16),
            pltpu.VMEM((NX, 2 * depth, width), jnp.bfloat16),
            pltpu.VMEM((NX, row_count, width), jnp.bfloat16),
            pltpu.SemaphoreType.DMA((2,)),
            pltpu.SemaphoreType.DMA((NX, 2, 2)),
            pltpu.SemaphoreType.DMA((NX,)),
        ],
        compiler_params=params(53),
        cost_estimate=pl.CostEstimate(
            flops=4 * row_count * width * depth * NX,
            bytes_accessed=4 * NX * depth * width + 2 * row_count * (2 * depth + NX * width),
            transcendentals=0,
        ),
    )(info, own, theirs, *weights)


def wide(value):
    return value.astype(jnp.float32)


def low(value):
    return value.astype(jnp.bfloat16)


def query_kernel(count, info, q, weights, *refs):
    parts, outs = refs[:count], refs[count : count + NX]
    held, sems = refs[-2:]
    cuts = halves(info[1 + NX], weights.shape[2])
    copies = [
        [
            pltpu.make_async_copy(
                weights.at[2 * info[1 + j] + info[0], i, :, pl.ds(0, SPAN)],
                held.at[j, cut],
                sems.at[j, i],
            )
            for i, cut in enumerate(cuts)
        ]
        for j in range(NX)
    ]
    start_all(copies[0])
    start_all(copies[1])
    for j in range(NX):
        wait_all(copies[j])
        if j + 2 < NX:
            start_all(copies[j + 2])
        product = dot(q[...], held[j], NT)
        outs[j][...] = product + parts[j][...] if count else product


def query_product(info, q, weights, parts=()):
    row_count, width = q.shape[0], 2 * weights.shape[2]
    return pl.pallas_call(
        lambda *refs: query_kernel(len(parts), *refs),
        out_shape=[jax.ShapeDtypeStruct((row_count, width), jnp.float32)] * NX,
        in_specs=[smem(), vmem(), anywhere()] + [vmem()] * len(parts),
        out_specs=[vmem()] * NX,
        scratch_shapes=[
            pltpu.VMEM((NX, width, SPAN), jnp.bfloat16),
            pltpu.SemaphoreType.DMA((NX, 2)),
        ],
        compiler_params=params(48),
        cost_estimate=pl.CostEstimate(
            flops=2 * row_count * width * SPAN * NX,
            bytes_accessed=2 * NX * SPAN * width + 4 * row_count * NX * width,
            transcendentals=0,
        ),
    )(info, q, weights, *parts)


def rest_kernel(info, *refs):
    parts = refs[:NX]
    kv, kv_back, kv_x, kv_back_x, weights = refs[NX : NX + 5]
    outs = refs[NX + 5 : 2 * NX + 5]
    lhs, held, ready, sems, out_sems = refs[2 * NX + 5 :]
    copies = [
        [
            pltpu.make_async_copy(
                weights.at[2 * info[1 + j] + (info[0] + side) % 2, i, :, pl.ds(SPAN, 2 * HS)],
                held.at[j, cut, pl.ds(side * 2 * HS, 2 * HS)],
                sems.at[j, side, i],
            )
            for side in range(2)
            for i, cut in enumerate(halves(info[1 + NX], weights.shape[2]))
        ]
        for j in range(NX)
    ]
    done = [pltpu.make_async_copy(ready.at[j], outs[j], out_sems.at[j]) for j in range(NX)]
    order = (2, 1, 3, 0)
    start_all(copies[order[0]])
    start_all(copies[order[1]])
    lhs[:, : 2 * HS] = low(kv[...] + wide(kv_back[...]))
    lhs[:, 2 * HS :] = low(wide(kv_x[...]) + wide(kv_back_x[...]))
    for i, j in enumerate(order):
        wait_all(copies[j])
        if i + 2 < NX:
            start_all(copies[order[i + 2]])
        ready[j] = low(parts[j][...] + dot(lhs[...], held[j], NT))
        done[j].start()
    wait_all(done)


def rest_product(info, parts, operands, weights):
    row_count, width = parts[0].shape
    return pl.pallas_call(
        rest_kernel,
        out_shape=[jax.ShapeDtypeStruct((row_count, width), jnp.bfloat16)] * NX,
        in_specs=[smem()] + [vmem()] * (NX + 4) + [anywhere()],
        out_specs=[anywhere()] * NX,
        scratch_shapes=[
            pltpu.VMEM((row_count, 4 * HS), jnp.bfloat16),
            pltpu.VMEM((NX, width, 4 * HS), jnp.bfloat16),
            pltpu.VMEM((NX, row_count, width), jnp.bfloat16),
            pltpu.SemaphoreType.DMA((NX, 2, 2)),
            pltpu.SemaphoreType.DMA((NX,)),
        ],
        compiler_params=params(48),
        cost_estimate=pl.CostEstimate(
            flops=8 * row_count * width * HS * NX,
            bytes_accessed=8 * NX * HS * width + 6 * row_count * NX * width,
            transcendentals=0,
        ),
    )(info, *parts, *operands, weights)


SCALING = 1.0 / math.sqrt(HS)
SPAN = GROUP * HS


def forward_kernel(
    keep_q, came_q, keep_kv, came_kv, prev_a, prev_b, mask, head_out, logs, queries, kv
):
    rows = keep_q.shape[0]
    queries[...] = low(keep_q[...] + wide(came_q[...]))
    kv[:rows] = low(wide(prev_a[...]) + wide(prev_b[...]))
    kv[rows:] = low(keep_kv[...] + wide(came_kv[...]))
    keys, turned = kv[:, :HS], kv[:, HS:].T

    @pl.loop(0, GROUP, unroll=GROUP)
    def _(h):
        lanes = pl.ds(pl.multiple_of(h * HS, HS), HS)
        scores = dot(keys, queries[:, lanes], NT) * SCALING
        scores = jnp.where(mask[...] > 0, scores, -1e30)
        highest = jnp.max(scores, axis=0, keepdims=True)
        raised = jnp.exp(scores - highest)
        inverse = 1.0 / jnp.sum(raised, axis=0, keepdims=True)
        logs[h, 0:1] = highest
        logs[h, 1:2] = inverse
        head_out[:, lanes] = low(dot(turned, low(raised * inverse)).T)


def backward_kernel(
    queries, kv, mask, head_out, logs, keep_grad, came_grad,
    dq, dkv_prev, dkv_own, dkv_low, dk, dv, grad_heads,
):
    rows = queries.shape[0]
    grad_heads[...] = low(keep_grad[...] + wide(came_grad[...]))
    keys, values = kv[:, :HS], kv[:, HS:]
    turned = keys.T
    dk[...] = jnp.zeros_like(dk)
    dv[...] = jnp.zeros_like(dv)

    @pl.loop(0, GROUP, unroll=GROUP)
    def _(h):
        lanes = pl.ds(pl.multiple_of(h * HS, HS), HS)
        query, grad = queries[:, lanes], grad_heads[:, lanes]
        scores = dot(keys, query, NT) * SCALING
        scores = jnp.where(mask[...] > 0, scores, -1e30)
        probability = jnp.exp(scores - logs[h, 0:1]) * logs[h, 1:2]
        delta = jnp.sum((wide(grad) * wide(head_out[:, lanes])).T, axis=0, keepdims=True)
        score_grad = low(probability * (dot(values, grad, NT) - delta))
        dv[...] += dot(low(probability), grad)
        dk[...] += dot(score_grad, query)
        dq[:, lanes] = low((dot(turned, score_grad) * SCALING).T)

    dkv_prev[:, :HS] = low(dk[:rows] * SCALING)
    dkv_prev[:, HS:] = low(dv[:rows])
    dkv_own[:, :HS] = dk[rows:] * SCALING
    dkv_own[:, HS:] = dv[rows:]
    dkv_low[...] = low(dkv_own[...])


def attend(keep_q, came_q, keep_kv, came_kv, prev_a, prev_b, mask):
    rows = keep_q.shape[0]
    return pl.pallas_call(
        forward_kernel,
        out_shape=(
            jax.ShapeDtypeStruct((rows, SPAN), jnp.bfloat16),
            jax.ShapeDtypeStruct((GROUP, 8, rows), jnp.float32),
            jax.ShapeDtypeStruct((rows, SPAN), jnp.bfloat16),
            jax.ShapeDtypeStruct((2 * rows, 2 * HS), jnp.bfloat16),
        ),
        in_specs=[vmem()] * 7,
        out_specs=(vmem(),) * 4,
        compiler_params=params(),
        cost_estimate=pl.CostEstimate(
            flops=8 * rows * rows * HS * GROUP * 2, bytes_accessed=4 * MB,
            transcendentals=2 * rows * rows * GROUP,
        ),
    )(keep_q, came_q, keep_kv, came_kv, prev_a, prev_b, mask)


def attend_back(queries, kv, mask, head_out, logs, keep_grad, came_grad):
    rows = queries.shape[0]
    return pl.pallas_call(
        backward_kernel,
        out_shape=(
            jax.ShapeDtypeStruct((rows, SPAN), jnp.bfloat16),
            jax.ShapeDtypeStruct((rows, 2 * HS), jnp.bfloat16),
            jax.ShapeDtypeStruct((rows, 2 * HS), jnp.float32),
            jax.ShapeDtypeStruct((rows, 2 * HS), jnp.bfloat16),
        ),
        in_specs=[vmem()] * 7,
        out_specs=(vmem(),) * 4,
        scratch_shapes=[pltpu.VMEM((2 * rows, HS), jnp.float32)] * 2
        + [pltpu.VMEM((rows, SPAN), jnp.bfloat16)],
        compiler_params=params(),
        cost_estimate=pl.CostEstimate(
            flops=20 * rows * rows * HS * GROUP * 2, bytes_accessed=5 * MB,
            transcendentals=2 * rows * rows * GROUP,
        ),
    )(queries, kv, mask, head_out, logs, keep_grad, came_grad)


def pick_blocks(array, wanted):
    blocks = array.reshape(-1, BLK, array.shape[1])
    return jnp.where(
        (wanted >= 0)[:, None, None],
        blocks[jnp.maximum(wanted, 0)],
        jnp.zeros((), jnp.bfloat16),
    )


def sources(landing, block_count):
    return (
        jnp.zeros((block_count,), jnp.int32)
        .at[jnp.where(landing >= 0, landing, block_count)]
        .set(jnp.arange(landing.shape[0], dtype=jnp.int32), mode="drop")
    )


def body(activations, qkv_weight, out_weight, grad_out, segments, send_list, recv_list):
    row_count, shard_width = activations.shape
    dp_index = lax.axis_index("dp")
    seq_index = lax.axis_index("seq")
    tensor_index = lax.axis_index("tensor")
    y_index, core = dp_index // 2, dp_index % 2
    x_index, z_lo = tensor_index // 2, tensor_index % 2
    straight = core == z_lo

    block_count = row_count // BLK
    send_slots, recv_slots = send_list[0], recv_list[0]
    in_own, out_own = qkv_weight[:, 0, :], out_weight[0]

    grad_x = lax.all_gather(
        grad_out, "tensor", axis=0, tiled=False, axis_index_groups=X_GROUPS
    )
    in_near, in_far, out_up, out_down, arrived = fence(
        [
            z_near(in_own),
            z_far(in_own),
            along_y(out_own, 1),
            along_y(out_own, -1),
            route_blocks(pick_blocks(activations, send_slots)),
        ],
        [grad_x],
    )

    in_pair = jnp.stack([jnp.where(straight, in_own, in_near), in_far])
    in_all = lax.all_gather(in_pair, "dp", axis=0, tiled=False)
    moved = arrived[sources(recv_slots, block_count)].reshape(row_count, shard_width)
    out_three = jnp.stack([out_own, out_up, out_down])
    half = out_own.shape[0] // 2
    first, second = fence([along_y(out_up[:half], 1), along_y(out_down[half:], -1)])
    out_one = jnp.concatenate([first, second], axis=0)[None]
    near, out_three_far, near_one, out_one_far, *moved_x = fence(
        [z_near(out_three), z_far(out_three), z_near(out_one), z_far(out_one)]
        + [along_x(moved, distance) for distance in OFFSETS[1:]]
    )
    moved_x = [moved, *moved_x]

    out_mine = [
        jnp.where(straight, out_three, near),
        out_three_far,
        jnp.where(straight, out_one, near_one),
        out_one_far,
    ]
    out_all = out_mine + [over_cores(piece) for piece in out_mine]

    places = (x_index + jnp.array(OFFSETS, jnp.int32)) % NX
    order = jnp.array(POSITION, jnp.int32)[(jnp.arange(NX) - y_index) % NY]
    give_info = jnp.concatenate([jnp.stack([straight, seq_index]), order]).astype(jnp.int32)
    keep_info = jnp.concatenate([jnp.stack([~straight, seq_index]), order]).astype(jnp.int32)
    give_grad = heads_product(give_info, grad_x, out_all, jnp.bfloat16)
    (places,) = fence([places], [give_grad])

    def in_info(head, columns):
        return jnp.concatenate([head[None], columns, seq_index[None]]).astype(jnp.int32)

    give_kv, give_q = proj_product(in_info(1 - z_lo, places), moved_x, in_all, jnp.bfloat16)
    keep_kv, keep_q = proj_product(in_info(z_lo, places), moved_x, in_all, jnp.float32)
    keep_grad = heads_product(keep_info, grad_x, out_all, jnp.float32)

    prev_a = send(
        give_kv, lambda x, y, zh, zl, c: (x, y, 1, 1 - zl, c) if zh == 0 else None
    )
    prev_b = send(
        low(keep_kv), lambda x, y, zh, zl, c: (x, y, 1, zl, c) if zh == 0 else None
    )
    query_ids = lax.dynamic_slice_in_dim(segments, seq_index * row_count, row_count)
    padded_ids = jnp.concatenate([jnp.full((row_count,), -1, jnp.int32), segments])
    key_ids = lax.dynamic_slice_in_dim(padded_ids, seq_index * row_count, 2 * row_count)
    positions = jnp.arange(2 * row_count)
    mask = (
        (query_ids[None, :] == key_ids[:, None])
        & (positions[:, None] <= positions[None, :row_count] + row_count)
    ).astype(jnp.float32)
    head_out, logs, queries, kv = attend(
        keep_q, over_z_lo(give_q), keep_kv, over_z_lo(give_kv), prev_a, prev_b, mask
    )
    grad_queries, dkv_prev, dkv_own, dkv_low = attend_back(
        queries, kv, mask, head_out, logs, keep_grad, over_z_lo(give_grad)
    )
    targets = (x_index + jnp.arange(NX)) % NX
    grad_queries_x = over_z_lo(grad_queries)
    back = send(
        dkv_prev, lambda x, y, zh, zl, c: (x, y, 0, zl, c) if zh == 1 else None
    )
    back_x = send(
        dkv_prev, lambda x, y, zh, zl, c: (x, y, 0, 1 - zl, c) if zh == 1 else None
    )
    totals = query_product(in_info(z_lo, targets), grad_queries, in_all)
    totals = query_product(in_info(1 - z_lo, targets), grad_queries_x, in_all, totals)
    here, up, across, down = rest_product(
        in_info(z_lo, targets), totals, [dkv_own, back, over_z_lo(dkv_low), back_x], in_all
    )

    half = row_count // 2
    from_below = along_x(across[:half], -1)
    from_above = along_x(across[half:], 1)

    up = jnp.concatenate(
        [(wide(up[:half]) + wide(from_below)).astype(jnp.bfloat16), up[half:]], axis=0
    )
    down = jnp.concatenate(
        [down[:half], (wide(down[half:]) + wide(from_above)).astype(jnp.bfloat16)], axis=0
    )
    up, down = along_x(up, -1), along_x(down, 1)
    grad_moved = (wide(here) + wide(up) + wide(down)).astype(jnp.bfloat16)

    (heads,) = fence([head_out], [grad_queries_x])
    parts = mixed_product(keep_info, heads, over_z_lo(heads), out_all)
    (parts,) = fence([parts], [up, down])
    attended = lax.psum_scatter(
        parts.reshape(NX * row_count, shard_width),
        "tensor",
        scatter_dimension=0,
        tiled=True,
        axis_index_groups=X_GROUPS,
    )

    returned = route_blocks(pick_blocks(grad_moved, recv_slots))
    grad_in = returned[sources(send_slots, block_count)]
    return (attended, grad_in.reshape(row_count, shard_width))


def solution(mesh):
    placed = (
        P(("dp", "seq"), "tensor"),
        P(("dp", "seq"), "tensor", None),
        P("tensor", None, ("dp", "seq")),
        P(("dp", "seq"), "tensor"),
        P("dp"),
        P(("dp", "seq"), None),
        P(("dp", "seq"), None),
    )
    return jax.shard_map(
        body,
        mesh=mesh,
        in_specs=placed,
        out_specs=(P(("dp", "seq"), "tensor"), P(("dp", "seq"), "tensor")),
        check_vma=False,
    )
```

```python
import math

import jax
import jax.numpy as jnp
from jax import lax
from jax.experimental import pallas as pl
from jax.experimental.pallas import tpu as pltpu
from jax.sharding import PartitionSpec as P

HS = 128
GROUP = 6
BLK = 32
AXES = ("dp", "seq", "tensor")
NX, NY, NZ = 4, 4, 4
X_GROUPS = [[0, 2, 4, 6], [1, 3, 5, 7]]


def place(index):
    dp, seq, tensor = index // 16, index // 8 % 2, index % 8
    return tensor // 2, dp // 2, seq, tensor % 2, dp % 2


def index_of(x, y, z_hi, z_lo, core):
    return (y % NY * 2 + core) * 16 + z_hi * 8 + x % NX * 2 + z_lo


def send(block, target):
    pairs = []
    for source in range(128):
        goal = target(*place(source))
        if goal is not None:
            pairs.append((source, index_of(*goal)))
    return lax.ppermute(block, AXES, pairs)


def along_y(block, distance):
    return send(block, lambda x, y, zh, zl, c: (x, y - distance, zh, zl, c))


def over_cores(block):
    return send(block, lambda x, y, zh, zl, c: (x, y, zh, zl, 1 - c))


def over_z_lo(block):
    return send(block, lambda x, y, zh, zl, c: (x, y, zh, 1 - zl, c))


def z_near(block):
    return send(
        block, lambda x, y, zh, zl, c: (x, y, zh, 1 - zl, 1 - c) if zl != c else None
    )


def z_far(block):
    return send(
        block,
        lambda x, y, zh, zl, c: (x, y, 1 - zh, zl, c)
        if zl == c
        else (x, y, 1 - zh, 1 - zl, 1 - c),
    )


def along_x(block, distance):
    return send(block, lambda x, y, zh, zl, c: (x - distance, y, zh, zl, c))


def route_blocks(buffer):
    return lax.all_to_all(buffer, ("dp", "seq"), split_axis=0, concat_axis=0, tiled=True)


def nothing(*refs):
    pass


def fence(values, after=()):
    return pl.pallas_call(
        nothing,
        out_shape=[jax.ShapeDtypeStruct(v.shape, v.dtype) for v in values],
        in_specs=[anywhere()] * (len(values) + len(after)),
        out_specs=[anywhere()] * len(values),
        input_output_aliases={i: i for i in range(len(values))},
        cost_estimate=pl.CostEstimate(flops=0, bytes_accessed=0, transcendentals=0),
    )(*values, *after)


def dot(a, b, contract=((1,), (0,))):
    return lax.dot_general(a, b, (contract, ((), ())), preferred_element_type=jnp.float32)


NT = ((1,), (1,))
NN = ((1,), (0,))
MB = 1 << 20
OFFSETS = (0, 1, -1, 2)
POSITION = (0, 1, 3, 2)


def vmem():
    return pl.BlockSpec(memory_space=pltpu.VMEM)


def smem():
    return pl.BlockSpec(memory_space=pltpu.SMEM)


def anywhere():
    return pl.BlockSpec(memory_space=pl.ANY)


def params(size=24):
    return pltpu.CompilerParams(vmem_limit_bytes=size * MB)


def start_all(copies):
    for copy in copies:
        copy.start()


def wait_all(copies):
    for copy in copies:
        copy.wait()


def proj_kernel(info, *refs):
    rows, weights, out_kv, out_q = refs[:NX], refs[NX], refs[NX + 1], refs[NX + 2]
    lhs, held, total, lhs_sems, sems = refs[NX + 3 :]
    cuts = halves(info[1 + NX], weights.shape[2])
    copies = [
        [pltpu.make_async_copy(rows[r], lhs.at[r], lhs_sems.at[r])]
        + [
            pltpu.make_async_copy(
                weights.at[2 * info[1 + r] + info[0], i], held.at[r, cut], sems.at[r, i]
            )
            for i, cut in enumerate(cuts)
        ]
        for r in range(NX)
    ]
    start_all(copies[0])
    start_all(copies[1])
    for r in range(NX):
        wait_all(copies[r])
        if r + 2 < NX:
            start_all(copies[r + 2])
        term = dot(lhs[r], held[r])
        if r == 0:
            total[...] = term
        elif r < NX - 1:
            total[...] += term
        else:
            term = (total[...] + term).astype(out_q.dtype)
            out_q[...] = term[:, :SPAN]
            out_kv[...] = term[:, SPAN:]


def proj_product(info, rows, weights, dtype):
    row_count, depth = rows[0].shape
    width, full = weights.shape[3], NX * depth
    return pl.pallas_call(
        proj_kernel,
        out_shape=(
            jax.ShapeDtypeStruct((row_count, 2 * HS), dtype),
            jax.ShapeDtypeStruct((row_count, SPAN), dtype),
        ),
        in_specs=[smem()] + [anywhere()] * (NX + 1),
        out_specs=(vmem(), vmem()),
        scratch_shapes=[
            pltpu.VMEM((NX, row_count, depth), jnp.bfloat16),
            pltpu.VMEM((NX, depth, width), jnp.bfloat16),
            pltpu.VMEM((row_count, width), jnp.float32),
            pltpu.SemaphoreType.DMA((NX,)),
            pltpu.SemaphoreType.DMA((NX, 2)),
        ],
        compiler_params=params(53),
        cost_estimate=pl.CostEstimate(
            flops=2 * row_count * width * full,
            bytes_accessed=2 * full * (width + row_count),
            transcendentals=0,
        ),
    )(info, *rows, weights)


def halves(z_hi, size):
    return [pl.ds(pl.multiple_of(z * size, size), size) for z in (z_hi, 1 - z_hi)]


def chunk_copies(weights, z_hi, index, held, at, rows, sems):
    return [
        pltpu.make_async_copy(piece.at[index], held.at[at, rows, cut], sems.at[i])
        for i, (piece, cut) in enumerate(zip(weights, halves(z_hi, weights[0].shape[2])))
    ]


def heads_kernel(
    info, rows, here, far, here_x, far_x, out, lhs, held, total, lhs_sems, sems
):
    def copies_of(r, pair):
        every = pl.ds(0, held.shape[1])
        return [pltpu.make_async_copy(rows.at[r], lhs.at[r], lhs_sems.at[r])] + chunk_copies(
            pair, info[1], info[2 + r], held, r, every, sems.at[r]
        )

    def begin(r):
        for pick, pair in ((0, (here, far)), (1, (here_x, far_x))):

            @pl.when(info[0] == pick)
            def _():
                start_all(copies_of(r, pair))

    begin(0)
    begin(1)
    for r in range(NX):
        wait_all(copies_of(r, (here, far)))
        if r + 2 < NX:
            begin(r + 2)
        term = dot(lhs[r], held[r], NT)
        if r == 0:
            total[...] = term
        elif r < NX - 1:
            total[...] += term
        else:
            out[...] = (total[...] + term).astype(out.dtype)


def heads_product(info, rows, weights, dtype):
    row_count, depth = rows.shape[1:]
    width, full = weights[0].shape[1], NX * depth
    return pl.pallas_call(
        heads_kernel,
        out_shape=jax.ShapeDtypeStruct((row_count, width), dtype),
        in_specs=[smem()] + [anywhere()] * 5,
        out_specs=vmem(),
        scratch_shapes=[
            pltpu.VMEM((NX, row_count, depth), jnp.bfloat16),
            pltpu.VMEM((NX, width, depth), jnp.bfloat16),
            pltpu.VMEM((row_count, width), jnp.float32),
            pltpu.SemaphoreType.DMA((NX,)),
            pltpu.SemaphoreType.DMA((NX, 2)),
        ],
        compiler_params=params(53),
        cost_estimate=pl.CostEstimate(
            flops=2 * row_count * width * full,
            bytes_accessed=2 * full * (width + row_count),
            transcendentals=0,
        ),
    )(info, rows, *weights)


def mixed_kernel(
    info, own, theirs, here, far, here_x, far_x, out, lhs, held, ready, lhs_sems, sems, out_sems
):
    depth = own.shape[1]
    lhs_copies = [
        pltpu.make_async_copy(piece, lhs.at[:, pl.ds(i * depth, depth)], lhs_sems.at[i])
        for i, piece in enumerate((own, theirs))
    ]
    mine, other = (here, far), (here_x, far_x)

    def copies_of(j, pairs):
        return [
            copy
            for side, pair in enumerate(pairs)
            for copy in chunk_copies(
                pair, info[1], info[2 + j], held, j, pl.ds(side * depth, depth), sems.at[j, side]
            )
        ]

    def begin(j):
        for pick, pairs in ((0, (mine, other)), (1, (other, mine))):

            @pl.when(info[0] == pick)
            def _():
                start_all(copies_of(j, pairs))

    done = [pltpu.make_async_copy(ready.at[j], out.at[j], out_sems.at[j]) for j in range(NX)]
    begin(0)
    start_all(lhs_copies)
    wait_all(lhs_copies)
    begin(1)
    for j in range(NX):
        wait_all(copies_of(j, (mine, other)))
        if j + 2 < NX:
            begin(j + 2)
        ready[j] = dot(lhs[...], held[j]).astype(out.dtype)
        done[j].start()
    wait_all(done)


def mixed_product(info, own, theirs, weights):
    row_count, depth = own.shape
    width = 2 * weights[0].shape[2]
    return pl.pallas_call(
        mixed_kernel,
        out_shape=jax.ShapeDtypeStruct((NX, row_count, width), jnp.bfloat16),
        in_specs=[smem()] + [anywhere()] * 6,
        out_specs=anywhere(),
        scratch_shapes=[
            pltpu.VMEM((row_count, 2 * depth), jnp.bfloat16),
            pltpu.VMEM((NX, 2 * depth, width), jnp.bfloat16),
            pltpu.VMEM((NX, row_count, width), jnp.bfloat16),
            pltpu.SemaphoreType.DMA((2,)),
            pltpu.SemaphoreType.DMA((NX, 2, 2)),
            pltpu.SemaphoreType.DMA((NX,)),
        ],
        compiler_params=params(53),
        cost_estimate=pl.CostEstimate(
            flops=4 * row_count * width * depth * NX,
            bytes_accessed=4 * NX * depth * width + 2 * row_count * (2 * depth + NX * width),
            transcendentals=0,
        ),
    )(info, own, theirs, *weights)


def wide(value):
    return value.astype(jnp.float32)


def low(value):
    return value.astype(jnp.bfloat16)


def query_kernel(count, info, q, weights, *refs):
    parts, outs = refs[:count], refs[count : count + NX]
    held, sems = refs[-2:]
    cuts = halves(info[1 + NX], weights.shape[2])
    copies = [
        [
            pltpu.make_async_copy(
                weights.at[2 * info[1 + j] + info[0], i, :, pl.ds(0, SPAN)],
                held.at[j, cut],
                sems.at[j, i],
            )
            for i, cut in enumerate(cuts)
        ]
        for j in range(NX)
    ]
    start_all(copies[0])
    start_all(copies[1])
    for j in range(NX):
        wait_all(copies[j])
        if j + 2 < NX:
            start_all(copies[j + 2])
        product = dot(q[...], held[j], NT)
        outs[j][...] = product + parts[j][...] if count else product


def query_product(info, q, weights, parts=()):
    row_count, width = q.shape[0], 2 * weights.shape[2]
    return pl.pallas_call(
        lambda *refs: query_kernel(len(parts), *refs),
        out_shape=[jax.ShapeDtypeStruct((row_count, width), jnp.float32)] * NX,
        in_specs=[smem(), vmem(), anywhere()] + [vmem()] * len(parts),
        out_specs=[vmem()] * NX,
        input_output_aliases={3 + j: j for j in range(len(parts))},
        scratch_shapes=[
            pltpu.VMEM((NX, width, SPAN), jnp.bfloat16),
            pltpu.SemaphoreType.DMA((NX, 2)),
        ],
        compiler_params=params(48),
        cost_estimate=pl.CostEstimate(
            flops=2 * row_count * width * SPAN * NX,
            bytes_accessed=2 * NX * SPAN * width + 4 * row_count * NX * width,
            transcendentals=0,
        ),
    )(info, q, weights, *parts)


def rest_kernel(info, *refs):
    parts = refs[:NX]
    kv, kv_back, kv_x, kv_back_x, weights = refs[NX : NX + 5]
    outs = refs[NX + 5 : 2 * NX + 5]
    lhs, held, ready, sems, out_sems = refs[2 * NX + 5 :]
    copies = [
        [
            pltpu.make_async_copy(
                weights.at[2 * info[1 + j] + (info[0] + side) % 2, i, :, pl.ds(SPAN, 2 * HS)],
                held.at[j, cut, pl.ds(side * 2 * HS, 2 * HS)],
                sems.at[j, side, i],
            )
            for side in range(2)
            for i, cut in enumerate(halves(info[1 + NX], weights.shape[2]))
        ]
        for j in range(NX)
    ]
    done = [pltpu.make_async_copy(ready.at[j], outs[j], out_sems.at[j]) for j in range(NX)]
    order = (2, 1, 3, 0)
    start_all(copies[order[0]])
    start_all(copies[order[1]])
    lhs[:, : 2 * HS] = low(kv[...] + wide(kv_back[...]))
    lhs[:, 2 * HS :] = low(wide(kv_x[...]) + wide(kv_back_x[...]))
    for i, j in enumerate(order):
        wait_all(copies[j])
        if i + 2 < NX:
            start_all(copies[order[i + 2]])
        ready[j] = low(parts[j][...] + dot(lhs[...], held[j], NT))
        done[j].start()
    wait_all(done)


def rest_product(info, parts, operands, weights):
    row_count, width = parts[0].shape
    return pl.pallas_call(
        rest_kernel,
        out_shape=[jax.ShapeDtypeStruct((row_count, width), jnp.bfloat16)] * NX,
        in_specs=[smem()] + [vmem()] * (NX + 4) + [anywhere()],
        out_specs=[anywhere()] * NX,
        scratch_shapes=[
            pltpu.VMEM((row_count, 4 * HS), jnp.bfloat16),
            pltpu.VMEM((NX, width, 4 * HS), jnp.bfloat16),
            pltpu.VMEM((NX, row_count, width), jnp.bfloat16),
            pltpu.SemaphoreType.DMA((NX, 2, 2)),
            pltpu.SemaphoreType.DMA((NX,)),
        ],
        compiler_params=params(48),
        cost_estimate=pl.CostEstimate(
            flops=8 * row_count * width * HS * NX,
            bytes_accessed=8 * NX * HS * width + 6 * row_count * NX * width,
            transcendentals=0,
        ),
    )(info, *parts, *operands, weights)


SCALING = 1.0 / math.sqrt(HS)
SPAN = GROUP * HS


def forward_kernel(
    keep_q, came_q, keep_kv, came_kv, prev_a, prev_b, mask, head_out, logs, queries, kv
):
    rows = keep_q.shape[0]
    queries[...] = low(keep_q[...] + wide(came_q[...]))
    kv[:rows] = low(wide(prev_a[...]) + wide(prev_b[...]))
    kv[rows:] = low(keep_kv[...] + wide(came_kv[...]))
    keys, turned = kv[:, :HS], kv[:, HS:].T

    @pl.loop(0, GROUP, unroll=GROUP)
    def _(h):
        lanes = pl.ds(pl.multiple_of(h * HS, HS), HS)
        scores = dot(keys, queries[:, lanes], NT) * SCALING
        scores = jnp.where(mask[...] > 0, scores, -1e30)
        highest = jnp.max(scores, axis=0, keepdims=True)
        raised = jnp.exp(scores - highest)
        inverse = 1.0 / jnp.sum(raised, axis=0, keepdims=True)
        logs[h, 0:1] = highest
        logs[h, 1:2] = inverse
        head_out[:, lanes] = low(dot(turned, low(raised * inverse)).T)


def backward_kernel(
    queries, kv, mask, head_out, logs, keep_grad, came_grad,
    dq, dkv_prev, dkv_own, dkv_low, dk, dv, grad_heads,
):
    rows = queries.shape[0]
    grad_heads[...] = low(keep_grad[...] + wide(came_grad[...]))
    keys, values = kv[:, :HS], kv[:, HS:]
    turned = keys.T
    dk[...] = jnp.zeros_like(dk)
    dv[...] = jnp.zeros_like(dv)

    @pl.loop(0, GROUP, unroll=GROUP)
    def _(h):
        lanes = pl.ds(pl.multiple_of(h * HS, HS), HS)
        query, grad = queries[:, lanes], grad_heads[:, lanes]
        scores = dot(keys, query, NT) * SCALING
        scores = jnp.where(mask[...] > 0, scores, -1e30)
        probability = jnp.exp(scores - logs[h, 0:1]) * logs[h, 1:2]
        delta = jnp.sum((wide(grad) * wide(head_out[:, lanes])).T, axis=0, keepdims=True)
        score_grad = low(probability * (dot(values, grad, NT) - delta))
        dv[...] += dot(low(probability), grad)
        dk[...] += dot(score_grad, query)
        dq[:, lanes] = low((dot(turned, score_grad) * SCALING).T)

    dkv_prev[:, :HS] = low(dk[:rows] * SCALING)
    dkv_prev[:, HS:] = low(dv[:rows])
    dkv_own[:, :HS] = dk[rows:] * SCALING
    dkv_own[:, HS:] = dv[rows:]
    dkv_low[...] = low(dkv_own[...])


def attend(keep_q, came_q, keep_kv, came_kv, prev_a, prev_b, mask):
    rows = keep_q.shape[0]
    return pl.pallas_call(
        forward_kernel,
        out_shape=(
            jax.ShapeDtypeStruct((rows, SPAN), jnp.bfloat16),
            jax.ShapeDtypeStruct((GROUP, 8, rows), jnp.float32),
            jax.ShapeDtypeStruct((rows, SPAN), jnp.bfloat16),
            jax.ShapeDtypeStruct((2 * rows, 2 * HS), jnp.bfloat16),
        ),
        in_specs=[vmem()] * 7,
        out_specs=(vmem(),) * 4,
        compiler_params=params(),
        cost_estimate=pl.CostEstimate(
            flops=8 * rows * rows * HS * GROUP * 2, bytes_accessed=4 * MB,
            transcendentals=2 * rows * rows * GROUP,
        ),
    )(keep_q, came_q, keep_kv, came_kv, prev_a, prev_b, mask)


def attend_back(queries, kv, mask, head_out, logs, keep_grad, came_grad):
    rows = queries.shape[0]
    return pl.pallas_call(
        backward_kernel,
        out_shape=(
            jax.ShapeDtypeStruct((rows, SPAN), jnp.bfloat16),
            jax.ShapeDtypeStruct((rows, 2 * HS), jnp.bfloat16),
            jax.ShapeDtypeStruct((rows, 2 * HS), jnp.float32),
            jax.ShapeDtypeStruct((rows, 2 * HS), jnp.bfloat16),
        ),
        in_specs=[vmem()] * 7,
        out_specs=(vmem(),) * 4,
        scratch_shapes=[pltpu.VMEM((2 * rows, HS), jnp.float32)] * 2
        + [pltpu.VMEM((rows, SPAN), jnp.bfloat16)],
        compiler_params=params(),
        cost_estimate=pl.CostEstimate(
            flops=20 * rows * rows * HS * GROUP * 2, bytes_accessed=5 * MB,
            transcendentals=2 * rows * rows * GROUP,
        ),
    )(queries, kv, mask, head_out, logs, keep_grad, came_grad)


def pick_blocks(array, wanted):
    blocks = array.reshape(-1, BLK, array.shape[1])
    return jnp.where(
        (wanted >= 0)[:, None, None],
        blocks[jnp.maximum(wanted, 0)],
        jnp.zeros((), jnp.bfloat16),
    )


def sources(landing, block_count):
    return (
        jnp.zeros((block_count,), jnp.int32)
        .at[jnp.where(landing >= 0, landing, block_count)]
        .set(jnp.arange(landing.shape[0], dtype=jnp.int32), mode="drop")
    )


def body(activations, qkv_weight, out_weight, grad_out, segments, send_list, recv_list):
    row_count, shard_width = activations.shape
    dp_index = lax.axis_index("dp")
    seq_index = lax.axis_index("seq")
    tensor_index = lax.axis_index("tensor")
    y_index, core = dp_index // 2, dp_index % 2
    x_index, z_lo = tensor_index // 2, tensor_index % 2
    straight = core == z_lo

    block_count = row_count // BLK
    send_slots, recv_slots = send_list[0], recv_list[0]
    in_own, out_own = qkv_weight[:, 0, :], out_weight[0]

    grad_x = lax.all_gather(
        grad_out, "tensor", axis=0, tiled=False, axis_index_groups=X_GROUPS
    )
    out_own = out_own[None]
    in_near, in_far, out_up, out_down, near_own, far_own, arrived = fence(
        [
            z_near(in_own),
            z_far(in_own),
            along_y(out_own, 1),
            along_y(out_own, -1),
            z_near(out_own),
            z_far(out_own),
            route_blocks(pick_blocks(activations, send_slots)),
        ],
        [grad_x],
    )

    in_pair = jnp.stack([jnp.where(straight, in_own, in_near), in_far])
    in_all = lax.all_gather(in_pair, "dp", axis=0, tiled=False)
    moved = arrived[sources(recv_slots, block_count)].reshape(row_count, shard_width)
    out_two = jnp.concatenate([out_up, out_down], axis=0)
    half = out_own.shape[1] // 2
    first, second = fence([along_y(out_up[:, :half], 1), along_y(out_down[:, half:], -1)])
    out_one = jnp.concatenate([first, second], axis=1)
    near_two, far_two, near_one, far_one, *moved_x = fence(
        [z_near(out_two), z_far(out_two), z_near(out_one), z_far(out_one)]
        + [along_x(moved, distance) for distance in OFFSETS[1:]]
    )
    moved_x = [moved, *moved_x]

    out_here = jnp.where(
        straight,
        jnp.concatenate([out_own, out_two, out_one], axis=0),
        jnp.concatenate([near_own, near_two, near_one], axis=0),
    )
    out_far = jnp.concatenate([far_own, far_two, far_one], axis=0)
    out_all = [out_here, out_far, over_cores(out_here), over_cores(out_far)]

    places = (x_index + jnp.array(OFFSETS, jnp.int32)) % NX
    order = jnp.array(POSITION, jnp.int32)[(jnp.arange(NX) - y_index) % NY]
    give_info = jnp.concatenate([jnp.stack([straight, seq_index]), order]).astype(jnp.int32)
    keep_info = jnp.concatenate([jnp.stack([~straight, seq_index]), order]).astype(jnp.int32)
    give_grad = heads_product(give_info, grad_x, out_all, jnp.bfloat16)
    (places,) = fence([places], [give_grad])

    def in_info(head, columns):
        return jnp.concatenate([head[None], columns, seq_index[None]]).astype(jnp.int32)

    give_kv, give_q = proj_product(in_info(1 - z_lo, places), moved_x, in_all, jnp.bfloat16)
    keep_kv, keep_q = proj_product(in_info(z_lo, places), moved_x, in_all, jnp.float32)
    keep_grad = heads_product(keep_info, grad_x, out_all, jnp.float32)

    prev_a = send(
        give_kv, lambda x, y, zh, zl, c: (x, y, 1, 1 - zl, c) if zh == 0 else None
    )
    prev_b = send(
        low(keep_kv), lambda x, y, zh, zl, c: (x, y, 1, zl, c) if zh == 0 else None
    )
    query_ids = lax.dynamic_slice_in_dim(segments, seq_index * row_count, row_count)
    padded_ids = jnp.concatenate([jnp.full((row_count,), -1, jnp.int32), segments])
    key_ids = lax.dynamic_slice_in_dim(padded_ids, seq_index * row_count, 2 * row_count)
    positions = jnp.arange(2 * row_count)
    mask = (
        (query_ids[None, :] == key_ids[:, None])
        & (positions[:, None] <= positions[None, :row_count] + row_count)
    ).astype(jnp.float32)
    head_out, logs, queries, kv = attend(
        keep_q, over_z_lo(give_q), keep_kv, over_z_lo(give_kv), prev_a, prev_b, mask
    )
    grad_queries, dkv_prev, dkv_own, dkv_low = attend_back(
        queries, kv, mask, head_out, logs, keep_grad, over_z_lo(give_grad)
    )
    targets = (x_index + jnp.arange(NX)) % NX
    grad_queries_x = over_z_lo(grad_queries)
    back = send(
        dkv_prev, lambda x, y, zh, zl, c: (x, y, 0, zl, c) if zh == 1 else None
    )
    back_x = send(
        dkv_prev, lambda x, y, zh, zl, c: (x, y, 0, 1 - zl, c) if zh == 1 else None
    )
    totals = query_product(in_info(z_lo, targets), grad_queries, in_all)
    totals = query_product(in_info(1 - z_lo, targets), grad_queries_x, in_all, totals)
    here, up, across, down = rest_product(
        in_info(z_lo, targets), totals, [dkv_own, back, over_z_lo(dkv_low), back_x], in_all
    )

    half = row_count // 2
    from_below = along_x(across[:half], -1)
    from_above = along_x(across[half:], 1)

    up = jnp.concatenate(
        [(wide(up[:half]) + wide(from_below)).astype(jnp.bfloat16), up[half:]], axis=0
    )
    down = jnp.concatenate(
        [down[:half], (wide(down[half:]) + wide(from_above)).astype(jnp.bfloat16)], axis=0
    )
    up, down = along_x(up, -1), along_x(down, 1)
    grad_moved = (wide(here) + wide(up) + wide(down)).astype(jnp.bfloat16)

    (heads,) = fence([head_out], [grad_queries_x])
    parts = mixed_product(keep_info, heads, over_z_lo(heads), out_all)
    (parts,) = fence([parts], [up, down])
    attended = lax.psum_scatter(
        parts.reshape(NX * row_count, shard_width),
        "tensor",
        scatter_dimension=0,
        tiled=True,
        axis_index_groups=X_GROUPS,
    )

    returned = route_blocks(pick_blocks(grad_moved, recv_slots))
    grad_in = returned[sources(send_slots, block_count)]
    return (attended, grad_in.reshape(row_count, shard_width))


def solution(mesh):
    placed = (
        P(("dp", "seq"), "tensor"),
        P(("dp", "seq"), "tensor", None),
        P("tensor", None, ("dp", "seq")),
        P(("dp", "seq"), "tensor"),
        P("dp"),
        P(("dp", "seq"), None),
        P(("dp", "seq"), None),
    )
    return jax.shard_map(
        body,
        mesh=mesh,
        in_specs=placed,
        out_specs=(P(("dp", "seq"), "tensor"), P(("dp", "seq"), "tensor")),
        check_vma=False,
    )
```

```python
import math

import jax
import jax.numpy as jnp
from jax import lax
from jax.experimental import pallas as pl
from jax.experimental.pallas import tpu as pltpu
from jax.sharding import PartitionSpec as P

HS = 128
GROUP = 6
BLK = 32
AXES = ("dp", "seq", "tensor")
NX, NY, NZ = 4, 4, 4
X_GROUPS = [[0, 2, 4, 6], [1, 3, 5, 7]]


def place(index):
    dp, seq, tensor = index // 16, index // 8 % 2, index % 8
    return tensor // 2, dp // 2, seq, tensor % 2, dp % 2


def index_of(x, y, z_hi, z_lo, core):
    return (y % NY * 2 + core) * 16 + z_hi * 8 + x % NX * 2 + z_lo


def send(block, target):
    pairs = []
    for source in range(128):
        goal = target(*place(source))
        if goal is not None:
            pairs.append((source, index_of(*goal)))
    return lax.ppermute(block, AXES, pairs)


def along_y(block, distance):
    return send(block, lambda x, y, zh, zl, c: (x, y - distance, zh, zl, c))


def over_cores(block):
    return send(block, lambda x, y, zh, zl, c: (x, y, zh, zl, 1 - c))


def over_z_lo(block):
    return send(block, lambda x, y, zh, zl, c: (x, y, zh, 1 - zl, c))


def z_near(block):
    return send(
        block, lambda x, y, zh, zl, c: (x, y, zh, 1 - zl, 1 - c) if zl != c else None
    )


def z_far(block):
    return send(
        block,
        lambda x, y, zh, zl, c: (x, y, 1 - zh, zl, c)
        if zl == c
        else (x, y, 1 - zh, 1 - zl, 1 - c),
    )


def along_x(block, distance):
    return send(block, lambda x, y, zh, zl, c: (x - distance, y, zh, zl, c))


def route_blocks(buffer):
    return lax.all_to_all(buffer, ("dp", "seq"), split_axis=0, concat_axis=0, tiled=True)


def nothing(*refs):
    pass


def fence(values, after=()):
    return pl.pallas_call(
        nothing,
        out_shape=[jax.ShapeDtypeStruct(v.shape, v.dtype) for v in values],
        in_specs=[anywhere()] * (len(values) + len(after)),
        out_specs=[anywhere()] * len(values),
        input_output_aliases={i: i for i in range(len(values))},
        cost_estimate=pl.CostEstimate(flops=0, bytes_accessed=0, transcendentals=0),
    )(*values, *after)


def dot(a, b, contract=((1,), (0,))):
    return lax.dot_general(a, b, (contract, ((), ())), preferred_element_type=jnp.float32)


NT = ((1,), (1,))
NN = ((1,), (0,))
MB = 1 << 20
OFFSETS = (0, 1, -1, 2)
POSITION = (0, 1, 3, 2)


def vmem():
    return pl.BlockSpec(memory_space=pltpu.VMEM)


def smem():
    return pl.BlockSpec(memory_space=pltpu.SMEM)


def anywhere():
    return pl.BlockSpec(memory_space=pl.ANY)


def params(size=24):
    return pltpu.CompilerParams(vmem_limit_bytes=size * MB)


def start_all(copies):
    for copy in copies:
        copy.start()


def wait_all(copies):
    for copy in copies:
        copy.wait()


def proj_kernel(info, *refs):
    rows, weights, out_kv, out_q = refs[:NX], refs[NX], refs[NX + 1], refs[NX + 2]
    lhs, held, total, lhs_sems, sems = refs[NX + 3 :]
    cuts = halves(info[1 + NX], weights.shape[2])
    copies = [
        [pltpu.make_async_copy(rows[r], lhs.at[r], lhs_sems.at[r])]
        + [
            pltpu.make_async_copy(
                weights.at[2 * info[1 + r] + info[0], i], held.at[r, cut], sems.at[r, i]
            )
            for i, cut in enumerate(cuts)
        ]
        for r in range(NX)
    ]
    start_all(copies[0])
    start_all(copies[1])
    for r in range(NX):
        wait_all(copies[r])
        if r + 2 < NX:
            start_all(copies[r + 2])
        term = dot(lhs[r], held[r])
        if r == 0:
            total[...] = term
        elif r < NX - 1:
            total[...] += term
        else:
            term = (total[...] + term).astype(out_q.dtype)
            out_q[...] = term[:, :SPAN]
            out_kv[...] = term[:, SPAN:]


def proj_product(info, rows, weights, dtype):
    row_count, depth = rows[0].shape
    width, full = weights.shape[3], NX * depth
    return pl.pallas_call(
        proj_kernel,
        out_shape=(
            jax.ShapeDtypeStruct((row_count, 2 * HS), dtype),
            jax.ShapeDtypeStruct((row_count, SPAN), dtype),
        ),
        in_specs=[smem()] + [anywhere()] * (NX + 1),
        out_specs=(vmem(), vmem()),
        scratch_shapes=[
            pltpu.VMEM((NX, row_count, depth), jnp.bfloat16),
            pltpu.VMEM((NX, depth, width), jnp.bfloat16),
            pltpu.VMEM((row_count, width), jnp.float32),
            pltpu.SemaphoreType.DMA((NX,)),
            pltpu.SemaphoreType.DMA((NX, 2)),
        ],
        compiler_params=params(53),
        cost_estimate=pl.CostEstimate(
            flops=2 * row_count * width * full,
            bytes_accessed=2 * full * (width + row_count),
            transcendentals=0,
        ),
    )(info, *rows, weights)


def halves(z_hi, size):
    return [pl.ds(pl.multiple_of(z * size, size), size) for z in (z_hi, 1 - z_hi)]


def chunk_copies(weights, z_hi, index, held, at, rows, sems):
    return [
        pltpu.make_async_copy(piece.at[index], held.at[at, rows, cut], sems.at[i])
        for i, (piece, cut) in enumerate(zip(weights, halves(z_hi, weights[0].shape[2])))
    ]


def heads_kernel(
    info, rows, here, far, here_x, far_x, out, lhs, held, total, lhs_sems, sems
):
    def copies_of(r, pair):
        every = pl.ds(0, held.shape[1])
        return [pltpu.make_async_copy(rows.at[r], lhs.at[r], lhs_sems.at[r])] + chunk_copies(
            pair, info[1], info[2 + r], held, r, every, sems.at[r]
        )

    def begin(r):
        for pick, pair in ((0, (here, far)), (1, (here_x, far_x))):

            @pl.when(info[0] == pick)
            def _():
                start_all(copies_of(r, pair))

    begin(0)
    begin(1)
    for r in range(NX):
        wait_all(copies_of(r, (here, far)))
        if r + 2 < NX:
            begin(r + 2)
        term = dot(lhs[r], held[r], NT)
        if r == 0:
            total[...] = term
        elif r < NX - 1:
            total[...] += term
        else:
            out[...] = (total[...] + term).astype(out.dtype)


def heads_product(info, rows, weights, dtype):
    row_count, depth = rows.shape[1:]
    width, full = weights[0].shape[1], NX * depth
    return pl.pallas_call(
        heads_kernel,
        out_shape=jax.ShapeDtypeStruct((row_count, width), dtype),
        in_specs=[smem()] + [anywhere()] * 5,
        out_specs=vmem(),
        scratch_shapes=[
            pltpu.VMEM((NX, row_count, depth), jnp.bfloat16),
            pltpu.VMEM((NX, width, depth), jnp.bfloat16),
            pltpu.VMEM((row_count, width), jnp.float32),
            pltpu.SemaphoreType.DMA((NX,)),
            pltpu.SemaphoreType.DMA((NX, 2)),
        ],
        compiler_params=params(53),
        cost_estimate=pl.CostEstimate(
            flops=2 * row_count * width * full,
            bytes_accessed=2 * full * (width + row_count),
            transcendentals=0,
        ),
    )(info, rows, *weights)


def mixed_kernel(
    info, own, theirs, here, far, here_x, far_x,
    out_0, out_1, out_2, out_3, lhs, held, ready, lhs_sems, sems, out_sems,
):
    depth = own.shape[1]
    lhs_copies = [
        pltpu.make_async_copy(piece, lhs.at[:, pl.ds(i * depth, depth)], lhs_sems.at[i])
        for i, piece in enumerate((own, theirs))
    ]
    mine, other = (here, far), (here_x, far_x)

    def copies_of(j, pairs):
        return [
            copy
            for side, pair in enumerate(pairs)
            for copy in chunk_copies(
                pair, info[1], info[2 + j], held, j, pl.ds(side * depth, depth), sems.at[j, side]
            )
        ]

    def begin(j):
        for pick, pairs in ((0, (mine, other)), (1, (other, mine))):

            @pl.when(info[0] == pick)
            def _():
                start_all(copies_of(j, pairs))

    outs = (out_0, out_1, out_2, out_3)
    done = [pltpu.make_async_copy(ready.at[j], outs[j], out_sems.at[j]) for j in range(NX)]
    begin(0)
    start_all(lhs_copies)
    wait_all(lhs_copies)
    begin(1)
    for j in range(NX):
        wait_all(copies_of(j, (mine, other)))
        if j + 2 < NX:
            begin(j + 2)
        ready[j] = low(dot(lhs[...], held[j]))
        done[j].start()
    wait_all(done)


def mixed_product(info, own, theirs, weights):
    row_count, depth = own.shape
    width = 2 * weights[0].shape[2]
    return pl.pallas_call(
        mixed_kernel,
        out_shape=[jax.ShapeDtypeStruct((row_count, width), jnp.bfloat16)] * NX,
        in_specs=[smem()] + [anywhere()] * 6,
        out_specs=[anywhere()] * NX,
        scratch_shapes=[
            pltpu.VMEM((row_count, 2 * depth), jnp.bfloat16),
            pltpu.VMEM((NX, 2 * depth, width), jnp.bfloat16),
            pltpu.VMEM((NX, row_count, width), jnp.bfloat16),
            pltpu.SemaphoreType.DMA((2,)),
            pltpu.SemaphoreType.DMA((NX, 2, 2)),
            pltpu.SemaphoreType.DMA((NX,)),
        ],
        compiler_params=params(53),
        cost_estimate=pl.CostEstimate(
            flops=4 * row_count * width * depth * NX,
            bytes_accessed=4 * NX * depth * width + 2 * row_count * (2 * depth + NX * width),
            transcendentals=0,
        ),
    )(info, own, theirs, *weights)


def wide(value):
    return value.astype(jnp.float32)


def low(value):
    return value.astype(jnp.bfloat16)


def query_kernel(count, info, q, weights, *refs):
    parts, outs = refs[:count], refs[count : count + NX]
    held, sems = refs[-2:]
    cuts = halves(info[1 + NX], weights.shape[2])
    copies = [
        [
            pltpu.make_async_copy(
                weights.at[2 * info[1 + j] + info[0], i, :, pl.ds(0, SPAN)],
                held.at[j, cut],
                sems.at[j, i],
            )
            for i, cut in enumerate(cuts)
        ]
        for j in range(NX)
    ]
    start_all(copies[0])
    start_all(copies[1])
    for j in range(NX):
        wait_all(copies[j])
        if j + 2 < NX:
            start_all(copies[j + 2])
        product = dot(q[...], held[j], NT)
        outs[j][...] = product + parts[j][...] if count else product


def query_product(info, q, weights, parts=()):
    row_count, width = q.shape[0], 2 * weights.shape[2]
    return pl.pallas_call(
        lambda *refs: query_kernel(len(parts), *refs),
        out_shape=[jax.ShapeDtypeStruct((row_count, width), jnp.float32)] * NX,
        in_specs=[smem(), vmem(), anywhere()] + [vmem()] * len(parts),
        out_specs=[vmem()] * NX,
        input_output_aliases={3 + j: j for j in range(len(parts))},
        scratch_shapes=[
            pltpu.VMEM((NX, width, SPAN), jnp.bfloat16),
            pltpu.SemaphoreType.DMA((NX, 2)),
        ],
        compiler_params=params(48),
        cost_estimate=pl.CostEstimate(
            flops=2 * row_count * width * SPAN * NX,
            bytes_accessed=2 * NX * SPAN * width + 4 * row_count * NX * width,
            transcendentals=0,
        ),
    )(info, q, weights, *parts)


def rest_kernel(info, *refs):
    parts = refs[:NX]
    kv, kv_back, kv_x, kv_back_x, weights = refs[NX : NX + 5]
    outs = refs[NX + 5 : 2 * NX + 5]
    lhs, held, ready, sems, out_sems = refs[2 * NX + 5 :]
    copies = [
        [
            pltpu.make_async_copy(
                weights.at[2 * info[1 + j] + (info[0] + side) % 2, i, :, pl.ds(SPAN, 2 * HS)],
                held.at[j, cut, pl.ds(side * 2 * HS, 2 * HS)],
                sems.at[j, side, i],
            )
            for side in range(2)
            for i, cut in enumerate(halves(info[1 + NX], weights.shape[2]))
        ]
        for j in range(NX)
    ]
    done = [pltpu.make_async_copy(ready.at[j], outs[j], out_sems.at[j]) for j in range(NX)]
    order = (2, 1, 3, 0)
    start_all(copies[order[0]])
    start_all(copies[order[1]])
    lhs[:, : 2 * HS] = low(kv[...] + wide(kv_back[...]))
    lhs[:, 2 * HS :] = low(wide(kv_x[...]) + wide(kv_back_x[...]))
    for i, j in enumerate(order):
        wait_all(copies[j])
        if i + 2 < NX:
            start_all(copies[order[i + 2]])
        ready[j] = low(parts[j][...] + dot(lhs[...], held[j], NT))
        done[j].start()
    wait_all(done)


def rest_product(info, parts, operands, weights):
    row_count, width = parts[0].shape
    return pl.pallas_call(
        rest_kernel,
        out_shape=[jax.ShapeDtypeStruct((row_count, width), jnp.bfloat16)] * NX,
        in_specs=[smem()] + [vmem()] * (NX + 4) + [anywhere()],
        out_specs=[anywhere()] * NX,
        scratch_shapes=[
            pltpu.VMEM((row_count, 4 * HS), jnp.bfloat16),
            pltpu.VMEM((NX, width, 4 * HS), jnp.bfloat16),
            pltpu.VMEM((NX, row_count, width), jnp.bfloat16),
            pltpu.SemaphoreType.DMA((NX, 2, 2)),
            pltpu.SemaphoreType.DMA((NX,)),
        ],
        compiler_params=params(48),
        cost_estimate=pl.CostEstimate(
            flops=8 * row_count * width * HS * NX,
            bytes_accessed=8 * NX * HS * width + 6 * row_count * NX * width,
            transcendentals=0,
        ),
    )(info, *parts, *operands, weights)


SCALING = 1.0 / math.sqrt(HS)
SPAN = GROUP * HS


def forward_kernel(
    keep_q, came_q, keep_kv, came_kv, prev_a, prev_b, mask, head_out, logs, queries, kv
):
    rows = keep_q.shape[0]
    queries[...] = low(keep_q[...] + wide(came_q[...]))
    kv[:rows] = low(wide(prev_a[...]) + wide(prev_b[...]))
    kv[rows:] = low(keep_kv[...] + wide(came_kv[...]))
    keys, turned = kv[:, :HS], kv[:, HS:].T

    @pl.loop(0, GROUP, unroll=GROUP)
    def _(h):
        lanes = pl.ds(pl.multiple_of(h * HS, HS), HS)
        scores = dot(keys, queries[:, lanes], NT) * SCALING
        scores = jnp.where(mask[...] > 0, scores, -1e30)
        highest = jnp.max(scores, axis=0, keepdims=True)
        raised = jnp.exp(scores - highest)
        inverse = 1.0 / jnp.sum(raised, axis=0, keepdims=True)
        logs[h, 0:1] = highest
        logs[h, 1:2] = inverse
        head_out[:, lanes] = low(dot(turned, low(raised * inverse)).T)


def backward_kernel(
    queries, kv, mask, head_out, logs, keep_grad, came_grad,
    dq, dkv_prev, dkv_own, dkv_low, dk, dv, grad_heads,
):
    rows = queries.shape[0]
    grad_heads[...] = low(keep_grad[...] + wide(came_grad[...]))
    keys, values = kv[:, :HS], kv[:, HS:]
    turned = keys.T
    dk[...] = jnp.zeros_like(dk)
    dv[...] = jnp.zeros_like(dv)

    @pl.loop(0, GROUP, unroll=GROUP)
    def _(h):
        lanes = pl.ds(pl.multiple_of(h * HS, HS), HS)
        query, grad = queries[:, lanes], grad_heads[:, lanes]
        scores = dot(keys, query, NT) * SCALING
        scores = jnp.where(mask[...] > 0, scores, -1e30)
        probability = jnp.exp(scores - logs[h, 0:1]) * logs[h, 1:2]
        delta = jnp.sum((wide(grad) * wide(head_out[:, lanes])).T, axis=0, keepdims=True)
        score_grad = low(probability * (dot(values, grad, NT) - delta))
        dv[...] += dot(low(probability), grad)
        dk[...] += dot(score_grad, query)
        dq[:, lanes] = low((dot(turned, score_grad) * SCALING).T)

    dkv_prev[:, :HS] = low(dk[:rows] * SCALING)
    dkv_prev[:, HS:] = low(dv[:rows])
    dkv_own[:, :HS] = dk[rows:] * SCALING
    dkv_own[:, HS:] = dv[rows:]
    dkv_low[...] = low(dkv_own[...])


def attend(keep_q, came_q, keep_kv, came_kv, prev_a, prev_b, mask):
    rows = keep_q.shape[0]
    return pl.pallas_call(
        forward_kernel,
        out_shape=(
            jax.ShapeDtypeStruct((rows, SPAN), jnp.bfloat16),
            jax.ShapeDtypeStruct((GROUP, 8, rows), jnp.float32),
            jax.ShapeDtypeStruct((rows, SPAN), jnp.bfloat16),
            jax.ShapeDtypeStruct((2 * rows, 2 * HS), jnp.bfloat16),
        ),
        in_specs=[vmem()] * 7,
        out_specs=(vmem(),) * 4,
        compiler_params=params(),
        cost_estimate=pl.CostEstimate(
            flops=8 * rows * rows * HS * GROUP * 2, bytes_accessed=4 * MB,
            transcendentals=2 * rows * rows * GROUP,
        ),
    )(keep_q, came_q, keep_kv, came_kv, prev_a, prev_b, mask)


def attend_back(queries, kv, mask, head_out, logs, keep_grad, came_grad):
    rows = queries.shape[0]
    return pl.pallas_call(
        backward_kernel,
        out_shape=(
            jax.ShapeDtypeStruct((rows, SPAN), jnp.bfloat16),
            jax.ShapeDtypeStruct((rows, 2 * HS), jnp.bfloat16),
            jax.ShapeDtypeStruct((rows, 2 * HS), jnp.float32),
            jax.ShapeDtypeStruct((rows, 2 * HS), jnp.bfloat16),
        ),
        in_specs=[vmem()] * 7,
        out_specs=(vmem(),) * 4,
        scratch_shapes=[pltpu.VMEM((2 * rows, HS), jnp.float32)] * 2
        + [pltpu.VMEM((rows, SPAN), jnp.bfloat16)],
        compiler_params=params(),
        cost_estimate=pl.CostEstimate(
            flops=20 * rows * rows * HS * GROUP * 2, bytes_accessed=5 * MB,
            transcendentals=2 * rows * rows * GROUP,
        ),
    )(queries, kv, mask, head_out, logs, keep_grad, came_grad)


def pick_blocks(array, wanted):
    blocks = array.reshape(-1, BLK, array.shape[1])
    return jnp.where(
        (wanted >= 0)[:, None, None],
        blocks[jnp.maximum(wanted, 0)],
        jnp.zeros((), jnp.bfloat16),
    )


def sources(landing, block_count):
    return (
        jnp.zeros((block_count,), jnp.int32)
        .at[jnp.where(landing >= 0, landing, block_count)]
        .set(jnp.arange(landing.shape[0], dtype=jnp.int32), mode="drop")
    )


def body(activations, qkv_weight, out_weight, grad_out, segments, send_list, recv_list):
    row_count, shard_width = activations.shape
    dp_index = lax.axis_index("dp")
    seq_index = lax.axis_index("seq")
    tensor_index = lax.axis_index("tensor")
    y_index, core = dp_index // 2, dp_index % 2
    x_index, z_lo = tensor_index // 2, tensor_index % 2
    straight = core == z_lo

    block_count = row_count // BLK
    send_slots, recv_slots = send_list[0], recv_list[0]
    in_own, out_own = qkv_weight[:, 0, :], out_weight[0]

    grad_x = lax.all_gather(
        grad_out, "tensor", axis=0, tiled=False, axis_index_groups=X_GROUPS
    )
    out_own = out_own[None]
    in_near, in_far, out_up, out_down, near_own, far_own = fence(
        [
            z_near(in_own),
            z_far(in_own),
            along_y(out_own, 1),
            along_y(out_own, -1),
            z_near(out_own),
            z_far(out_own),
        ],
    )

    in_pair = jnp.stack([jnp.where(straight, in_own, in_near), in_far])
    in_all = lax.all_gather(in_pair, "dp", axis=0, tiled=False)
    out_two = jnp.concatenate([out_up, out_down], axis=0)
    half = out_own.shape[1] // 2
    near_two, far_two, first, second, arrived = fence(
        [
            z_near(out_two),
            z_far(out_two),
            along_y(out_up[:, :half], 1),
            along_y(out_down[:, half:], -1),
            route_blocks(pick_blocks(activations, send_slots)),
        ],
        [grad_x],
    )

    moved = arrived[sources(recv_slots, block_count)].reshape(row_count, shard_width)
    out_one = jnp.concatenate([first, second], axis=1)
    near_one, far_one, moved_up, moved_down = fence(
        [z_near(out_one), z_far(out_one), along_x(moved, 1), along_x(moved, -1)]
    )
    moved_x = [moved, moved_up, moved_down, along_x(moved, 2)]

    out_here = jnp.where(
        straight,
        jnp.concatenate([out_own, out_two, out_one], axis=0),
        jnp.concatenate([near_own, near_two, near_one], axis=0),
    )
    out_far = jnp.concatenate([far_own, far_two, far_one], axis=0)
    out_all = [out_here, out_far, over_cores(out_here), over_cores(out_far)]

    places = (x_index + jnp.array(OFFSETS, jnp.int32)) % NX
    order = jnp.array(POSITION, jnp.int32)[(jnp.arange(NX) - y_index) % NY]
    give_info = jnp.concatenate([jnp.stack([straight, seq_index]), order]).astype(jnp.int32)
    keep_info = jnp.concatenate([jnp.stack([~straight, seq_index]), order]).astype(jnp.int32)
    give_grad = heads_product(give_info, grad_x, out_all, jnp.bfloat16)
    (places,) = fence([places], [give_grad])

    def in_info(head, columns):
        return jnp.concatenate([head[None], columns, seq_index[None]]).astype(jnp.int32)

    give_kv, give_q = proj_product(in_info(1 - z_lo, places), moved_x, in_all, jnp.bfloat16)
    keep_kv, keep_q = proj_product(in_info(z_lo, places), moved_x, in_all, jnp.float32)
    keep_grad = heads_product(keep_info, grad_x, out_all, jnp.float32)

    (late_kv,) = fence([give_kv], [keep_kv])
    prev_a = send(
        late_kv, lambda x, y, zh, zl, c: (x, y, 1, 1 - zl, c) if zh == 0 else None
    )
    prev_b = send(
        low(keep_kv), lambda x, y, zh, zl, c: (x, y, 1, zl, c) if zh == 0 else None
    )
    query_ids = lax.dynamic_slice_in_dim(segments, seq_index * row_count, row_count)
    padded_ids = jnp.concatenate([jnp.full((row_count,), -1, jnp.int32), segments])
    key_ids = lax.dynamic_slice_in_dim(padded_ids, seq_index * row_count, 2 * row_count)
    positions = jnp.arange(2 * row_count)
    mask = (
        (query_ids[None, :] == key_ids[:, None])
        & (positions[:, None] <= positions[None, :row_count] + row_count)
    ).astype(jnp.float32)
    head_out, logs, queries, kv = attend(
        keep_q, over_z_lo(give_q), keep_kv, over_z_lo(give_kv), prev_a, prev_b, mask
    )
    grad_queries, dkv_prev, dkv_own, dkv_low = attend_back(
        queries, kv, mask, head_out, logs, keep_grad, over_z_lo(give_grad)
    )
    targets = (x_index + jnp.arange(NX)) % NX
    grad_queries_x = over_z_lo(grad_queries)
    back = send(
        dkv_prev, lambda x, y, zh, zl, c: (x, y, 0, zl, c) if zh == 1 else None
    )
    back_x = send(
        dkv_prev, lambda x, y, zh, zl, c: (x, y, 0, 1 - zl, c) if zh == 1 else None
    )
    totals = query_product(in_info(z_lo, targets), grad_queries, in_all)
    totals = query_product(in_info(1 - z_lo, targets), grad_queries_x, in_all, totals)
    here, up, across, down = rest_product(
        in_info(z_lo, targets), totals, [dkv_own, back, over_z_lo(dkv_low), back_x], in_all
    )

    half = row_count // 2
    from_below = along_x(across[:half], -1)
    from_above = along_x(across[half:], 1)

    up = jnp.concatenate(
        [(wide(up[:half]) + wide(from_below)).astype(jnp.bfloat16), up[half:]], axis=0
    )
    down = jnp.concatenate(
        [down[:half], (wide(down[half:]) + wide(from_above)).astype(jnp.bfloat16)], axis=0
    )
    up, down = along_x(up, -1), along_x(down, 1)
    grad_moved = (wide(here) + wide(up) + wide(down)).astype(jnp.bfloat16)

    (heads,) = fence([head_out], [grad_queries_x])
    order = jnp.array(POSITION, jnp.int32)[(targets - y_index) % NY]
    mixed_info = jnp.concatenate([keep_info[:2], order])
    own_part, *others = mixed_product(mixed_info, heads, over_z_lo(heads), out_all)
    others = fence(others, [up, down])
    attended = wide(own_part)
    for part, distance in zip(others, (-1, 2, 1)):
        attended += wide(along_x(part, distance))
    attended = low(attended)

    returned = route_blocks(pick_blocks(grad_moved, recv_slots))
    grad_in = returned[sources(send_slots, block_count)]
    return (attended, grad_in.reshape(row_count, shard_width))


def solution(mesh):
    placed = (
        P(("dp", "seq"), "tensor"),
        P(("dp", "seq"), "tensor", None),
        P("tensor", None, ("dp", "seq")),
        P(("dp", "seq"), "tensor"),
        P("dp"),
        P(("dp", "seq"), None),
        P(("dp", "seq"), None),
    )
    return jax.shard_map(
        body,
        mesh=mesh,
        in_specs=placed,
        out_specs=(P(("dp", "seq"), "tensor"), P(("dp", "seq"), "tensor")),
        check_vma=False,
    )
```

```python
import math

import jax
import jax.numpy as jnp
from jax import lax
from jax.experimental import pallas as pl
from jax.experimental.pallas import tpu as pltpu
from jax.sharding import PartitionSpec as P

HS = 128
GROUP = 6
BLK = 32
AXES = ("dp", "seq", "tensor")
NX, NY, NZ = 4, 4, 4
X_GROUPS = [[0, 2, 4, 6], [1, 3, 5, 7]]


def place(index):
    dp, seq, tensor = index // 16, index // 8 % 2, index % 8
    return tensor // 2, dp // 2, seq, tensor % 2, dp % 2


def index_of(x, y, z_hi, z_lo, core):
    return (y % NY * 2 + core) * 16 + z_hi * 8 + x % NX * 2 + z_lo


def send(block, target):
    pairs = []
    for source in range(128):
        goal = target(*place(source))
        if goal is not None:
            pairs.append((source, index_of(*goal)))
    return lax.ppermute(block, AXES, pairs)


def along_y(block, distance):
    return send(block, lambda x, y, zh, zl, c: (x, y - distance, zh, zl, c))


def over_cores(block):
    return send(block, lambda x, y, zh, zl, c: (x, y, zh, zl, 1 - c))


def over_z_lo(block):
    return send(block, lambda x, y, zh, zl, c: (x, y, zh, 1 - zl, c))


def z_near(block):
    return send(
        block, lambda x, y, zh, zl, c: (x, y, zh, 1 - zl, 1 - c) if zl != c else None
    )


def z_far(block):
    return send(
        block,
        lambda x, y, zh, zl, c: (x, y, 1 - zh, zl, c)
        if zl == c
        else (x, y, 1 - zh, 1 - zl, 1 - c),
    )


def along_x(block, distance):
    return send(block, lambda x, y, zh, zl, c: (x - distance, y, zh, zl, c))


def route_blocks(buffer):
    return lax.all_to_all(buffer, ("dp", "seq"), split_axis=0, concat_axis=0, tiled=True)


def nothing(*refs):
    pass


def fence(values, after=()):
    return pl.pallas_call(
        nothing,
        out_shape=[jax.ShapeDtypeStruct(v.shape, v.dtype) for v in values],
        in_specs=[anywhere()] * (len(values) + len(after)),
        out_specs=[anywhere()] * len(values),
        input_output_aliases={i: i for i in range(len(values))},
        cost_estimate=pl.CostEstimate(flops=0, bytes_accessed=0, transcendentals=0),
    )(*values, *after)


def dot(a, b, contract=((1,), (0,))):
    return lax.dot_general(a, b, (contract, ((), ())), preferred_element_type=jnp.float32)


NT = ((1,), (1,))
NN = ((1,), (0,))
MB = 1 << 20
OFFSETS = (0, 1, -1, 2)
POSITION = (0, 1, 3, 2)


def vmem():
    return pl.BlockSpec(memory_space=pltpu.VMEM)


def smem():
    return pl.BlockSpec(memory_space=pltpu.SMEM)


def anywhere():
    return pl.BlockSpec(memory_space=pl.ANY)


def params(size=24):
    return pltpu.CompilerParams(vmem_limit_bytes=size * MB)


def start_all(copies):
    for copy in copies:
        copy.start()


def wait_all(copies):
    for copy in copies:
        copy.wait()


def proj_kernel(info, *refs):
    rows, weights, out_kv, out_q = refs[:NX], refs[NX], refs[NX + 1], refs[NX + 2]
    lhs, held, total, lhs_sems, sems = refs[NX + 3 :]
    cuts = halves(info[1 + NX], weights.shape[2])
    copies = [
        [pltpu.make_async_copy(rows[r], lhs.at[r], lhs_sems.at[r])]
        + [
            pltpu.make_async_copy(
                weights.at[2 * info[1 + r] + info[0], i], held.at[r, cut], sems.at[r, i]
            )
            for i, cut in enumerate(cuts)
        ]
        for r in range(NX)
    ]
    start_all(copies[0])
    start_all(copies[1])
    for r in range(NX):
        wait_all(copies[r])
        if r + 2 < NX:
            start_all(copies[r + 2])
        term = dot(lhs[r], held[r])
        if r == 0:
            total[...] = term
        elif r < NX - 1:
            total[...] += term
        else:
            term = (total[...] + term).astype(out_q.dtype)
            out_q[...] = term[:, :SPAN]
            out_kv[...] = term[:, SPAN:]


def proj_product(info, rows, weights, dtype):
    row_count, depth = rows[0].shape
    width, full = weights.shape[3], NX * depth
    return pl.pallas_call(
        proj_kernel,
        out_shape=(
            jax.ShapeDtypeStruct((row_count, 2 * HS), dtype),
            jax.ShapeDtypeStruct((row_count, SPAN), dtype),
        ),
        in_specs=[smem()] + [anywhere()] * (NX + 1),
        out_specs=(vmem(), vmem()),
        scratch_shapes=[
            pltpu.VMEM((NX, row_count, depth), jnp.bfloat16),
            pltpu.VMEM((NX, depth, width), jnp.bfloat16),
            pltpu.VMEM((row_count, width), jnp.float32),
            pltpu.SemaphoreType.DMA((NX,)),
            pltpu.SemaphoreType.DMA((NX, 2)),
        ],
        compiler_params=params(53),
        cost_estimate=pl.CostEstimate(
            flops=2 * row_count * width * full,
            bytes_accessed=2 * full * (width + row_count),
            transcendentals=0,
        ),
    )(info, *rows, weights)


def halves(z_hi, size):
    return [pl.ds(pl.multiple_of(z * size, size), size) for z in (z_hi, 1 - z_hi)]


def chunk_copies(weights, z_hi, index, held, at, rows, sems):
    return [
        pltpu.make_async_copy(piece.at[index], held.at[at, rows, cut], sems.at[i])
        for i, (piece, cut) in enumerate(zip(weights, halves(z_hi, weights[0].shape[2])))
    ]


def heads_kernel(
    info, rows, here, far, here_x, far_x, out, lhs, held, total, lhs_sems, sems
):
    def copies_of(r, pair):
        every = pl.ds(0, held.shape[1])
        return [pltpu.make_async_copy(rows.at[r], lhs.at[r], lhs_sems.at[r])] + chunk_copies(
            pair, info[1], info[2 + r], held, r, every, sems.at[r]
        )

    def begin(r):
        for pick, pair in ((0, (here, far)), (1, (here_x, far_x))):

            @pl.when(info[0] == pick)
            def _():
                start_all(copies_of(r, pair))

    begin(0)
    begin(1)
    for r in range(NX):
        wait_all(copies_of(r, (here, far)))
        if r + 2 < NX:
            begin(r + 2)
        term = dot(lhs[r], held[r], NT)
        if r == 0:
            total[...] = term
        elif r < NX - 1:
            total[...] += term
        else:
            out[...] = (total[...] + term).astype(out.dtype)


def heads_product(info, rows, weights, dtype):
    row_count, depth = rows.shape[1:]
    width, full = weights[0].shape[1], NX * depth
    return pl.pallas_call(
        heads_kernel,
        out_shape=jax.ShapeDtypeStruct((row_count, width), dtype),
        in_specs=[smem()] + [anywhere()] * 5,
        out_specs=vmem(),
        scratch_shapes=[
            pltpu.VMEM((NX, row_count, depth), jnp.bfloat16),
            pltpu.VMEM((NX, width, depth), jnp.bfloat16),
            pltpu.VMEM((row_count, width), jnp.float32),
            pltpu.SemaphoreType.DMA((NX,)),
            pltpu.SemaphoreType.DMA((NX, 2)),
        ],
        compiler_params=params(53),
        cost_estimate=pl.CostEstimate(
            flops=2 * row_count * width * full,
            bytes_accessed=2 * full * (width + row_count),
            transcendentals=0,
        ),
    )(info, rows, *weights)


def mixed_kernel(
    info, own, theirs, here, far, here_x, far_x,
    out_0, out_1, out_2, out_3, lhs, held, ready, lhs_sems, sems, out_sems,
):
    depth = own.shape[1]
    lhs_copies = [
        pltpu.make_async_copy(piece, lhs.at[:, pl.ds(i * depth, depth)], lhs_sems.at[i])
        for i, piece in enumerate((own, theirs))
    ]
    mine, other = (here, far), (here_x, far_x)

    def copies_of(j, pairs):
        return [
            copy
            for side, pair in enumerate(pairs)
            for copy in chunk_copies(
                pair, info[1], info[2 + j], held, j, pl.ds(side * depth, depth), sems.at[j, side]
            )
        ]

    def begin(j):
        for pick, pairs in ((0, (mine, other)), (1, (other, mine))):

            @pl.when(info[0] == pick)
            def _():
                start_all(copies_of(j, pairs))

    outs = (out_0, out_1, out_2, out_3)
    done = [pltpu.make_async_copy(ready.at[j], outs[j], out_sems.at[j]) for j in range(NX)]
    begin(0)
    start_all(lhs_copies)
    wait_all(lhs_copies)
    begin(1)
    for j in range(NX):
        wait_all(copies_of(j, (mine, other)))
        if j + 2 < NX:
            begin(j + 2)
        ready[j] = low(dot(lhs[...], held[j]))
        done[j].start()
    wait_all(done)


def mixed_product(info, own, theirs, weights):
    row_count, depth = own.shape
    width = 2 * weights[0].shape[2]
    return pl.pallas_call(
        mixed_kernel,
        out_shape=[jax.ShapeDtypeStruct((row_count, width), jnp.bfloat16)] * NX,
        in_specs=[smem()] + [anywhere()] * 6,
        out_specs=[anywhere()] * NX,
        scratch_shapes=[
            pltpu.VMEM((row_count, 2 * depth), jnp.bfloat16),
            pltpu.VMEM((NX, 2 * depth, width), jnp.bfloat16),
            pltpu.VMEM((NX, row_count, width), jnp.bfloat16),
            pltpu.SemaphoreType.DMA((2,)),
            pltpu.SemaphoreType.DMA((NX, 2, 2)),
            pltpu.SemaphoreType.DMA((NX,)),
        ],
        compiler_params=params(53),
        cost_estimate=pl.CostEstimate(
            flops=4 * row_count * width * depth * NX,
            bytes_accessed=4 * NX * depth * width + 2 * row_count * (2 * depth + NX * width),
            transcendentals=0,
        ),
    )(info, own, theirs, *weights)


def wide(value):
    return value.astype(jnp.float32)


def low(value):
    return value.astype(jnp.bfloat16)


def query_kernel(count, info, q, weights, *refs):
    parts, outs = refs[:count], refs[count : count + NX]
    held, sems = refs[-2:]
    cuts = halves(info[1 + NX], weights.shape[2])
    copies = [
        [
            pltpu.make_async_copy(
                weights.at[2 * info[1 + j] + info[0], i, :, pl.ds(0, SPAN)],
                held.at[j, cut],
                sems.at[j, i],
            )
            for i, cut in enumerate(cuts)
        ]
        for j in range(NX)
    ]
    start_all(copies[0])
    start_all(copies[1])
    for j in range(NX):
        wait_all(copies[j])
        if j + 2 < NX:
            start_all(copies[j + 2])
        product = dot(q[...], held[j], NT)
        outs[j][...] = product + parts[j][...] if count else product


def query_product(info, q, weights, parts=()):
    row_count, width = q.shape[0], 2 * weights.shape[2]
    return pl.pallas_call(
        lambda *refs: query_kernel(len(parts), *refs),
        out_shape=[jax.ShapeDtypeStruct((row_count, width), jnp.float32)] * NX,
        in_specs=[smem(), vmem(), anywhere()] + [vmem()] * len(parts),
        out_specs=[vmem()] * NX,
        input_output_aliases={3 + j: j for j in range(len(parts))},
        scratch_shapes=[
            pltpu.VMEM((NX, width, SPAN), jnp.bfloat16),
            pltpu.SemaphoreType.DMA((NX, 2)),
        ],
        compiler_params=params(48),
        cost_estimate=pl.CostEstimate(
            flops=2 * row_count * width * SPAN * NX,
            bytes_accessed=2 * NX * SPAN * width + 4 * row_count * NX * width,
            transcendentals=0,
        ),
    )(info, q, weights, *parts)


def rest_kernel(info, *refs):
    parts = refs[:NX]
    kv, kv_back, kv_x, kv_back_x, weights = refs[NX : NX + 5]
    outs = refs[NX + 5 : 2 * NX + 5]
    lhs, held, ready, sems, out_sems = refs[2 * NX + 5 :]
    copies = [
        [
            pltpu.make_async_copy(
                weights.at[2 * info[1 + j] + (info[0] + side) % 2, i, :, pl.ds(SPAN, 2 * HS)],
                held.at[j, cut, pl.ds(side * 2 * HS, 2 * HS)],
                sems.at[j, side, i],
            )
            for side in range(2)
            for i, cut in enumerate(halves(info[1 + NX], weights.shape[2]))
        ]
        for j in range(NX)
    ]
    done = [pltpu.make_async_copy(ready.at[j], outs[j], out_sems.at[j]) for j in range(NX)]
    order = (2, 1, 3, 0)
    start_all(copies[order[0]])
    start_all(copies[order[1]])
    lhs[:, : 2 * HS] = low(kv[...] + wide(kv_back[...]))
    lhs[:, 2 * HS :] = low(wide(kv_x[...]) + wide(kv_back_x[...]))
    for i, j in enumerate(order):
        wait_all(copies[j])
        if i + 2 < NX:
            start_all(copies[order[i + 2]])
        ready[j] = low(parts[j][...] + dot(lhs[...], held[j], NT))
        done[j].start()
    wait_all(done)


def rest_product(info, parts, operands, weights):
    row_count, width = parts[0].shape
    return pl.pallas_call(
        rest_kernel,
        out_shape=[jax.ShapeDtypeStruct((row_count, width), jnp.bfloat16)] * NX,
        in_specs=[smem()] + [vmem()] * (NX + 4) + [anywhere()],
        out_specs=[anywhere()] * NX,
        scratch_shapes=[
            pltpu.VMEM((row_count, 4 * HS), jnp.bfloat16),
            pltpu.VMEM((NX, width, 4 * HS), jnp.bfloat16),
            pltpu.VMEM((NX, row_count, width), jnp.bfloat16),
            pltpu.SemaphoreType.DMA((NX, 2, 2)),
            pltpu.SemaphoreType.DMA((NX,)),
        ],
        compiler_params=params(48),
        cost_estimate=pl.CostEstimate(
            flops=8 * row_count * width * HS * NX,
            bytes_accessed=8 * NX * HS * width + 6 * row_count * NX * width,
            transcendentals=0,
        ),
    )(info, *parts, *operands, weights)


SCALING = 1.0 / math.sqrt(HS)
SPAN = GROUP * HS


def forward_kernel(
    keep_q, came_q, keep_kv, came_kv, prev_a, prev_b, mask, head_out, logs, queries, kv
):
    rows = keep_q.shape[0]
    queries[...] = low(keep_q[...] + wide(came_q[...]))
    kv[:rows] = low(wide(prev_a[...]) + wide(prev_b[...]))
    kv[rows:] = low(keep_kv[...] + wide(came_kv[...]))
    keys, turned = kv[:, :HS], kv[:, HS:].T

    @pl.loop(0, GROUP, unroll=GROUP)
    def _(h):
        lanes = pl.ds(pl.multiple_of(h * HS, HS), HS)
        scores = dot(keys, queries[:, lanes], NT) * SCALING
        scores = jnp.where(mask[...] > 0, scores, -1e30)
        highest = jnp.max(scores, axis=0, keepdims=True)
        raised = jnp.exp(scores - highest)
        inverse = 1.0 / jnp.sum(raised, axis=0, keepdims=True)
        logs[h, 0:1] = highest
        logs[h, 1:2] = inverse
        head_out[:, lanes] = low(dot(turned, low(raised * inverse)).T)


def backward_kernel(
    queries, kv, mask, head_out, logs, keep_grad, came_grad,
    dq, dkv_prev, dkv_own, dkv_low, dk, dv, grad_heads,
):
    rows = queries.shape[0]
    grad_heads[...] = low(keep_grad[...] + wide(came_grad[...]))
    keys, values = kv[:, :HS], kv[:, HS:]
    turned = keys.T
    dk[...] = jnp.zeros_like(dk)
    dv[...] = jnp.zeros_like(dv)

    @pl.loop(0, GROUP, unroll=GROUP)
    def _(h):
        lanes = pl.ds(pl.multiple_of(h * HS, HS), HS)
        query, grad = queries[:, lanes], grad_heads[:, lanes]
        scores = dot(keys, query, NT) * SCALING
        scores = jnp.where(mask[...] > 0, scores, -1e30)
        probability = jnp.exp(scores - logs[h, 0:1]) * logs[h, 1:2]
        delta = jnp.sum((wide(grad) * wide(head_out[:, lanes])).T, axis=0, keepdims=True)
        score_grad = low(probability * (dot(values, grad, NT) - delta))
        dv[...] += dot(low(probability), grad)
        dk[...] += dot(score_grad, query)
        dq[:, lanes] = low((dot(turned, score_grad) * SCALING).T)

    dkv_prev[:, :HS] = low(dk[:rows] * SCALING)
    dkv_prev[:, HS:] = low(dv[:rows])
    dkv_own[:, :HS] = dk[rows:] * SCALING
    dkv_own[:, HS:] = dv[rows:]
    dkv_low[...] = low(dkv_own[...])


def attend(keep_q, came_q, keep_kv, came_kv, prev_a, prev_b, mask):
    rows = keep_q.shape[0]
    return pl.pallas_call(
        forward_kernel,
        out_shape=(
            jax.ShapeDtypeStruct((rows, SPAN), jnp.bfloat16),
            jax.ShapeDtypeStruct((GROUP, 8, rows), jnp.float32),
            jax.ShapeDtypeStruct((rows, SPAN), jnp.bfloat16),
            jax.ShapeDtypeStruct((2 * rows, 2 * HS), jnp.bfloat16),
        ),
        in_specs=[vmem()] * 7,
        out_specs=(vmem(),) * 4,
        compiler_params=params(),
        cost_estimate=pl.CostEstimate(
            flops=8 * rows * rows * HS * GROUP * 2, bytes_accessed=4 * MB,
            transcendentals=2 * rows * rows * GROUP,
        ),
    )(keep_q, came_q, keep_kv, came_kv, prev_a, prev_b, mask)


def attend_back(queries, kv, mask, head_out, logs, keep_grad, came_grad):
    rows = queries.shape[0]
    return pl.pallas_call(
        backward_kernel,
        out_shape=(
            jax.ShapeDtypeStruct((rows, SPAN), jnp.bfloat16),
            jax.ShapeDtypeStruct((rows, 2 * HS), jnp.bfloat16),
            jax.ShapeDtypeStruct((rows, 2 * HS), jnp.float32),
            jax.ShapeDtypeStruct((rows, 2 * HS), jnp.bfloat16),
        ),
        in_specs=[vmem()] * 7,
        out_specs=(vmem(),) * 4,
        scratch_shapes=[pltpu.VMEM((2 * rows, HS), jnp.float32)] * 2
        + [pltpu.VMEM((rows, SPAN), jnp.bfloat16)],
        compiler_params=params(),
        cost_estimate=pl.CostEstimate(
            flops=20 * rows * rows * HS * GROUP * 2, bytes_accessed=5 * MB,
            transcendentals=2 * rows * rows * GROUP,
        ),
    )(queries, kv, mask, head_out, logs, keep_grad, came_grad)


def pick_blocks(array, wanted):
    blocks = array.reshape(-1, BLK, array.shape[1])
    return jnp.where(
        (wanted >= 0)[:, None, None],
        blocks[jnp.maximum(wanted, 0)],
        jnp.zeros((), jnp.bfloat16),
    )


def sources(landing, block_count):
    return (
        jnp.zeros((block_count,), jnp.int32)
        .at[jnp.where(landing >= 0, landing, block_count)]
        .set(jnp.arange(landing.shape[0], dtype=jnp.int32), mode="drop")
    )


def body(activations, qkv_weight, out_weight, grad_out, segments, send_list, recv_list):
    row_count, shard_width = activations.shape
    dp_index = lax.axis_index("dp")
    seq_index = lax.axis_index("seq")
    tensor_index = lax.axis_index("tensor")
    y_index, core = dp_index // 2, dp_index % 2
    x_index, z_lo = tensor_index // 2, tensor_index % 2
    straight = core == z_lo

    block_count = row_count // BLK
    send_slots, recv_slots = send_list[0], recv_list[0]
    in_own, out_own = qkv_weight[:, 0, :], out_weight[0]

    grad_x = lax.all_gather(
        grad_out, "tensor", axis=0, tiled=False, axis_index_groups=X_GROUPS
    )
    out_own = out_own[None]
    in_near, in_far, out_up, out_down, near_own, far_own, arrived = fence(
        [
            z_near(in_own),
            z_far(in_own),
            along_y(out_own, 1),
            along_y(out_own, -1),
            z_near(out_own),
            z_far(out_own),
            route_blocks(pick_blocks(activations, send_slots)),
        ],
        [grad_x],
    )

    in_pair = jnp.stack([jnp.where(straight, in_own, in_near), in_far])
    in_all = lax.all_gather(in_pair, "dp", axis=0, tiled=False)
    moved = arrived[sources(recv_slots, block_count)].reshape(row_count, shard_width)
    out_two = jnp.concatenate([out_up, out_down], axis=0)
    half = out_own.shape[1] // 2
    first, second = fence([along_y(out_up[:, :half], 1), along_y(out_down[:, half:], -1)])
    out_one = jnp.concatenate([first, second], axis=1)
    near_two, far_two, near_one, far_one, *moved_x = fence(
        [z_near(out_two), z_far(out_two), z_near(out_one), z_far(out_one)]
        + [along_x(moved, distance) for distance in OFFSETS[1:]]
    )
    moved_x = [moved, *moved_x]

    out_here = jnp.where(
        straight,
        jnp.concatenate([out_own, out_two, out_one], axis=0),
        jnp.concatenate([near_own, near_two, near_one], axis=0),
    )
    out_far = jnp.concatenate([far_own, far_two, far_one], axis=0)
    out_all = [out_here, out_far, over_cores(out_here), over_cores(out_far)]

    places = (x_index + jnp.array(OFFSETS, jnp.int32)) % NX
    order = jnp.array(POSITION, jnp.int32)[(jnp.arange(NX) - y_index) % NY]
    give_info = jnp.concatenate([jnp.stack([straight, seq_index]), order]).astype(jnp.int32)
    keep_info = jnp.concatenate([jnp.stack([~straight, seq_index]), order]).astype(jnp.int32)
    give_grad = heads_product(give_info, grad_x, out_all, jnp.bfloat16)
    (places,) = fence([places], [give_grad])

    def in_info(head, columns):
        return jnp.concatenate([head[None], columns, seq_index[None]]).astype(jnp.int32)

    give_kv, give_q = proj_product(in_info(1 - z_lo, places), moved_x, in_all, jnp.bfloat16)
    keep_kv, keep_q = proj_product(in_info(z_lo, places), moved_x, in_all, jnp.float32)
    keep_grad = heads_product(keep_info, grad_x, out_all, jnp.float32)

    (late_kv,) = fence([give_kv], [keep_kv])
    prev_a = send(
        late_kv, lambda x, y, zh, zl, c: (x, y, 1, 1 - zl, c) if zh == 0 else None
    )
    prev_b = send(
        low(keep_kv), lambda x, y, zh, zl, c: (x, y, 1, zl, c) if zh == 0 else None
    )
    query_ids = lax.dynamic_slice_in_dim(segments, seq_index * row_count, row_count)
    padded_ids = jnp.concatenate([jnp.full((row_count,), -1, jnp.int32), segments])
    key_ids = lax.dynamic_slice_in_dim(padded_ids, seq_index * row_count, 2 * row_count)
    positions = jnp.arange(2 * row_count)
    mask = (
        (query_ids[None, :] == key_ids[:, None])
        & (positions[:, None] <= positions[None, :row_count] + row_count)
    ).astype(jnp.float32)
    head_out, logs, queries, kv = attend(
        keep_q, over_z_lo(give_q), keep_kv, over_z_lo(give_kv), prev_a, prev_b, mask
    )
    grad_queries, dkv_prev, dkv_own, dkv_low = attend_back(
        queries, kv, mask, head_out, logs, keep_grad, over_z_lo(give_grad)
    )
    targets = (x_index + jnp.arange(NX)) % NX
    grad_queries_x = over_z_lo(grad_queries)
    back = send(
        dkv_prev, lambda x, y, zh, zl, c: (x, y, 0, zl, c) if zh == 1 else None
    )
    back_x = send(
        dkv_prev, lambda x, y, zh, zl, c: (x, y, 0, 1 - zl, c) if zh == 1 else None
    )
    totals = query_product(in_info(z_lo, targets), grad_queries, in_all)
    totals = query_product(in_info(1 - z_lo, targets), grad_queries_x, in_all, totals)
    here, up, across, down = rest_product(
        in_info(z_lo, targets), totals, [dkv_own, back, over_z_lo(dkv_low), back_x], in_all
    )

    half = row_count // 2
    from_below = along_x(across[:half], -1)
    from_above = along_x(across[half:], 1)

    up = jnp.concatenate(
        [(wide(up[:half]) + wide(from_below)).astype(jnp.bfloat16), up[half:]], axis=0
    )
    down = jnp.concatenate(
        [down[:half], (wide(down[half:]) + wide(from_above)).astype(jnp.bfloat16)], axis=0
    )
    up, down = along_x(up, -1), along_x(down, 1)
    grad_moved = (wide(here) + wide(up) + wide(down)).astype(jnp.bfloat16)

    (heads,) = fence([head_out], [grad_queries_x])
    order = jnp.array(POSITION, jnp.int32)[(targets - y_index) % NY]
    mixed_info = jnp.concatenate([keep_info[:2], order])
    own_part, *others = mixed_product(mixed_info, heads, over_z_lo(heads), out_all)
    others = fence(others, [up, down])
    attended = wide(own_part)
    for part, distance in zip(others, (-1, 2, 1)):
        attended += wide(along_x(part, distance))
    attended = low(attended)

    returned = route_blocks(pick_blocks(grad_moved, recv_slots))
    grad_in = returned[sources(send_slots, block_count)]
    return (attended, grad_in.reshape(row_count, shard_width))


def solution(mesh):
    placed = (
        P(("dp", "seq"), "tensor"),
        P(("dp", "seq"), "tensor", None),
        P("tensor", None, ("dp", "seq")),
        P(("dp", "seq"), "tensor"),
        P("dp"),
        P(("dp", "seq"), None),
        P(("dp", "seq"), None),
    )
    return jax.shard_map(
        body,
        mesh=mesh,
        in_specs=placed,
        out_specs=(P(("dp", "seq"), "tensor"), P(("dp", "seq"), "tensor")),
        check_vma=False,
    )
```

```python
import math

import jax
import jax.numpy as jnp
from jax import lax
from jax.experimental import pallas as pl
from jax.experimental.pallas import tpu as pltpu
from jax.sharding import PartitionSpec as P

HS = 128
GROUP = 6
BLK = 32
AXES = ("dp", "seq", "tensor")
NX, NY, NZ = 4, 4, 4
X_GROUPS = [[0, 2, 4, 6], [1, 3, 5, 7]]


def place(index):
    dp, seq, tensor = index // 16, index // 8 % 2, index % 8
    return tensor // 2, dp // 2, seq, tensor % 2, dp % 2


def index_of(x, y, z_hi, z_lo, core):
    return (y % NY * 2 + core) * 16 + z_hi * 8 + x % NX * 2 + z_lo


def send(block, target):
    pairs = []
    for source in range(128):
        goal = target(*place(source))
        if goal is not None:
            pairs.append((source, index_of(*goal)))
    return lax.ppermute(block, AXES, pairs)


def along_y(block, distance):
    return send(block, lambda x, y, zh, zl, c: (x, y - distance, zh, zl, c))


def over_cores(block):
    return send(block, lambda x, y, zh, zl, c: (x, y, zh, zl, 1 - c))


def over_z_lo(block):
    return send(block, lambda x, y, zh, zl, c: (x, y, zh, 1 - zl, c))


def z_near(block):
    return send(
        block, lambda x, y, zh, zl, c: (x, y, zh, 1 - zl, 1 - c) if zl != c else None
    )


def z_far(block):
    return send(
        block,
        lambda x, y, zh, zl, c: (x, y, 1 - zh, zl, c)
        if zl == c
        else (x, y, 1 - zh, 1 - zl, 1 - c),
    )


def along_x(block, distance):
    return send(block, lambda x, y, zh, zl, c: (x - distance, y, zh, zl, c))


def route_blocks(buffer):
    return lax.all_to_all(buffer, ("dp", "seq"), split_axis=0, concat_axis=0, tiled=True)


def nothing(*refs):
    pass


def fence(values, after=()):
    return pl.pallas_call(
        nothing,
        out_shape=[jax.ShapeDtypeStruct(v.shape, v.dtype) for v in values],
        in_specs=[anywhere()] * (len(values) + len(after)),
        out_specs=[anywhere()] * len(values),
        input_output_aliases={i: i for i in range(len(values))},
        cost_estimate=pl.CostEstimate(flops=0, bytes_accessed=0, transcendentals=0),
    )(*values, *after)


def dot(a, b, contract=((1,), (0,))):
    return lax.dot_general(a, b, (contract, ((), ())), preferred_element_type=jnp.float32)


NT = ((1,), (1,))
NN = ((1,), (0,))
MB = 1 << 20
OFFSETS = (0, 1, -1, 2)
POSITION = (0, 1, 3, 2)


def vmem():
    return pl.BlockSpec(memory_space=pltpu.VMEM)


def smem():
    return pl.BlockSpec(memory_space=pltpu.SMEM)


def anywhere():
    return pl.BlockSpec(memory_space=pl.ANY)


def params(size=24):
    return pltpu.CompilerParams(vmem_limit_bytes=size * MB)


def start_all(copies):
    for copy in copies:
        copy.start()


def wait_all(copies):
    for copy in copies:
        copy.wait()


def proj_kernel(info, *refs):
    rows, weights, out_kv, out_q = refs[:NX], refs[NX], refs[NX + 1], refs[NX + 2]
    lhs, held, total, lhs_sems, sems = refs[NX + 3 :]
    cuts = halves(info[1 + NX], weights.shape[2])
    copies = [
        [pltpu.make_async_copy(rows[r], lhs.at[r], lhs_sems.at[r])]
        + [
            pltpu.make_async_copy(
                weights.at[2 * info[1 + r] + info[0], i], held.at[r, cut], sems.at[r, i]
            )
            for i, cut in enumerate(cuts)
        ]
        for r in range(NX)
    ]
    start_all(copies[0])
    start_all(copies[1])
    for r in range(NX):
        wait_all(copies[r])
        if r + 2 < NX:
            start_all(copies[r + 2])
        term = dot(lhs[r], held[r])
        if r == 0:
            total[...] = term
        elif r < NX - 1:
            total[...] += term
        else:
            term = (total[...] + term).astype(out_q.dtype)
            out_q[...] = term[:, :SPAN]
            out_kv[...] = term[:, SPAN:]


def proj_product(info, rows, weights, dtype):
    row_count, depth = rows[0].shape
    width, full = weights.shape[3], NX * depth
    return pl.pallas_call(
        proj_kernel,
        out_shape=(
            jax.ShapeDtypeStruct((row_count, 2 * HS), dtype),
            jax.ShapeDtypeStruct((row_count, SPAN), dtype),
        ),
        in_specs=[smem()] + [anywhere()] * (NX + 1),
        out_specs=(vmem(), vmem()),
        scratch_shapes=[
            pltpu.VMEM((NX, row_count, depth), jnp.bfloat16),
            pltpu.VMEM((NX, depth, width), jnp.bfloat16),
            pltpu.VMEM((row_count, width), jnp.float32),
            pltpu.SemaphoreType.DMA((NX,)),
            pltpu.SemaphoreType.DMA((NX, 2)),
        ],
        compiler_params=params(53),
        cost_estimate=pl.CostEstimate(
            flops=2 * row_count * width * full,
            bytes_accessed=2 * full * (width + row_count),
            transcendentals=0,
        ),
    )(info, *rows, weights)


def halves(z_hi, size):
    return [pl.ds(pl.multiple_of(z * size, size), size) for z in (z_hi, 1 - z_hi)]


def chunk_copies(weights, z_hi, index, held, at, rows, sems):
    return [
        pltpu.make_async_copy(piece.at[index], held.at[at, rows, cut], sems.at[i])
        for i, (piece, cut) in enumerate(zip(weights, halves(z_hi, weights[0].shape[2])))
    ]


def heads_kernel(
    info, rows, here, far, here_x, far_x, out, lhs, held, total, lhs_sems, sems
):
    def copies_of(r, pair):
        every = pl.ds(0, held.shape[1])
        return [pltpu.make_async_copy(rows.at[r], lhs.at[r], lhs_sems.at[r])] + chunk_copies(
            pair, info[1], info[2 + r], held, r, every, sems.at[r]
        )

    def begin(r):
        for pick, pair in ((0, (here, far)), (1, (here_x, far_x))):

            @pl.when(info[0] == pick)
            def _():
                start_all(copies_of(r, pair))

    begin(0)
    begin(1)
    for r in range(NX):
        wait_all(copies_of(r, (here, far)))
        if r + 2 < NX:
            begin(r + 2)
        term = dot(lhs[r], held[r], NT)
        if r == 0:
            total[...] = term
        elif r < NX - 1:
            total[...] += term
        else:
            out[...] = (total[...] + term).astype(out.dtype)


def heads_product(info, rows, weights, dtype):
    row_count, depth = rows.shape[1:]
    width, full = weights[0].shape[1], NX * depth
    return pl.pallas_call(
        heads_kernel,
        out_shape=jax.ShapeDtypeStruct((row_count, width), dtype),
        in_specs=[smem()] + [anywhere()] * 5,
        out_specs=vmem(),
        scratch_shapes=[
            pltpu.VMEM((NX, row_count, depth), jnp.bfloat16),
            pltpu.VMEM((NX, width, depth), jnp.bfloat16),
            pltpu.VMEM((row_count, width), jnp.float32),
            pltpu.SemaphoreType.DMA((NX,)),
            pltpu.SemaphoreType.DMA((NX, 2)),
        ],
        compiler_params=params(53),
        cost_estimate=pl.CostEstimate(
            flops=2 * row_count * width * full,
            bytes_accessed=2 * full * (width + row_count),
            transcendentals=0,
        ),
    )(info, rows, *weights)


def mixed_kernel(
    info, own, theirs, here, far, here_x, far_x,
    out_0, out_1, out_2, out_3, lhs, held, ready, lhs_sems, sems, out_sems,
):
    depth = own.shape[1]
    lhs_copies = [
        pltpu.make_async_copy(piece, lhs.at[:, pl.ds(i * depth, depth)], lhs_sems.at[i])
        for i, piece in enumerate((own, theirs))
    ]
    mine, other = (here, far), (here_x, far_x)

    def copies_of(j, pairs):
        return [
            copy
            for side, pair in enumerate(pairs)
            for copy in chunk_copies(
                pair, info[1], info[2 + j], held, j, pl.ds(side * depth, depth), sems.at[j, side]
            )
        ]

    def begin(j):
        for pick, pairs in ((0, (mine, other)), (1, (other, mine))):

            @pl.when(info[0] == pick)
            def _():
                start_all(copies_of(j, pairs))

    outs = (out_0, out_1, out_2, out_3)
    done = [pltpu.make_async_copy(ready.at[j], outs[j], out_sems.at[j]) for j in range(NX)]
    begin(0)
    start_all(lhs_copies)
    wait_all(lhs_copies)
    begin(1)
    for j in range(NX):
        wait_all(copies_of(j, (mine, other)))
        if j + 2 < NX:
            begin(j + 2)
        ready[j] = low(dot(lhs[...], held[j]))
        done[j].start()
    wait_all(done)


def mixed_product(info, own, theirs, weights):
    row_count, depth = own.shape
    width = 2 * weights[0].shape[2]
    return pl.pallas_call(
        mixed_kernel,
        out_shape=[jax.ShapeDtypeStruct((row_count, width), jnp.bfloat16)] * NX,
        in_specs=[smem()] + [anywhere()] * 6,
        out_specs=[anywhere()] * NX,
        scratch_shapes=[
            pltpu.VMEM((row_count, 2 * depth), jnp.bfloat16),
            pltpu.VMEM((NX, 2 * depth, width), jnp.bfloat16),
            pltpu.VMEM((NX, row_count, width), jnp.bfloat16),
            pltpu.SemaphoreType.DMA((2,)),
            pltpu.SemaphoreType.DMA((NX, 2, 2)),
            pltpu.SemaphoreType.DMA((NX,)),
        ],
        compiler_params=params(53),
        cost_estimate=pl.CostEstimate(
            flops=4 * row_count * width * depth * NX,
            bytes_accessed=4 * NX * depth * width + 2 * row_count * (2 * depth + NX * width),
            transcendentals=0,
        ),
    )(info, own, theirs, *weights)


def wide(value):
    return value.astype(jnp.float32)


def low(value):
    return value.astype(jnp.bfloat16)


def query_kernel(count, info, q, weights, *refs):
    parts, outs = refs[:count], refs[count : count + NX]
    held, sems = refs[-2:]
    cuts = halves(info[1 + NX], weights.shape[2])
    copies = [
        [
            pltpu.make_async_copy(
                weights.at[2 * info[1 + j] + info[0], i, :, pl.ds(0, SPAN)],
                held.at[j, cut],
                sems.at[j, i],
            )
            for i, cut in enumerate(cuts)
        ]
        for j in range(NX)
    ]
    start_all(copies[0])
    start_all(copies[1])
    for j in range(NX):
        wait_all(copies[j])
        if j + 2 < NX:
            start_all(copies[j + 2])
        product = dot(q[...], held[j], NT)
        outs[j][...] = product + parts[j][...] if count else product


def query_product(info, q, weights, parts=()):
    row_count, width = q.shape[0], 2 * weights.shape[2]
    return pl.pallas_call(
        lambda *refs: query_kernel(len(parts), *refs),
        out_shape=[jax.ShapeDtypeStruct((row_count, width), jnp.float32)] * NX,
        in_specs=[smem(), vmem(), anywhere()] + [vmem()] * len(parts),
        out_specs=[vmem()] * NX,
        input_output_aliases={3 + j: j for j in range(len(parts))},
        scratch_shapes=[
            pltpu.VMEM((NX, width, SPAN), jnp.bfloat16),
            pltpu.SemaphoreType.DMA((NX, 2)),
        ],
        compiler_params=params(48),
        cost_estimate=pl.CostEstimate(
            flops=2 * row_count * width * SPAN * NX,
            bytes_accessed=2 * NX * SPAN * width + 4 * row_count * NX * width,
            transcendentals=0,
        ),
    )(info, q, weights, *parts)


def rest_kernel(info, *refs):
    parts = refs[:NX]
    kv, kv_back, kv_x, kv_back_x, weights = refs[NX : NX + 5]
    outs = refs[NX + 5 : 2 * NX + 5]
    lhs, held, ready, sems, out_sems = refs[2 * NX + 5 :]
    copies = [
        [
            pltpu.make_async_copy(
                weights.at[2 * info[1 + j] + (info[0] + side) % 2, i, :, pl.ds(SPAN, 2 * HS)],
                held.at[j, cut, pl.ds(side * 2 * HS, 2 * HS)],
                sems.at[j, side, i],
            )
            for side in range(2)
            for i, cut in enumerate(halves(info[1 + NX], weights.shape[2]))
        ]
        for j in range(NX)
    ]
    done = [pltpu.make_async_copy(ready.at[j], outs[j], out_sems.at[j]) for j in range(NX)]
    order = (2, 1, 3, 0)
    start_all(copies[order[0]])
    start_all(copies[order[1]])
    lhs[:, : 2 * HS] = low(kv[...] + wide(kv_back[...]))
    lhs[:, 2 * HS :] = low(wide(kv_x[...]) + wide(kv_back_x[...]))
    for i, j in enumerate(order):
        wait_all(copies[j])
        if i + 2 < NX:
            start_all(copies[order[i + 2]])
        ready[j] = low(parts[j][...] + dot(lhs[...], held[j], NT))
        done[j].start()
    wait_all(done)


def rest_product(info, parts, operands, weights):
    row_count, width = parts[0].shape
    return pl.pallas_call(
        rest_kernel,
        out_shape=[jax.ShapeDtypeStruct((row_count, width), jnp.bfloat16)] * NX,
        in_specs=[smem()] + [vmem()] * (NX + 4) + [anywhere()],
        out_specs=[anywhere()] * NX,
        scratch_shapes=[
            pltpu.VMEM((row_count, 4 * HS), jnp.bfloat16),
            pltpu.VMEM((NX, width, 4 * HS), jnp.bfloat16),
            pltpu.VMEM((NX, row_count, width), jnp.bfloat16),
            pltpu.SemaphoreType.DMA((NX, 2, 2)),
            pltpu.SemaphoreType.DMA((NX,)),
        ],
        compiler_params=params(48),
        cost_estimate=pl.CostEstimate(
            flops=8 * row_count * width * HS * NX,
            bytes_accessed=8 * NX * HS * width + 6 * row_count * NX * width,
            transcendentals=0,
        ),
    )(info, *parts, *operands, weights)


SCALING = 1.0 / math.sqrt(HS)
SPAN = GROUP * HS


def forward_kernel(
    keep_q, came_q, keep_kv, came_kv, prev_a, prev_b, mask, head_out, logs, queries, kv
):
    rows = keep_q.shape[0]
    queries[...] = low(keep_q[...] + wide(came_q[...]))
    kv[:rows] = low(wide(prev_a[...]) + wide(prev_b[...]))
    kv[rows:] = low(keep_kv[...] + wide(came_kv[...]))
    keys, turned = kv[:, :HS], kv[:, HS:].T

    @pl.loop(0, GROUP, unroll=GROUP)
    def _(h):
        lanes = pl.ds(pl.multiple_of(h * HS, HS), HS)
        scores = dot(keys, queries[:, lanes], NT) * SCALING
        scores = jnp.where(mask[...] > 0, scores, -1e30)
        highest = jnp.max(scores, axis=0, keepdims=True)
        raised = jnp.exp(scores - highest)
        inverse = 1.0 / jnp.sum(raised, axis=0, keepdims=True)
        logs[h, 0:1] = highest
        logs[h, 1:2] = inverse
        head_out[:, lanes] = low(dot(turned, low(raised * inverse)).T)


def backward_kernel(
    queries, kv, mask, head_out, logs, keep_grad, came_grad,
    dq, dkv_prev, dkv_own, dkv_low, dk, dv, grad_heads,
):
    rows = queries.shape[0]
    grad_heads[...] = low(keep_grad[...] + wide(came_grad[...]))
    keys, values = kv[:, :HS], kv[:, HS:]
    turned = keys.T
    dk[...] = jnp.zeros_like(dk)
    dv[...] = jnp.zeros_like(dv)

    @pl.loop(0, GROUP, unroll=GROUP)
    def _(h):
        lanes = pl.ds(pl.multiple_of(h * HS, HS), HS)
        query, grad = queries[:, lanes], grad_heads[:, lanes]
        scores = dot(keys, query, NT) * SCALING
        scores = jnp.where(mask[...] > 0, scores, -1e30)
        probability = jnp.exp(scores - logs[h, 0:1]) * logs[h, 1:2]
        delta = jnp.sum((wide(grad) * wide(head_out[:, lanes])).T, axis=0, keepdims=True)
        score_grad = low(probability * (dot(values, grad, NT) - delta))
        dv[...] += dot(low(probability), grad)
        dk[...] += dot(score_grad, query)
        dq[:, lanes] = low((dot(turned, score_grad) * SCALING).T)

    dkv_prev[:, :HS] = low(dk[:rows] * SCALING)
    dkv_prev[:, HS:] = low(dv[:rows])
    dkv_own[:, :HS] = dk[rows:] * SCALING
    dkv_own[:, HS:] = dv[rows:]
    dkv_low[...] = low(dkv_own[...])


def attend(keep_q, came_q, keep_kv, came_kv, prev_a, prev_b, mask):
    rows = keep_q.shape[0]
    return pl.pallas_call(
        forward_kernel,
        out_shape=(
            jax.ShapeDtypeStruct((rows, SPAN), jnp.bfloat16),
            jax.ShapeDtypeStruct((GROUP, 8, rows), jnp.float32),
            jax.ShapeDtypeStruct((rows, SPAN), jnp.bfloat16),
            jax.ShapeDtypeStruct((2 * rows, 2 * HS), jnp.bfloat16),
        ),
        in_specs=[vmem()] * 7,
        out_specs=(vmem(),) * 4,
        compiler_params=params(),
        cost_estimate=pl.CostEstimate(
            flops=8 * rows * rows * HS * GROUP * 2, bytes_accessed=4 * MB,
            transcendentals=2 * rows * rows * GROUP,
        ),
    )(keep_q, came_q, keep_kv, came_kv, prev_a, prev_b, mask)


def attend_back(queries, kv, mask, head_out, logs, keep_grad, came_grad):
    rows = queries.shape[0]
    return pl.pallas_call(
        backward_kernel,
        out_shape=(
            jax.ShapeDtypeStruct((rows, SPAN), jnp.bfloat16),
            jax.ShapeDtypeStruct((rows, 2 * HS), jnp.bfloat16),
            jax.ShapeDtypeStruct((rows, 2 * HS), jnp.float32),
            jax.ShapeDtypeStruct((rows, 2 * HS), jnp.bfloat16),
        ),
        in_specs=[vmem()] * 7,
        out_specs=(vmem(),) * 4,
        scratch_shapes=[pltpu.VMEM((2 * rows, HS), jnp.float32)] * 2
        + [pltpu.VMEM((rows, SPAN), jnp.bfloat16)],
        compiler_params=params(),
        cost_estimate=pl.CostEstimate(
            flops=20 * rows * rows * HS * GROUP * 2, bytes_accessed=5 * MB,
            transcendentals=2 * rows * rows * GROUP,
        ),
    )(queries, kv, mask, head_out, logs, keep_grad, came_grad)


def pick_blocks(array, wanted):
    blocks = array.reshape(-1, BLK, array.shape[1])
    return jnp.where(
        (wanted >= 0)[:, None, None],
        blocks[jnp.maximum(wanted, 0)],
        jnp.zeros((), jnp.bfloat16),
    )


def sources(landing, block_count):
    return (
        jnp.zeros((block_count,), jnp.int32)
        .at[jnp.where(landing >= 0, landing, block_count)]
        .set(jnp.arange(landing.shape[0], dtype=jnp.int32), mode="drop")
    )


def body(activations, qkv_weight, out_weight, grad_out, segments, send_list, recv_list):
    row_count, shard_width = activations.shape
    dp_index = lax.axis_index("dp")
    seq_index = lax.axis_index("seq")
    tensor_index = lax.axis_index("tensor")
    y_index, core = dp_index // 2, dp_index % 2
    x_index, z_lo = tensor_index // 2, tensor_index % 2
    straight = core == z_lo

    block_count = row_count // BLK
    send_slots, recv_slots = send_list[0], recv_list[0]
    in_own, out_own = qkv_weight[:, 0, :], out_weight[0]

    grad_x = lax.all_gather(
        grad_out, "tensor", axis=0, tiled=False, axis_index_groups=X_GROUPS
    )
    out_own = out_own[None]
    in_near, in_far, out_up, out_down, near_own, far_own, arrived = fence(
        [
            z_near(in_own),
            z_far(in_own),
            along_y(out_own, 1),
            along_y(out_own, -1),
            z_near(out_own),
            z_far(out_own),
            route_blocks(pick_blocks(activations, send_slots)),
        ],
        [grad_x],
    )

    in_pair = jnp.stack([jnp.where(straight, in_own, in_near), in_far])
    in_all = lax.all_gather(in_pair, "dp", axis=0, tiled=False)
    moved = arrived[sources(recv_slots, block_count)].reshape(row_count, shard_width)
    out_two = jnp.concatenate([out_up, out_down], axis=0)
    half = out_own.shape[1] // 2
    first, second = fence([along_y(out_up[:, :half], 1), along_y(out_down[:, half:], -1)])
    out_one = jnp.concatenate([first, second], axis=1)
    near_two, far_two, near_one, far_one, *moved_x = fence(
        [z_near(out_two), z_far(out_two), z_near(out_one), z_far(out_one)]
        + [along_x(moved, distance) for distance in OFFSETS[1:]]
    )
    moved_x = [moved, *moved_x]

    out_here = jnp.where(
        straight,
        jnp.concatenate([out_own, out_two, out_one], axis=0),
        jnp.concatenate([near_own, near_two, near_one], axis=0),
    )
    out_far = jnp.concatenate([far_own, far_two, far_one], axis=0)
    out_all = [out_here, out_far, over_cores(out_here), over_cores(out_far)]

    places = (x_index + jnp.array(OFFSETS, jnp.int32)) % NX
    order = jnp.array(POSITION, jnp.int32)[(jnp.arange(NX) - y_index) % NY]
    give_info = jnp.concatenate([jnp.stack([straight, seq_index]), order]).astype(jnp.int32)
    keep_info = jnp.concatenate([jnp.stack([~straight, seq_index]), order]).astype(jnp.int32)
    give_grad = heads_product(give_info, grad_x, out_all, jnp.bfloat16)
    (places,) = fence([places], [give_grad])

    def in_info(head, columns):
        return jnp.concatenate([head[None], columns, seq_index[None]]).astype(jnp.int32)

    give_kv, give_q = proj_product(in_info(1 - z_lo, places), moved_x, in_all, jnp.bfloat16)
    keep_kv, keep_q = proj_product(in_info(z_lo, places), moved_x, in_all, jnp.float32)
    keep_grad = heads_product(keep_info, grad_x, out_all, jnp.float32)

    (late_kv,) = fence([give_kv], [keep_kv])
    prev_a = send(
        late_kv, lambda x, y, zh, zl, c: (x, y, 1, 1 - zl, c) if zh == 0 else None
    )
    prev_b = send(
        low(keep_kv), lambda x, y, zh, zl, c: (x, y, 1, zl, c) if zh == 0 else None
    )
    query_ids = lax.dynamic_slice_in_dim(segments, seq_index * row_count, row_count)
    padded_ids = jnp.concatenate([jnp.full((row_count,), -1, jnp.int32), segments])
    key_ids = lax.dynamic_slice_in_dim(padded_ids, seq_index * row_count, 2 * row_count)
    positions = jnp.arange(2 * row_count)
    mask = (
        (query_ids[None, :] == key_ids[:, None])
        & (positions[:, None] <= positions[None, :row_count] + row_count)
    ).astype(jnp.float32)
    head_out, logs, queries, kv = attend(
        keep_q, over_z_lo(give_q), keep_kv, over_z_lo(give_kv), prev_a, prev_b, mask
    )
    grad_queries, dkv_prev, dkv_own, dkv_low = attend_back(
        queries, kv, mask, head_out, logs, keep_grad, over_z_lo(give_grad)
    )
    targets = (x_index + jnp.arange(NX)) % NX
    grad_queries_x = over_z_lo(grad_queries)
    back = send(
        dkv_prev, lambda x, y, zh, zl, c: (x, y, 0, zl, c) if zh == 1 else None
    )
    back_x = send(
        dkv_prev, lambda x, y, zh, zl, c: (x, y, 0, 1 - zl, c) if zh == 1 else None
    )
    totals = query_product(in_info(z_lo, targets), grad_queries, in_all)
    totals = query_product(in_info(1 - z_lo, targets), grad_queries_x, in_all, totals)
    here, up, across, down = rest_product(
        in_info(z_lo, targets), totals, [dkv_own, back, over_z_lo(dkv_low), back_x], in_all
    )

    half = row_count // 2
    from_below = along_x(across[:half], -1)
    from_above = along_x(across[half:], 1)

    up = jnp.concatenate(
        [(wide(up[:half]) + wide(from_below)).astype(jnp.bfloat16), up[half:]], axis=0
    )
    down = jnp.concatenate(
        [down[:half], (wide(down[half:]) + wide(from_above)).astype(jnp.bfloat16)], axis=0
    )
    up, down = along_x(up, -1), along_x(down, 1)
    grad_moved = (wide(here) + wide(up) + wide(down)).astype(jnp.bfloat16)

    (heads,) = fence([head_out], [grad_queries_x])
    order = jnp.array(POSITION, jnp.int32)[(targets - y_index) % NY]
    mixed_info = jnp.concatenate([keep_info[:2], order])
    own_part, *others = mixed_product(mixed_info, heads, over_z_lo(heads), out_all)
    others = fence(others, [grad_moved])
    attended = wide(own_part)
    for part, distance in zip(others, (-1, 2, 1)):
        attended += wide(along_x(part, distance))
    attended = low(attended)

    returned = route_blocks(pick_blocks(grad_moved, recv_slots))
    grad_in = returned[sources(send_slots, block_count)]
    return (attended, grad_in.reshape(row_count, shard_width))


def solution(mesh):
    placed = (
        P(("dp", "seq"), "tensor"),
        P(("dp", "seq"), "tensor", None),
        P("tensor", None, ("dp", "seq")),
        P(("dp", "seq"), "tensor"),
        P("dp"),
        P(("dp", "seq"), None),
        P(("dp", "seq"), None),
    )
    return jax.shard_map(
        body,
        mesh=mesh,
        in_specs=placed,
        out_specs=(P(("dp", "seq"), "tensor"), P(("dp", "seq"), "tensor")),
        check_vma=False,
    )
```

```python
import math

import jax
import jax.numpy as jnp
from jax import lax
from jax.experimental import pallas as pl
from jax.experimental.pallas import tpu as pltpu
from jax.sharding import PartitionSpec as P

HS = 128
GROUP = 6
BLK = 32
AXES = ("dp", "seq", "tensor")
NX, NY, NZ = 4, 4, 4
X_GROUPS = [[0, 2, 4, 6], [1, 3, 5, 7]]


def place(index):
    dp, seq, tensor = index // 16, index // 8 % 2, index % 8
    return tensor // 2, dp // 2, seq, tensor % 2, dp % 2


def index_of(x, y, z_hi, z_lo, core):
    return (y % NY * 2 + core) * 16 + z_hi * 8 + x % NX * 2 + z_lo


def send(block, target):
    pairs = []
    for source in range(128):
        goal = target(*place(source))
        if goal is not None:
            pairs.append((source, index_of(*goal)))
    return lax.ppermute(block, AXES, pairs)


def along_y(block, distance):
    return send(block, lambda x, y, zh, zl, c: (x, y - distance, zh, zl, c))


def over_cores(block):
    return send(block, lambda x, y, zh, zl, c: (x, y, zh, zl, 1 - c))


def over_z_lo(block):
    return send(block, lambda x, y, zh, zl, c: (x, y, zh, 1 - zl, c))


def z_near(block):
    return send(
        block, lambda x, y, zh, zl, c: (x, y, zh, 1 - zl, 1 - c) if zl != c else None
    )


def z_far(block):
    return send(
        block,
        lambda x, y, zh, zl, c: (x, y, 1 - zh, zl, c)
        if zl == c
        else (x, y, 1 - zh, 1 - zl, 1 - c),
    )


def along_x(block, distance):
    return send(block, lambda x, y, zh, zl, c: (x - distance, y, zh, zl, c))


def route_blocks(buffer):
    return lax.all_to_all(buffer, ("dp", "seq"), split_axis=0, concat_axis=0, tiled=True)


def nothing(*refs):
    pass


def fence(values, after=()):
    return pl.pallas_call(
        nothing,
        out_shape=[jax.ShapeDtypeStruct(v.shape, v.dtype) for v in values],
        in_specs=[anywhere()] * (len(values) + len(after)),
        out_specs=[anywhere()] * len(values),
        input_output_aliases={i: i for i in range(len(values))},
        cost_estimate=pl.CostEstimate(flops=0, bytes_accessed=0, transcendentals=0),
    )(*values, *after)


def dot(a, b, contract=((1,), (0,))):
    return lax.dot_general(a, b, (contract, ((), ())), preferred_element_type=jnp.float32)


NT = ((1,), (1,))
NN = ((1,), (0,))
MB = 1 << 20
OFFSETS = (0, 1, -1, 2)
POSITION = (0, 1, 3, 2)


def vmem():
    return pl.BlockSpec(memory_space=pltpu.VMEM)


def smem():
    return pl.BlockSpec(memory_space=pltpu.SMEM)


def anywhere():
    return pl.BlockSpec(memory_space=pl.ANY)


def params(size=24):
    return pltpu.CompilerParams(vmem_limit_bytes=size * MB)


def start_all(copies):
    for copy in copies:
        copy.start()


def wait_all(copies):
    for copy in copies:
        copy.wait()


def proj_kernel(info, *refs):
    rows, weights, out_kv, out_q = refs[:NX], refs[NX], refs[NX + 1], refs[NX + 2]
    lhs, held, total, lhs_sems, sems = refs[NX + 3 :]
    cuts = halves(info[1 + NX], weights.shape[2])
    copies = [
        [pltpu.make_async_copy(rows[r], lhs.at[r], lhs_sems.at[r])]
        + [
            pltpu.make_async_copy(
                weights.at[2 * info[1 + r] + info[0], i], held.at[r, cut], sems.at[r, i]
            )
            for i, cut in enumerate(cuts)
        ]
        for r in range(NX)
    ]
    start_all(copies[0])
    start_all(copies[1])
    for r in range(NX):
        wait_all(copies[r])
        if r + 2 < NX:
            start_all(copies[r + 2])
        term = dot(lhs[r], held[r])
        if r == 0:
            total[...] = term
        elif r < NX - 1:
            total[...] += term
        else:
            term = (total[...] + term).astype(out_q.dtype)
            out_q[...] = term[:, :SPAN]
            out_kv[...] = term[:, SPAN:]


def proj_product(info, rows, weights, dtype):
    row_count, depth = rows[0].shape
    width, full = weights.shape[3], NX * depth
    return pl.pallas_call(
        proj_kernel,
        out_shape=(
            jax.ShapeDtypeStruct((row_count, 2 * HS), dtype),
            jax.ShapeDtypeStruct((row_count, SPAN), dtype),
        ),
        in_specs=[smem()] + [anywhere()] * (NX + 1),
        out_specs=(vmem(), vmem()),
        scratch_shapes=[
            pltpu.VMEM((NX, row_count, depth), jnp.bfloat16),
            pltpu.VMEM((NX, depth, width), jnp.bfloat16),
            pltpu.VMEM((row_count, width), jnp.float32),
            pltpu.SemaphoreType.DMA((NX,)),
            pltpu.SemaphoreType.DMA((NX, 2)),
        ],
        compiler_params=params(53),
        cost_estimate=pl.CostEstimate(
            flops=2 * row_count * width * full,
            bytes_accessed=2 * full * (width + row_count),
            transcendentals=0,
        ),
    )(info, *rows, weights)


def halves(z_hi, size):
    return [pl.ds(pl.multiple_of(z * size, size), size) for z in (z_hi, 1 - z_hi)]


def chunk_copies(weights, z_hi, index, held, at, rows, sems):
    return [
        pltpu.make_async_copy(piece.at[index], held.at[at, rows, cut], sems.at[i])
        for i, (piece, cut) in enumerate(zip(weights, halves(z_hi, weights[0].shape[2])))
    ]


def heads_kernel(
    info, rows, here, far, here_x, far_x, out, lhs, held, total, lhs_sems, sems
):
    def copies_of(r, pair):
        every = pl.ds(0, held.shape[1])
        return [pltpu.make_async_copy(rows.at[r], lhs.at[r], lhs_sems.at[r])] + chunk_copies(
            pair, info[1], info[2 + r], held, r, every, sems.at[r]
        )

    def begin(r):
        for pick, pair in ((0, (here, far)), (1, (here_x, far_x))):

            @pl.when(info[0] == pick)
            def _():
                start_all(copies_of(r, pair))

    begin(0)
    begin(1)
    for r in range(NX):
        wait_all(copies_of(r, (here, far)))
        if r + 2 < NX:
            begin(r + 2)
        term = dot(lhs[r], held[r], NT)
        if r == 0:
            total[...] = term
        elif r < NX - 1:
            total[...] += term
        else:
            out[...] = (total[...] + term).astype(out.dtype)


def heads_product(info, rows, weights, dtype):
    row_count, depth = rows.shape[1:]
    width, full = weights[0].shape[1], NX * depth
    return pl.pallas_call(
        heads_kernel,
        out_shape=jax.ShapeDtypeStruct((row_count, width), dtype),
        in_specs=[smem()] + [anywhere()] * 5,
        out_specs=vmem(),
        scratch_shapes=[
            pltpu.VMEM((NX, row_count, depth), jnp.bfloat16),
            pltpu.VMEM((NX, width, depth), jnp.bfloat16),
            pltpu.VMEM((row_count, width), jnp.float32),
            pltpu.SemaphoreType.DMA((NX,)),
            pltpu.SemaphoreType.DMA((NX, 2)),
        ],
        compiler_params=params(53),
        cost_estimate=pl.CostEstimate(
            flops=2 * row_count * width * full,
            bytes_accessed=2 * full * (width + row_count),
            transcendentals=0,
        ),
    )(info, rows, *weights)


def mixed_kernel(
    info, own, theirs, here, far, here_x, far_x,
    out_0, out_1, out_2, out_3, lhs, held, ready, lhs_sems, sems, out_sems,
):
    depth = own.shape[1]
    lhs_copies = [
        pltpu.make_async_copy(piece, lhs.at[:, pl.ds(i * depth, depth)], lhs_sems.at[i])
        for i, piece in enumerate((own, theirs))
    ]
    mine, other = (here, far), (here_x, far_x)

    def copies_of(j, pairs):
        return [
            copy
            for side, pair in enumerate(pairs)
            for copy in chunk_copies(
                pair, info[1], info[2 + j], held, j, pl.ds(side * depth, depth), sems.at[j, side]
            )
        ]

    def begin(j):
        for pick, pairs in ((0, (mine, other)), (1, (other, mine))):

            @pl.when(info[0] == pick)
            def _():
                start_all(copies_of(j, pairs))

    outs = (out_0, out_1, out_2, out_3)
    done = [pltpu.make_async_copy(ready.at[j], outs[j], out_sems.at[j]) for j in range(NX)]
    begin(0)
    start_all(lhs_copies)
    wait_all(lhs_copies)
    begin(1)
    for j in range(NX):
        wait_all(copies_of(j, (mine, other)))
        if j + 2 < NX:
            begin(j + 2)
        ready[j] = low(dot(lhs[...], held[j]))
        done[j].start()
    wait_all(done)


def mixed_product(info, own, theirs, weights):
    row_count, depth = own.shape
    width = 2 * weights[0].shape[2]
    return pl.pallas_call(
        mixed_kernel,
        out_shape=[jax.ShapeDtypeStruct((row_count, width), jnp.bfloat16)] * NX,
        in_specs=[smem()] + [anywhere()] * 6,
        out_specs=[anywhere()] * NX,
        scratch_shapes=[
            pltpu.VMEM((row_count, 2 * depth), jnp.bfloat16),
            pltpu.VMEM((NX, 2 * depth, width), jnp.bfloat16),
            pltpu.VMEM((NX, row_count, width), jnp.bfloat16),
            pltpu.SemaphoreType.DMA((2,)),
            pltpu.SemaphoreType.DMA((NX, 2, 2)),
            pltpu.SemaphoreType.DMA((NX,)),
        ],
        compiler_params=params(53),
        cost_estimate=pl.CostEstimate(
            flops=4 * row_count * width * depth * NX,
            bytes_accessed=4 * NX * depth * width + 2 * row_count * (2 * depth + NX * width),
            transcendentals=0,
        ),
    )(info, own, theirs, *weights)


def wide(value):
    return value.astype(jnp.float32)


def low(value):
    return value.astype(jnp.bfloat16)


def query_kernel(count, info, q, weights, *refs):
    parts, outs = refs[:count], refs[count : count + NX]
    held, sems = refs[-2:]
    cuts = halves(info[1 + NX], weights.shape[2])
    copies = [
        [
            pltpu.make_async_copy(
                weights.at[2 * info[1 + j] + info[0], i, :, pl.ds(0, SPAN)],
                held.at[j, cut],
                sems.at[j, i],
            )
            for i, cut in enumerate(cuts)
        ]
        for j in range(NX)
    ]
    start_all(copies[0])
    start_all(copies[1])
    for j in range(NX):
        wait_all(copies[j])
        if j + 2 < NX:
            start_all(copies[j + 2])
        product = dot(q[...], held[j], NT)
        outs[j][...] = product + parts[j][...] if count else product


def query_product(info, q, weights, parts=()):
    row_count, width = q.shape[0], 2 * weights.shape[2]
    return pl.pallas_call(
        lambda *refs: query_kernel(len(parts), *refs),
        out_shape=[jax.ShapeDtypeStruct((row_count, width), jnp.float32)] * NX,
        in_specs=[smem(), vmem(), anywhere()] + [vmem()] * len(parts),
        out_specs=[vmem()] * NX,
        input_output_aliases={3 + j: j for j in range(len(parts))},
        scratch_shapes=[
            pltpu.VMEM((NX, width, SPAN), jnp.bfloat16),
            pltpu.SemaphoreType.DMA((NX, 2)),
        ],
        compiler_params=params(48),
        cost_estimate=pl.CostEstimate(
            flops=2 * row_count * width * SPAN * NX,
            bytes_accessed=2 * NX * SPAN * width + 4 * row_count * NX * width,
            transcendentals=0,
        ),
    )(info, q, weights, *parts)


def rest_kernel(info, *refs):
    parts = refs[:NX]
    kv, kv_back, kv_x, kv_back_x, weights = refs[NX : NX + 5]
    outs = refs[NX + 5 : 2 * NX + 5]
    lhs, held, ready, sems, out_sems = refs[2 * NX + 5 :]
    copies = [
        [
            pltpu.make_async_copy(
                weights.at[2 * info[1 + j] + (info[0] + side) % 2, i, :, pl.ds(SPAN, 2 * HS)],
                held.at[j, cut, pl.ds(side * 2 * HS, 2 * HS)],
                sems.at[j, side, i],
            )
            for side in range(2)
            for i, cut in enumerate(halves(info[1 + NX], weights.shape[2]))
        ]
        for j in range(NX)
    ]
    done = [pltpu.make_async_copy(ready.at[j], outs[j], out_sems.at[j]) for j in range(NX)]
    order = (2, 1, 3, 0)
    start_all(copies[order[0]])
    start_all(copies[order[1]])
    lhs[:, : 2 * HS] = low(kv[...] + wide(kv_back[...]))
    lhs[:, 2 * HS :] = low(wide(kv_x[...]) + wide(kv_back_x[...]))
    for i, j in enumerate(order):
        wait_all(copies[j])
        if i + 2 < NX:
            start_all(copies[order[i + 2]])
        ready[j] = low(parts[j][...] + dot(lhs[...], held[j], NT))
        done[j].start()
    wait_all(done)


def rest_product(info, parts, operands, weights):
    row_count, width = parts[0].shape
    return pl.pallas_call(
        rest_kernel,
        out_shape=[jax.ShapeDtypeStruct((row_count, width), jnp.bfloat16)] * NX,
        in_specs=[smem()] + [vmem()] * (NX + 4) + [anywhere()],
        out_specs=[anywhere()] * NX,
        scratch_shapes=[
            pltpu.VMEM((row_count, 4 * HS), jnp.bfloat16),
            pltpu.VMEM((NX, width, 4 * HS), jnp.bfloat16),
            pltpu.VMEM((NX, row_count, width), jnp.bfloat16),
            pltpu.SemaphoreType.DMA((NX, 2, 2)),
            pltpu.SemaphoreType.DMA((NX,)),
        ],
        compiler_params=params(48),
        cost_estimate=pl.CostEstimate(
            flops=8 * row_count * width * HS * NX,
            bytes_accessed=8 * NX * HS * width + 6 * row_count * NX * width,
            transcendentals=0,
        ),
    )(info, *parts, *operands, weights)


SCALING = 1.0 / math.sqrt(HS)
SPAN = GROUP * HS


def forward_kernel(
    keep_q, came_q, keep_kv, came_kv, prev_a, prev_b, mask, head_out, logs, queries, kv
):
    rows = keep_q.shape[0]
    queries[...] = low(keep_q[...] + wide(came_q[...]))
    kv[:rows] = low(wide(prev_a[...]) + wide(prev_b[...]))
    kv[rows:] = low(keep_kv[...] + wide(came_kv[...]))
    keys, turned = kv[:, :HS], kv[:, HS:].T

    @pl.loop(0, GROUP, unroll=GROUP)
    def _(h):
        lanes = pl.ds(pl.multiple_of(h * HS, HS), HS)
        scores = dot(keys, queries[:, lanes], NT) * SCALING
        scores = jnp.where(mask[...] > 0, scores, -1e30)
        highest = jnp.max(scores, axis=0, keepdims=True)
        raised = jnp.exp(scores - highest)
        inverse = 1.0 / jnp.sum(raised, axis=0, keepdims=True)
        logs[h, 0:1] = highest
        logs[h, 1:2] = inverse
        head_out[:, lanes] = low(dot(turned, low(raised * inverse)).T)


def backward_kernel(
    queries, kv, mask, head_out, logs, keep_grad, came_grad,
    dq, dkv_prev, dkv_own, dkv_low, dk, dv, grad_heads,
):
    rows = queries.shape[0]
    grad_heads[...] = low(keep_grad[...] + wide(came_grad[...]))
    keys, values = kv[:, :HS], kv[:, HS:]
    turned = keys.T
    dk[...] = jnp.zeros_like(dk)
    dv[...] = jnp.zeros_like(dv)

    @pl.loop(0, GROUP, unroll=GROUP)
    def _(h):
        lanes = pl.ds(pl.multiple_of(h * HS, HS), HS)
        query, grad = queries[:, lanes], grad_heads[:, lanes]
        scores = dot(keys, query, NT) * SCALING
        scores = jnp.where(mask[...] > 0, scores, -1e30)
        probability = jnp.exp(scores - logs[h, 0:1]) * logs[h, 1:2]
        delta = jnp.sum((wide(grad) * wide(head_out[:, lanes])).T, axis=0, keepdims=True)
        score_grad = low(probability * (dot(values, grad, NT) - delta))
        dv[...] += dot(low(probability), grad)
        dk[...] += dot(score_grad, query)
        dq[:, lanes] = low((dot(turned, score_grad) * SCALING).T)

    dkv_prev[:, :HS] = low(dk[:rows] * SCALING)
    dkv_prev[:, HS:] = low(dv[:rows])
    dkv_own[:, :HS] = dk[rows:] * SCALING
    dkv_own[:, HS:] = dv[rows:]
    dkv_low[...] = low(dkv_own[...])


def attend(keep_q, came_q, keep_kv, came_kv, prev_a, prev_b, mask):
    rows = keep_q.shape[0]
    return pl.pallas_call(
        forward_kernel,
        out_shape=(
            jax.ShapeDtypeStruct((rows, SPAN), jnp.bfloat16),
            jax.ShapeDtypeStruct((GROUP, 8, rows), jnp.float32),
            jax.ShapeDtypeStruct((rows, SPAN), jnp.bfloat16),
            jax.ShapeDtypeStruct((2 * rows, 2 * HS), jnp.bfloat16),
        ),
        in_specs=[vmem()] * 7,
        out_specs=(vmem(),) * 4,
        compiler_params=params(),
        cost_estimate=pl.CostEstimate(
            flops=8 * rows * rows * HS * GROUP * 2, bytes_accessed=4 * MB,
            transcendentals=2 * rows * rows * GROUP,
        ),
    )(keep_q, came_q, keep_kv, came_kv, prev_a, prev_b, mask)


def attend_back(queries, kv, mask, head_out, logs, keep_grad, came_grad):
    rows = queries.shape[0]
    return pl.pallas_call(
        backward_kernel,
        out_shape=(
            jax.ShapeDtypeStruct((rows, SPAN), jnp.bfloat16),
            jax.ShapeDtypeStruct((rows, 2 * HS), jnp.bfloat16),
            jax.ShapeDtypeStruct((rows, 2 * HS), jnp.float32),
            jax.ShapeDtypeStruct((rows, 2 * HS), jnp.bfloat16),
        ),
        in_specs=[vmem()] * 7,
        out_specs=(vmem(),) * 4,
        scratch_shapes=[pltpu.VMEM((2 * rows, HS), jnp.float32)] * 2
        + [pltpu.VMEM((rows, SPAN), jnp.bfloat16)],
        compiler_params=params(),
        cost_estimate=pl.CostEstimate(
            flops=20 * rows * rows * HS * GROUP * 2, bytes_accessed=5 * MB,
            transcendentals=2 * rows * rows * GROUP,
        ),
    )(queries, kv, mask, head_out, logs, keep_grad, came_grad)


def pick_blocks(array, wanted):
    blocks = array.reshape(-1, BLK, array.shape[1])
    return jnp.where(
        (wanted >= 0)[:, None, None],
        blocks[jnp.maximum(wanted, 0)],
        jnp.zeros((), jnp.bfloat16),
    )


def sources(landing, block_count):
    return (
        jnp.zeros((block_count,), jnp.int32)
        .at[jnp.where(landing >= 0, landing, block_count)]
        .set(jnp.arange(landing.shape[0], dtype=jnp.int32), mode="drop")
    )


def body(activations, qkv_weight, out_weight, grad_out, segments, send_list, recv_list):
    row_count, shard_width = activations.shape
    dp_index = lax.axis_index("dp")
    seq_index = lax.axis_index("seq")
    tensor_index = lax.axis_index("tensor")
    y_index, core = dp_index // 2, dp_index % 2
    x_index, z_lo = tensor_index // 2, tensor_index % 2
    straight = core == z_lo

    block_count = row_count // BLK
    send_slots, recv_slots = send_list[0], recv_list[0]
    in_own, out_own = qkv_weight[:, 0, :], out_weight[0]

    grad_x = lax.all_gather(
        grad_out, "tensor", axis=0, tiled=False, axis_index_groups=X_GROUPS
    )
    out_own = out_own[None]
    in_near, in_far, out_up, out_down, arrived = fence(
        [
            z_near(in_own),
            z_far(in_own),
            along_y(out_own, 1),
            along_y(out_own, -1),
            route_blocks(pick_blocks(activations, send_slots)),
        ],
        [grad_x],
    )

    in_pair = jnp.stack([jnp.where(straight, in_own, in_near), in_far])
    in_all = lax.all_gather(in_pair, "dp", axis=0, tiled=False)
    moved = arrived[sources(recv_slots, block_count)].reshape(row_count, shard_width)
    out_three = jnp.concatenate([out_own, out_up, out_down], axis=0)
    half = out_own.shape[1] // 2
    first, second = fence([along_y(out_up[:, :half], 1), along_y(out_down[:, half:], -1)])
    out_one = jnp.concatenate([first, second], axis=1)
    near_three, far_three, near_one, far_one, *moved_x = fence(
        [z_near(out_three), z_far(out_three), z_near(out_one), z_far(out_one)]
        + [along_x(moved, distance) for distance in OFFSETS[1:]]
    )
    moved_x = [moved, *moved_x]

    out_here = jnp.where(
        straight,
        jnp.concatenate([out_three, out_one], axis=0),
        jnp.concatenate([near_three, near_one], axis=0),
    )
    out_far = jnp.concatenate([far_three, far_one], axis=0)
    out_all = [out_here, out_far, over_cores(out_here), over_cores(out_far)]

    places = (x_index + jnp.array(OFFSETS, jnp.int32)) % NX
    order = jnp.array(POSITION, jnp.int32)[(jnp.arange(NX) - y_index) % NY]
    give_info = jnp.concatenate([jnp.stack([straight, seq_index]), order]).astype(jnp.int32)
    keep_info = jnp.concatenate([jnp.stack([~straight, seq_index]), order]).astype(jnp.int32)

    def in_info(head, columns):
        return jnp.concatenate([head[None], columns, seq_index[None]]).astype(jnp.int32)

    give_kv, give_q = proj_product(in_info(1 - z_lo, places), moved_x, in_all, jnp.bfloat16)
    keep_kv, keep_q = proj_product(in_info(z_lo, places), moved_x, in_all, jnp.float32)
    (give_info,) = fence([give_info], [keep_kv])
    give_grad = heads_product(give_info, grad_x, out_all, jnp.bfloat16)
    keep_grad = heads_product(keep_info, grad_x, out_all, jnp.float32)

    (late_kv,) = fence([give_kv], [keep_kv])
    prev_a = send(
        late_kv, lambda x, y, zh, zl, c: (x, y, 1, 1 - zl, c) if zh == 0 else None
    )
    prev_b = send(
        low(keep_kv), lambda x, y, zh, zl, c: (x, y, 1, zl, c) if zh == 0 else None
    )
    query_ids = lax.dynamic_slice_in_dim(segments, seq_index * row_count, row_count)
    padded_ids = jnp.concatenate([jnp.full((row_count,), -1, jnp.int32), segments])
    key_ids = lax.dynamic_slice_in_dim(padded_ids, seq_index * row_count, 2 * row_count)
    positions = jnp.arange(2 * row_count)
    mask = (
        (query_ids[None, :] == key_ids[:, None])
        & (positions[:, None] <= positions[None, :row_count] + row_count)
    ).astype(jnp.float32)
    head_out, logs, queries, kv = attend(
        keep_q, over_z_lo(give_q), keep_kv, over_z_lo(give_kv), prev_a, prev_b, mask
    )
    grad_queries, dkv_prev, dkv_own, dkv_low = attend_back(
        queries, kv, mask, head_out, logs, keep_grad, over_z_lo(give_grad)
    )
    targets = (x_index + jnp.arange(NX)) % NX
    grad_queries_x = over_z_lo(grad_queries)
    back = send(
        dkv_prev, lambda x, y, zh, zl, c: (x, y, 0, zl, c) if zh == 1 else None
    )
    back_x = send(
        dkv_prev, lambda x, y, zh, zl, c: (x, y, 0, 1 - zl, c) if zh == 1 else None
    )
    totals = query_product(in_info(z_lo, targets), grad_queries, in_all)
    totals = query_product(in_info(1 - z_lo, targets), grad_queries_x, in_all, totals)
    here, up, across, down = rest_product(
        in_info(z_lo, targets), totals, [dkv_own, back, over_z_lo(dkv_low), back_x], in_all
    )

    half = row_count // 2
    from_below = along_x(across[:half], -1)
    from_above = along_x(across[half:], 1)

    up = jnp.concatenate(
        [(wide(up[:half]) + wide(from_below)).astype(jnp.bfloat16), up[half:]], axis=0
    )
    down = jnp.concatenate(
        [down[:half], (wide(down[half:]) + wide(from_above)).astype(jnp.bfloat16)], axis=0
    )
    up, down = along_x(up, -1), along_x(down, 1)
    grad_moved = (wide(here) + wide(up) + wide(down)).astype(jnp.bfloat16)

    (heads,) = fence([head_out], [grad_queries_x])
    order = jnp.array(POSITION, jnp.int32)[(targets - y_index) % NY]
    mixed_info = jnp.concatenate([keep_info[:2], order])
    own_part, *others = mixed_product(mixed_info, heads, over_z_lo(heads), out_all)
    others = fence(others, [grad_moved])
    attended = wide(own_part)
    for part, distance in zip(others, (-1, 2, 1)):
        attended += wide(along_x(part, distance))
    attended = low(attended)

    returned = route_blocks(pick_blocks(grad_moved, recv_slots))
    grad_in = returned[sources(send_slots, block_count)]
    return (attended, grad_in.reshape(row_count, shard_width))


def solution(mesh):
    placed = (
        P(("dp", "seq"), "tensor"),
        P(("dp", "seq"), "tensor", None),
        P("tensor", None, ("dp", "seq")),
        P(("dp", "seq"), "tensor"),
        P("dp"),
        P(("dp", "seq"), None),
        P(("dp", "seq"), None),
    )
    return jax.shard_map(
        body,
        mesh=mesh,
        in_specs=placed,
        out_specs=(P(("dp", "seq"), "tensor"), P(("dp", "seq"), "tensor")),
        check_vma=False,
    )
```
